32 devices in a mesh: dp: 16 (over z, y, x), tensor: 2 (over core).
Axes of the slice: x: 2, y: 2, z: 4, core: 2. Of those that a mesh axis runs over, the one named last changes fastest.
Arguments:
- inputs: float32 [16384, 1280], P(('dp', 'tensor')), may hold values from -6 to 6
- cotangent: float32 [16384, 1280], P(('dp', 'tensor')), may hold values from -6 to 6
- query_weight: bfloat16 [2, 1280, 1280], P(None, 'dp', 'tensor'), may hold values from -0.15625 to 0.15625
- key_weight: bfloat16 [2, 1280, 1280], P(None, 'dp', 'tensor'), may hold values from -0.15625 to 0.15625
- value_weight: bfloat16 [2, 1280, 1280], P(None, 'dp', 'tensor'), may hold values from -0.15625 to 0.15625
- output_weight: bfloat16 [2, 1280, 1280], P(None, 'tensor', 'dp'), may hold values from -2.5 to 2.5
- up_weight: bfloat16 [2, 1280, 1280], P(None, 'dp', 'tensor'), may hold values from -0.15625 to 0.15625
- down_weight: bfloat16 [2, 1280, 1280], P(None, 'tensor', 'dp'), may hold values from -0.15625 to 0.15625
- attention_gain: float32 [2, 1280], replicated, may hold values from 0.1 to 1.9
- feed_gain: float32 [2, 1280], replicated, may hold values from 0.1 to 1.9
- query_scale: float32 [2, 80], replicated, may hold values from -0.5 to 1.5
- cont_lengths: int32 [16, 4], P('dp'), may hold values from 1 to 192, 512 in all within a row
Outputs:
- block_output: float32 [16384, 1280], P(('dp', 'tensor'))
- input_grad: float32 [16384, 1280], P(('dp', 'tensor'))
- grad_query: float32 [2, 1280, 1280], P(None, 'dp', 'tensor')
- grad_key: float32 [2, 1280, 1280], P(None, 'dp', 'tensor')
- grad_value: float32 [2, 1280, 1280], P(None, 'dp', 'tensor')
- grad_output: float32 [2, 1280, 1280], P(None, 'tensor', 'dp')
- grad_up: float32 [2, 1280, 1280], P(None, 'dp', 'tensor')
- grad_down: float32 [2, 1280, 1280], P(None, 'tensor', 'dp')
- grad_attention: float32 [2, 1280], replicated
- grad_feed: float32 [2, 1280], replicated
- grad_scale: float32 [2, 80], replicated
The draws below stay inside these ranges and needn't reach their ends.
Inputs may be any that keep to these rules, and one draw needn't show every extreme that they name: `cont_lengths`: each row holds the lengths of one dp index's 4 continuations in order; they sum to 512 and the largest is 192.
All inputs are finite; a program needn't handle non-finite values.
Results may differ from the reference program's by a relative error of at most 0.038.
Values may be sent and summed in bfloat16 or wider, within the bound.
No kernel may reach another device: no remote copies, remote signals or barrier semaphores. Data moves between devices by JAX's collectives and lax.ppermute only.
A program may use at most 256 MiB of HBM per device.

```python
import math
import jax
import jax.numpy as jnp
import numpy as np
from jax import lax

D = 1280
HEADS = 16
HD = 80
FF = 1280
LAYERS = 2
CPD = 4
PROMPT_DEV = 512
CONT_TOK = 512
CONT_MOST = 192
TOK_DP = 1024
TOKENS = 16384
N_DP = 16


def with_spikes(values, own_key, source, target, shards_of, factor):
    owner, partner = [(jnp.arange(values.shape[position]) // (values.shape[position] // shards_of)).reshape([-1 if axis == position else 1 for axis in range(values.ndim)]) for position in (source, target)]
    chosen = jax.random.permutation(own_key, shards_of)[partner]
    strong = (owner == chosen) | (owner == (partner + shards_of // 2) % shards_of)
    return jnp.where(strong, factor * values, values)


def block_levels(own_key, shape, pieces, least, largest):
    gain, own = 1.0, jax.random.fold_in(own_key, 6)
    for axis_at, shards_of in pieces:
        steps = jnp.exp(jax.random.uniform(jax.random.fold_in(own, axis_at), (shards_of,), jnp.float32, least / len(pieces), largest / len(pieces)))
        gain = gain * jnp.repeat(steps, shape[axis_at] // shards_of).reshape([-1 if axis == axis_at else 1 for axis in range(len(shape))])
    return gain


def profile(number_of, total, bound, skew):
    loads = [(1 << 20) // math.isqrt(grade ** skew) + 1 for grade in range(2, number_of + 1)]
    surplus, given = total - bound - (number_of - 1), [1] * (number_of - 1)
    while surplus > 0:
        candidates = [i for i in range(number_of - 1) if given[i] < bound]
        whole, left = sum([loads[i] for i in candidates]), surplus
        for i in candidates:
            more = min(bound - given[i], max(1, left * loads[i] // whole), surplus)
            given[i] = given[i] + more
            surplus = surplus - more
    return np.array([bound] + given)


def ragged(own_key, number_of, total, limit, skew):
    if number_of == 2:
        one = jax.random.randint(own_key, (), max(1, total - limit), min(limit, total - 1) + 1)
        return jnp.stack([one, total - one])
    lengths = jnp.asarray(profile(number_of, total, limit, skew), jnp.int32)
    pairs = (number_of - 1) // 2
    source_of, taker = lengths[1:1 + 2 * pairs:2], lengths[2:2 + 2 * pairs:2]
    slack = jnp.minimum(source_of - 1, limit - taker)
    moved = jax.random.randint(jax.random.fold_in(own_key, 1), (pairs,), 0, 1 << 20) % (slack + 1)
    lengths = lengths.at[1:1 + 2 * pairs:2].set(source_of - moved).at[2:2 + 2 * pairs:2].set(taker + moved)
    return lengths[jax.random.permutation(jax.random.fold_in(own_key, 2), number_of)]


def normal_values(rng, dims, scale, most, pieces=(), kind=jnp.bfloat16):
    gain = block_levels(rng, dims, pieces, -0.22, 0.18) if pieces else 1.0
    values = jax.random.normal(rng, dims, jnp.float32) * scale * gain
    return jnp.minimum(jnp.maximum(values, -most), most).astype(kind)


def noise_with(key, dims, scale, limit, pieces, heavy, kind=jnp.bfloat16):
    entries = scale * jax.random.normal(key, dims, jnp.float32)
    if pieces:
        entries = entries * block_levels(key, dims, pieces, -0.22, 0.18)
    return jnp.clip(with_spikes(entries, jax.random.fold_in(key, 3), *heavy), -limit, limit).astype(kind)


def setup_inputs(seed: int = 0) -> dict:
    arg_keys = jax.random.split(jax.random.key(seed), 13)
    return {
        "inputs": normal_values(arg_keys[0], (TOKENS, D), 1.0, 6.0, ((0, 32),), jnp.float32),
        "cotangent": noise_with(arg_keys[1], (TOKENS, D), 1.0, 6.0, ((0, 32),), (0, 1, 32, 2.75), jnp.float32),
        "query_weight": normal_values(arg_keys[2], (LAYERS, D, D), D ** -0.5, 0.15625, ((1, 16), (2, 2))),
        "key_weight": normal_values(arg_keys[3], (LAYERS, D, D), D ** -0.5, 0.15625, ((1, 16), (2, 2))),
        "value_weight": normal_values(arg_keys[4], (LAYERS, D, D), D ** -0.5, 0.15625, ((1, 16), (2, 2))),
        "output_weight": normal_values(arg_keys[5], (LAYERS, D, D), (max(D // 256, 2)) ** -0.5, 2.5, ((1, 2), (2, 16))),
        "up_weight": normal_values(arg_keys[6], (LAYERS, D, FF), D ** -0.5, 0.15625, ((1, 16), (2, 2))),
        "down_weight": normal_values(arg_keys[7], (LAYERS, FF, D), FF ** -0.5, 0.15625, ((1, 2), (2, 16))),
        "attention_gain": jnp.clip(1.0 + 0.18 * jax.random.normal(arg_keys[8], (LAYERS, D), jnp.float32), 0.1, 1.9),
        "feed_gain": jnp.clip(1.0 + 0.18 * jax.random.normal(arg_keys[9], (LAYERS, D), jnp.float32), 0.1, 1.9),
        "query_scale": jnp.clip(jax.random.uniform(arg_keys[10], (LAYERS, HD), jnp.float32, -0.5, 1.5), -0.5, 1.5),
        "cont_lengths": jax.vmap(lambda own: ragged(own, CPD, CONT_TOK, CONT_MOST, 1))(jax.random.split(arg_keys[11], N_DP)).reshape((N_DP, CPD)).astype(jnp.int32),
    }


@jax.custom_vjp
def low(v):
    return lax.optimization_barrier(v.astype(jnp.bfloat16)).astype(jnp.float32)

@jax.custom_vjp
def low_back(v):
    return v

def low_keep(v):
    return (low(v), None)

def low_pass(kept, grad):
    return (grad,)

def back_keep(v):
    return (v, None)

def back_low(kept, grad):
    return (low(grad),)
low.defvjp(low_keep, low_pass)
low_back.defvjp(back_keep, back_low)
EPSILON = 1e-06
LOG_TWO_E = 1.4426950408889634
NEGATIVE = -1e+30

def matmul(former, latter):
    return jnp.dot(former, latter, precision=lax.Precision.HIGHEST, preferred_element_type=jnp.float32)

def softplus(values):
    return jnp.log1p(jnp.exp(values))

def norm_rows(source, gain_row):
    return source * lax.rsqrt(lax.optimization_barrier(jnp.mean(source * source, axis=1, keepdims=True)) + EPSILON) * gain_row

def group_segments(pair_lengths):
    offsets = jnp.arange(TOK_DP, dtype=jnp.int32) - PROMPT_DEV
    bounds = jnp.cumsum(pair_lengths, axis=1)
    passed = lax.optimization_barrier(jnp.sum((offsets[None, :, None] >= bounds[:, None, :]).astype(jnp.int32), axis=2))
    halves = jnp.arange(2, dtype=jnp.int32)[:, None]
    segment = jnp.where(offsets[None, :] < 0, 0, 1 + halves * CPD + passed)
    return segment.reshape(2 * TOK_DP).astype(jnp.int32)

def group_attention(queries, key_rows, value_rows, segment):
    row_count = segment.shape[0]
    places = jnp.arange(row_count, dtype=jnp.int32)
    earlier = places[None, :] <= places[:, None]
    query_cont = segment[:, None] != 0
    allowed = (segment[None, :] == 0) & (query_cont | earlier) | (segment[None, :] == segment[:, None]) & query_cont & earlier

    def one_head(operands):
        query_head, key_head, value_head = operands
        scores = low_back(matmul(query_head, key_head.T))
        scores = jnp.where(allowed, scores, NEGATIVE)
        highest = lax.optimization_barrier(jnp.max(scores, axis=1, keepdims=True))
        weights = jnp.exp(scores - highest)
        shares = weights / lax.optimization_barrier(jnp.sum(weights, axis=1, keepdims=True))
        return matmul(low(low_back(shares)), value_head)
    return lax.map(jax.checkpoint(one_head), (queries, key_rows, value_rows))

def block_group(tokens, segment, params):
    query_weight, key_weight, value_weight, output_weight, up_weight, down_weight, attention_gain, feed_gain, query_scale = params
    row_count = tokens.shape[0]
    for layer_index in range(LAYERS):
        normed = low(norm_rows(tokens, attention_gain[layer_index]))
        query_raw = low_back(matmul(normed, query_weight[layer_index]))
        gain_q = softplus(query_scale[layer_index]) * LOG_TWO_E / math.sqrt(HD)
        queries = low(query_raw.reshape(row_count, HEADS, HD) * gain_q)
        key_rows = low(low_back(matmul(normed, key_weight[layer_index]))).reshape(row_count, HEADS, HD)
        value_rows = low(low_back(matmul(normed, value_weight[layer_index]))).reshape(row_count, HEADS, HD)
        mixed = group_attention(queries.transpose(1, 0, 2), key_rows.transpose(1, 0, 2), value_rows.transpose(1, 0, 2), segment)
        mixed = low(low_back(mixed.transpose(1, 0, 2).reshape(row_count, D)))
        middle = tokens + low_back(matmul(mixed, output_weight[layer_index]))
        normed_feed = low(norm_rows(middle, feed_gain[layer_index]))
        upper = low_back(matmul(normed_feed, up_weight[layer_index]))
        hidden = low(low_back(upper * jax.nn.sigmoid(upper)))
        tokens = middle + low_back(matmul(hidden, down_weight[layer_index]))
    return tokens

def reference(inputs, cotangent, query_weight, key_weight, value_weight, output_weight, up_weight, down_weight, attention_gain, feed_gain, query_scale, cont_lengths):
    pairs = cont_lengths.reshape(N_DP // 2, 2, CPD)
    segments = jax.vmap(group_segments)(pairs)
    params = (query_weight.astype(jnp.float32), key_weight.astype(jnp.float32), value_weight.astype(jnp.float32), output_weight.astype(jnp.float32), up_weight.astype(jnp.float32), down_weight.astype(jnp.float32), attention_gain, feed_gain, query_scale)

    def whole(tokens, weights):
        groups = tokens.reshape(N_DP // 2, 2 * TOK_DP, D)

        def one_group(operands):
            return block_group(operands[0], operands[1], weights)
        return lax.map(jax.checkpoint(one_group), (groups, segments)).reshape(TOKENS, D)
    result, pullback = jax.vjp(whole, inputs, params)
    grad_inputs, grad_params = pullback(cotangent)
    return (result, grad_inputs, grad_params[0], grad_params[1], grad_params[2], grad_params[3], grad_params[4], grad_params[5], grad_params[6], grad_params[7], grad_params[8])
```

```python
from functools import partial
import math

import jax
import jax.numpy as jnp
from jax import lax
from jax.sharding import PartitionSpec as P

HD = 80
LAYERS = 2
PROMPT_DEV = 512


EPSILON = 1e-06
LOG_TWO_E = 1.4426950408889634
NEGATIVE = -1e30


def from_partner(shard, axis, distance):
    return lax.ppermute(shard, axis, [(i, i ^ 1 << distance) for i in range(lax.axis_size(axis))])


def lowered(values):
    return values.astype(jnp.bfloat16)


def matmul(former, latter):
    return jnp.dot(former, latter, preferred_element_type=jnp.float32)


def inner_rows(former, latter):
    return lax.dot_general(
        former, latter, (((0,), (0,)), ((), ())), preferred_element_type=jnp.float32
    )


def inner_columns(former, latter):
    return lax.dot_general(
        former, latter, (((1,), (1,)), ((), ())), preferred_element_type=jnp.float32
    )


def inverse_root(source):
    return lax.rsqrt(jnp.mean(source * source, axis=1, keepdims=True) + EPSILON)


def softplus(values):
    return jnp.log1p(jnp.exp(values))


def split_heads(values):
    row_count = values.shape[0]
    return values.reshape(row_count, values.shape[1] // HD, HD).transpose(1, 0, 2)


def merge_heads(values):
    return values.transpose(1, 0, 2).reshape(values.shape[1], values.shape[0] * values.shape[2])


def norm_backward(source, inverse, gain_row, incoming):
    unit_rows = source * inverse
    gain_grad = jnp.sum(incoming * unit_rows, axis=0)
    scaled = incoming * gain_row
    return (
        gain_grad,
        inverse * (scaled - unit_rows * jnp.mean(scaled * unit_rows, axis=1, keepdims=True)),
    )


def segment_ids(lengths_row, total_rows):
    offsets = jnp.arange(total_rows, dtype=jnp.int32) - PROMPT_DEV
    bounds = jnp.cumsum(lengths_row)
    passed = jnp.sum((offsets[:, None] >= bounds[None, :]).astype(jnp.int32), axis=1)
    return jnp.where(offsets < 0, 0, 1 + passed)


def pair_swap(values, axis, bit):
    size = lax.axis_size(axis)
    return lax.ppermute(values, axis, [(i, i ^ bit) for i in range(size)])


def gather_orders(size):
    if size == 16:
        return ((8, 4, 2, 1), (8, 4, 1, 2), (1, 2, 8, 4), (8, 4, 1, 2), (1, 8, 4, 2), (2, 8, 4, 1))
    bits = tuple(1 << k for k in reversed(range(size.bit_length() - 1)))
    return (bits,) * 6


def my_bit(axis, bit):
    return (lax.axis_index(axis) & bit) != 0


def place_of(bit, done):
    return sum(1 for other in done if other > bit)


def doubled_gather(shard, order):
    values, done = shard, []
    for bit in order:
        other = pair_swap(values, "dp", bit)
        upper = my_bit("dp", bit)
        at = place_of(bit, done)
        values = jnp.stack(
            [jnp.where(upper, other, values), jnp.where(upper, values, other)], axis=at
        )
        done.append(bit)
    return values.reshape((-1, shard.shape[1]))


def halved_scatter(values, order):
    size = lax.axis_size("dp")
    width = values.shape[1]
    left = sorted(order, reverse=True)
    values = values.reshape((2,) * len(order) + (values.shape[0] // size, width))
    for bit in reversed(order):
        at = left.index(bit)
        left.remove(bit)
        upper = my_bit("dp", bit).astype(jnp.int32)
        keep = lax.dynamic_index_in_dim(values, upper, at, keepdims=False)
        send = lax.dynamic_index_in_dim(values, 1 - upper, at, keepdims=False)
        got = pair_swap(lowered(send), "dp", bit)
        values = keep.astype(jnp.float32) + got.astype(jnp.float32)
        if left:
            values = lowered(values)
    return values


def own_rows(values, axis="tensor"):
    count = values.shape[0] // lax.axis_size(axis)
    return lax.dynamic_slice_in_dim(values, lax.axis_index(axis) * count, count, 0)


def gather_rows(local_rows):
    if lax.axis_size("tensor") != 2:
        return lax.all_gather(local_rows, "tensor", axis=0, tiled=True)
    other = pair_swap(local_rows, "tensor", 1)
    upper = my_bit("tensor", 1)
    return jnp.concatenate(
        [jnp.where(upper, other, local_rows), jnp.where(upper, local_rows, other)], axis=0
    )


gather_grads = gather_rows


def scatter_rows(values, weight, product):
    if lax.axis_size("tensor") != 2:
        return lax.psum_scatter(
            lowered(product(values, weight)), "tensor", scatter_dimension=0, tiled=True
        ).astype(jnp.float32)
    count = values.shape[0] // 2
    place = lax.axis_index("tensor")
    theirs = lax.dynamic_slice_in_dim(values, (1 - place) * count, count, 0)
    got = pair_swap(lowered(product(theirs, weight)), "tensor", 1)
    mine = lax.dynamic_slice_in_dim(values, place * count, count, 0)
    return product(mine, weight) + got.astype(jnp.float32)


def reduce_rows(values, weight):
    return scatter_rows(values, weight, inner_columns)


def reduce_back(values, weight):
    return scatter_rows(values, weight, inner_columns)


def feed_gather(values):
    if lax.axis_size("tensor") != 2:
        return lax.all_gather(values, "tensor", axis=1, tiled=True)
    return jnp.concatenate([values, pair_swap(values, "tensor", 1)], axis=1)


def feed_scatter(values):
    if lax.axis_size("tensor") != 2:
        return lax.psum_scatter(
            lowered(values), "tensor", scatter_dimension=1, tiled=True
        ).astype(jnp.float32)
    count = values.shape[1] // 2
    got = pair_swap(lowered(values[:, count:]), "tensor", 1)
    return values[:, :count] + got.astype(jnp.float32)


def head_forward(allowed, operands):
    query_rows, key_rows, value_rows = operands
    scores = jnp.where(allowed, inner_columns(query_rows, key_rows), NEGATIVE)
    highest = jnp.max(scores, axis=1, keepdims=True)
    weights = jnp.exp(scores - highest)
    totals = jnp.sum(weights, axis=1, keepdims=True)
    shares_low = lowered(weights / totals)
    return (matmul(shares_low, value_rows), (highest + jnp.log(totals))[:, 0])


def head_backward(allowed, operands):
    query_rows, key_rows, value_rows, log_totals, grad_rows = operands
    scores = inner_columns(query_rows, key_rows)
    shares = jnp.exp(jnp.where(allowed, scores - log_totals[:, None], NEGATIVE))
    grad_shares = lowered(inner_columns(grad_rows, value_rows)).astype(jnp.float32)
    deltas = jnp.sum(shares * grad_shares, axis=1, keepdims=True)
    grad_scores = lowered(shares * (grad_shares - deltas))
    return (
        matmul(grad_scores, key_rows),
        inner_rows(grad_scores, query_rows),
        inner_rows(lowered(shares), grad_rows),
    )


def body(
    inputs,
    cotangent,
    query_weight,
    key_weight,
    value_weight,
    output_weight,
    up_weight,
    down_weight,
    attention_gain,
    feed_gain,
    query_scale,
    cont_lengths,
):
    row_total = inputs.shape[0] * lax.axis_size("tensor")
    local_width = query_weight.shape[2]
    pair_side = lax.axis_index("dp") % 2
    own_segment = segment_ids(cont_lengths[0], row_total)
    own_place = pair_side * row_total + jnp.arange(row_total, dtype=jnp.int32)
    far_place = (1 - pair_side) * row_total + jnp.arange(PROMPT_DEV, dtype=jnp.int32)
    key_segment = jnp.concatenate([jnp.zeros((PROMPT_DEV,), jnp.int32), own_segment])
    key_place = jnp.concatenate([far_place, own_place])
    earlier = key_place[None, :] <= own_place[:, None]
    query_cont = own_segment[:, None] != 0
    allowed = (key_segment[None, :] == 0) & (query_cont | earlier) | (
        key_segment[None, :] == own_segment[:, None]
    ) & query_cont & earlier
    forward_head = partial(head_forward, allowed)
    backward_head = partial(head_backward, allowed)
    orders = gather_orders(lax.axis_size("dp"))
    stored = []
    current = inputs
    for layer_index in range(LAYERS):
        shards = (
            query_weight[layer_index],
            key_weight[layer_index],
            value_weight[layer_index],
            output_weight[layer_index].T,
            up_weight[layer_index],
            down_weight[layer_index].T,
        )
        gathered = [doubled_gather(*member) for member in zip(shards, orders)]
        joint_weight = jnp.concatenate([gathered[0], gathered[1], gathered[2]], axis=1)
        out_weight = gathered[3]
        inverse_attn = inverse_root(current)
        normed_all = gather_rows(lowered(current * inverse_attn * attention_gain[layer_index]))
        joint = matmul(normed_all, joint_weight)
        query_raw = joint[:, :local_width]
        gain_q = softplus(query_scale[layer_index]) * LOG_TWO_E / math.sqrt(HD)
        query_low = lowered(query_raw.reshape(row_total, local_width // HD, HD) * gain_q).reshape(
            row_total, local_width
        )
        key_low = lowered(joint[:, local_width : 2 * local_width])
        value_low = lowered(joint[:, 2 * local_width :])
        far_keys, far_values = from_partner((key_low[:PROMPT_DEV], value_low[:PROMPT_DEV]), "dp", 0)
        key_all = jnp.concatenate([far_keys, key_low], axis=0)
        value_all = jnp.concatenate([far_values, value_low], axis=0)
        head_outs, log_totals = lax.map(
            forward_head, (split_heads(query_low), split_heads(key_all), split_heads(value_all))
        )
        mixed = lowered(merge_heads(head_outs))
        middle = current + reduce_rows(mixed, out_weight)
        inverse_feed = inverse_root(middle)
        feed_local = lowered(middle * inverse_feed * feed_gain[layer_index])
        upper_weight, lower_weight = feed_gather(gathered[4]), feed_gather(gathered[5])
        feed_rows = feed_local
        upper = matmul(feed_rows, upper_weight)
        hidden = lowered(upper * jax.nn.sigmoid(upper))
        branch_out = inner_columns(hidden, lower_weight)
        stored.append(
            (
                current,
                inverse_attn,
                normed_all,
                joint_weight,
                out_weight,
                query_raw,
                gain_q,
                query_low,
                key_all,
                value_all,
                log_totals,
                mixed,
                middle,
                inverse_feed,
                feed_rows,
                upper_weight,
                lower_weight,
                upper,
                hidden,
            )
        )
        current = middle + branch_out
    layer_grads = [None] * LAYERS
    attention_grads = [None] * LAYERS
    feed_grads = [None] * LAYERS
    scale_grads = [None] * LAYERS
    grad = cotangent
    for layer_index in reversed(range(LAYERS)):
        (
            source,
            inverse_attn,
            normed_all,
            joint_weight,
            out_weight,
            query_raw,
            gain_q,
            query_low,
            key_all,
            value_all,
            log_totals,
            mixed,
            middle,
            inverse_feed,
            feed_rows,
            upper_weight,
            lower_weight,
            upper,
            hidden,
        ) = stored[layer_index]
        grad_low = lowered(grad)
        down_grad = inner_rows(grad_low, hidden)
        hidden_grad = lowered(matmul(grad_low, lower_weight))
        sigmoid_upper = jax.nn.sigmoid(upper)
        upper_grad = lowered(
            hidden_grad.astype(jnp.float32)
            * (sigmoid_upper * (1.0 + upper * (1.0 - sigmoid_upper)))
        )
        up_grad = inner_rows(feed_rows, upper_grad)
        feed_grad = inner_columns(upper_grad, upper_weight)
        up_grad, down_grad = feed_scatter(up_grad), feed_scatter(down_grad)
        feed_gain_grad, middle_part = norm_backward(
            middle, inverse_feed, feed_gain[layer_index], feed_grad
        )
        grad_middle = grad + middle_part
        middle_rows = gather_grads(lowered(grad_middle))
        out_grad = inner_rows(middle_rows, mixed)
        mixed_grad = lowered(matmul(middle_rows, out_weight))
        query_grads, key_grads, value_grads = lax.map(
            backward_head,
            (
                split_heads(query_low),
                split_heads(key_all),
                split_heads(value_all),
                log_totals,
                split_heads(mixed_grad),
            ),
        )
        query_grad_rows = merge_heads(query_grads)
        key_grad_rows = merge_heads(key_grads)
        value_grad_rows = merge_heads(value_grads)
        back_keys, back_values = (
            from_partner(key_grad_rows[:PROMPT_DEV].astype(jnp.bfloat16), "dp", 0).astype(
                jnp.float32
            ),
            from_partner(value_grad_rows[:PROMPT_DEV].astype(jnp.bfloat16), "dp", 0).astype(
                jnp.float32
            ),
        )
        own_keys = key_grad_rows[PROMPT_DEV:]
        own_values = value_grad_rows[PROMPT_DEV:]
        own_keys = jnp.concatenate(
            [own_keys[:PROMPT_DEV] + back_keys, own_keys[PROMPT_DEV:]], axis=0
        )
        own_values = jnp.concatenate(
            [own_values[:PROMPT_DEV] + back_values, own_values[PROMPT_DEV:]], axis=0
        )
        query_heads = query_grad_rows.reshape(row_total, local_width // HD, HD)
        raw_heads = query_raw.reshape(row_total, local_width // HD, HD)
        scale_raw = jnp.sum(query_heads * raw_heads, axis=(0, 1))
        scale_grads[layer_index] = (
            scale_raw * jax.nn.sigmoid(query_scale[layer_index]) * LOG_TWO_E / math.sqrt(HD)
        )
        joint_grad = jnp.concatenate(
            [
                lowered(query_heads * gain_q).reshape(row_total, local_width),
                lowered(own_keys),
                lowered(own_values),
            ],
            axis=1,
        )
        joint_weight_grad = inner_rows(normed_all, joint_grad)
        normed_grad = reduce_back(joint_grad, joint_weight)
        attention_gain_grad, input_part = norm_backward(
            source, inverse_attn, attention_gain[layer_index], normed_grad
        )
        grad = grad_middle + input_part
        attention_grads[layer_index] = attention_gain_grad
        feed_grads[layer_index] = feed_gain_grad
        members = (
            joint_weight_grad[:, :local_width],
            joint_weight_grad[:, local_width : 2 * local_width],
            joint_weight_grad[:, 2 * local_width :],
            out_grad,
            up_grad,
            down_grad,
        )
        reduced = [
            halved_scatter(lowered(member), order) for member, order in zip(members, orders)
        ]
        reduced[3], reduced[5] = reduced[3].T, reduced[5].T
        layer_grads[layer_index] = reduced
    summed = [
        jnp.stack([layer_grads[depth_index][member] for depth_index in range(LAYERS)])
        for member in range(6)
    ]
    attention_total, feed_total, scale_total = lax.psum(
        (jnp.stack(attention_grads), jnp.stack(feed_grads), jnp.stack(scale_grads)),
        ("dp", "tensor"),
    )
    return (
        current,
        grad,
        summed[0],
        summed[1],
        summed[2],
        summed[3],
        summed[4],
        summed[5],
        attention_total,
        feed_total,
        scale_total,
    )


def solution(mesh):
    in_specs = (
        P(("dp", "tensor"), None),
        P(("dp", "tensor"), None),
        P(None, "dp", "tensor"),
        P(None, "dp", "tensor"),
        P(None, "dp", "tensor"),
        P(None, "tensor", "dp"),
        P(None, "dp", "tensor"),
        P(None, "tensor", "dp"),
        P(),
        P(),
        P(),
        P("dp", None),
    )
    out_specs = (
        P(("dp", "tensor"), None),
        P(("dp", "tensor"), None),
        P(None, "dp", "tensor"),
        P(None, "dp", "tensor"),
        P(None, "dp", "tensor"),
        P(None, "tensor", "dp"),
        P(None, "dp", "tensor"),
        P(None, "tensor", "dp"),
        P(),
        P(),
        P(),
    )
    return jax.shard_map(body, mesh=mesh, in_specs=in_specs, out_specs=out_specs, check_vma=False)
```

```python
from functools import partial
import math

import jax
import jax.numpy as jnp
from jax import lax
from jax.experimental import pallas as pl
from jax.experimental.pallas import tpu as pltpu
from jax.sharding import PartitionSpec as P

HD = 80
LAYERS = 2
PROMPT_DEV = 512
TILE = 256

EPSILON = 1e-06
LOG_TWO_E = 1.4426950408889634
LN_TWO = 0.6931471805599453
NEGATIVE = -1e30


def lowered(values):
    return values.astype(jnp.bfloat16)


def dot_nn(former, latter):
    return jnp.dot(former, latter, preferred_element_type=jnp.float32)


def dot_tn(former, latter):
    return lax.dot_general(
        former, latter, (((0,), (0,)), ((), ())), preferred_element_type=jnp.float32
    )


def dot_nt(former, latter):
    return lax.dot_general(
        former, latter, (((1,), (1,)), ((), ())), preferred_element_type=jnp.float32
    )


def inverse_root(source):
    return lax.rsqrt(jnp.mean(source * source, axis=0, keepdims=True) + EPSILON)


def softplus(values):
    return jnp.log1p(jnp.exp(values))


def norm_backward(source, inverse, gain, incoming):
    unit = source * inverse
    gain_grad = jnp.sum(incoming * unit, axis=1)
    scaled = incoming * gain
    return (
        gain_grad,
        inverse * (scaled - unit * jnp.mean(scaled * unit, axis=0, keepdims=True)),
    )


def pair_swap(values, axis, bit):
    size = lax.axis_size(axis)
    return lax.ppermute(values, axis, [(i, i ^ bit) for i in range(size)])


def my_bit(axis, bit):
    return (lax.axis_index(axis) & bit) != 0


def exchange_orders(size):
    if size == 16:
        return (8, 4, 2, 1), (8, 4, 1, 2), (1, 8, 4, 2), (2, 8, 4, 1)
    bits = tuple(1 << k for k in reversed(range(size.bit_length() - 1)))
    return (bits,) * 4


def doubled_gather(shards, order):
    values, done = shards, []
    for bit in order:
        other = pair_swap(values, "dp", bit)
        upper = my_bit("dp", bit)
        at = 1 + sum(1 for earlier in done if earlier > bit)
        values = jnp.stack(
            [jnp.where(upper, other, values), jnp.where(upper, values, other)], axis=at
        )
        done.append(bit)
    return values.reshape((shards.shape[0], -1, shards.shape[2]))


def halved_scatter(values, order):
    members, rows, width = values.shape
    left = sorted(order, reverse=True)
    values = values.reshape((members,) + (2,) * len(order) + (rows >> len(order), width))
    for bit in reversed(order):
        at = 1 + left.index(bit)
        left.remove(bit)
        upper = my_bit("dp", bit).astype(jnp.int32)
        keep = lax.dynamic_index_in_dim(values, upper, at, keepdims=False)
        send = lax.dynamic_index_in_dim(values, 1 - upper, at, keepdims=False)
        got = pair_swap(send, "dp", bit)
        values = keep.astype(jnp.float32) + got.astype(jnp.float32)
        if left:
            values = lowered(values)
    return values


def gather_tokens(local):
    if lax.axis_size("tensor") != 2:
        return lax.all_gather(local, "tensor", axis=1, tiled=True)
    other = pair_swap(local, "tensor", 1)
    upper = my_bit("tensor", 1)
    return jnp.concatenate([jnp.where(upper, other, local), jnp.where(upper, local, other)], axis=1)


def scatter_tokens(product, *values):
    if lax.axis_size("tensor") != 2:
        return lax.psum_scatter(
            lowered(product(*values)), "tensor", scatter_dimension=1, tiled=True
        ).astype(jnp.float32)
    count = values[0].shape[1] // 2
    place = lax.axis_index("tensor")
    theirs = [lax.dynamic_slice_in_dim(v, (1 - place) * count, count, 1) for v in values]
    got = pair_swap(lowered(product(*theirs)), "tensor", 1)
    mine = [lax.dynamic_slice_in_dim(v, place * count, count, 1) for v in values]
    return product(*mine) + got.astype(jnp.float32)


def feed_gather(values):
    if lax.axis_size("tensor") != 2:
        return lax.all_gather(values, "tensor", axis=1, tiled=True)
    return jnp.concatenate([values, pair_swap(values, "tensor", 1)], axis=1)


def feed_scatter(values):
    if lax.axis_size("tensor") != 2:
        return lax.psum_scatter(lowered(values), "tensor", scatter_dimension=1, tiled=True)
    count = values.shape[1] // 2
    got = pair_swap(lowered(values[:, count:]), "tensor", 1)
    return lowered(values[:, :count] + got.astype(jnp.float32))


def key_parts(tile):
    first = tile * TILE
    if first < PROMPT_DEV:
        return ([(0, first, "free")] if first else []) + [(first, TILE, "earlier")]
    return [(0, PROMPT_DEV, "free"), (PROMPT_DEV, first - PROMPT_DEV + TILE, "segment")]


def masked(scores, kind, first_key, first_query, start):
    if kind == "free":
        return scores
    key = lax.broadcasted_iota(jnp.int32, scores.shape, 0) + first_key
    query = lax.broadcasted_iota(jnp.int32, scores.shape, 1) + first_query
    allowed = key <= query
    if kind == "segment":
        allowed = allowed & (key >= start)
    return jnp.where(allowed, scores, NEGATIVE)


def forward_kernel(side_ref, start_ref, q_ref, kf_ref, ko_ref, vf_ref, vo_ref, out_ref, lse_ref):
    far_k = kf_ref[...].T
    own_k = ko_ref[...].T

    def work(tile, far):
        first = tile * TILE
        at = slice(first, first + TILE)
        query = q_ref[:, at]
        start = start_ref[:, at]
        parts = [(dot_nn(far_k, query), vf_ref[...])] if far else []
        for key, count, kind in key_parts(tile):
            scores = dot_nn(own_k[key : key + count], query)
            parts.append((masked(scores, kind, key, first, start), vo_ref[:, key : key + count]))
        highest = jnp.max(parts[0][0], axis=0, keepdims=True)
        for scores, _ in parts[1:]:
            highest = jnp.maximum(highest, jnp.max(scores, axis=0, keepdims=True))
        total, mixed = 0.0, 0.0
        for scores, value in parts:
            weights = jnp.exp2(scores - highest)
            total = total + jnp.sum(weights, axis=0, keepdims=True)
            mixed = mixed + dot_nn(value, lowered(weights))
        out_ref[:, at] = lowered(mixed / total)
        lse_ref[:, at] = highest + jnp.log2(total)

    tiles = range(q_ref.shape[1] // TILE)

    @pl.when(side_ref[0] == 0)
    def _():
        for tile in tiles:
            work(tile, tile * TILE >= PROMPT_DEV)

    @pl.when(side_ref[0] != 0)
    def _():
        for tile in tiles:
            work(tile, True)


def backward_kernel(
    side_ref,
    start_ref,
    q_ref,
    kf_ref,
    ko_ref,
    vf_ref,
    vo_ref,
    out_ref,
    grad_ref,
    lse_ref,
    dq_ref,
    dkf_ref,
    dko_ref,
    dvf_ref,
    dvo_ref,
    kf_total,
    ko_total,
    vf_total,
    vo_total,
):
    far = (kf_ref[...].T, vf_ref[...].T, kf_ref, kf_total, vf_total)
    own = (ko_ref[...].T, vo_ref[...].T, ko_ref, ko_total, vo_total)
    deltas = jnp.sum(
        out_ref[...].astype(jnp.float32) * grad_ref[...].astype(jnp.float32), axis=0, keepdims=True
    )

    def work(tile, with_far, seen):
        first = tile * TILE
        at = slice(first, first + TILE)
        query, grad = q_ref[:, at], grad_ref[:, at]
        start, lse, delta = start_ref[:, at], lse_ref[:, at], deltas[:, at]
        parts = [(far, 0, PROMPT_DEV, "free")] if with_far else []
        parts += [(own,) + part for part in key_parts(tile)]
        dq = 0.0
        for source, key, count, kind in parts:
            keys, values, keys_t, k_total, v_total = source
            scores = masked(dot_nn(keys[key : key + count], query), kind, key, first, start)
            shares = jnp.exp2(scores - lse)
            d_shares = dot_nn(values[key : key + count], grad)
            d_scores = lowered(shares * (d_shares - delta))
            dv = dot_nt(grad, lowered(shares))
            dk = dot_nt(query, d_scores)
            dq = dq + dot_nn(keys_t[:, key : key + count], d_scores)
            for offset in range(0, count, TILE):
                there = slice(key + offset, key + offset + TILE)
                here = slice(offset, offset + TILE)
                mark = (source is own, key + offset)
                if mark in seen:
                    k_total[:, there] += dk[:, here]
                    v_total[:, there] += dv[:, here]
                else:
                    seen.add(mark)
                    k_total[:, there] = dk[:, here]
                    v_total[:, there] = dv[:, here]
        dq_ref[:, at] = dq

    tiles = range(q_ref.shape[1] // TILE)

    @pl.when(side_ref[0] == 0)
    def _():
        seen = set()
        for tile in tiles:
            work(tile, tile * TILE >= PROMPT_DEV, seen)

    @pl.when(side_ref[0] != 0)
    def _():
        seen = set()
        for tile in tiles:
            work(tile, True, seen)

    dkf_ref[...] = lowered(kf_total[...] * LN_TWO)
    dko_ref[...] = lowered(ko_total[...] * LN_TWO)
    dvf_ref[...] = lowered(vf_total[...])
    dvo_ref[...] = lowered(vo_total[...])


def head_block(count):
    return pl.BlockSpec((HD, count), lambda head: (head, 0))


def attention_specs(tokens):
    return [
        pl.BlockSpec(memory_space=pltpu.SMEM),
        pl.BlockSpec((1, tokens), lambda head: (0, 0)),
        head_block(tokens),
        head_block(PROMPT_DEV),
        head_block(tokens),
        head_block(PROMPT_DEV),
        head_block(tokens),
    ]


def attention(side, start, queries, far_keys, own_keys, far_values, own_values):
    width, tokens = queries.shape
    heads = width // HD
    pairs = heads * tokens * (tokens + PROMPT_DEV)
    return pl.pallas_call(
        forward_kernel,
        grid=(heads,),
        in_specs=attention_specs(tokens),
        out_specs=[
            head_block(tokens),
            pl.BlockSpec((None, 1, tokens), lambda head: (head, 0, 0)),
        ],
        out_shape=[
            jax.ShapeDtypeStruct(queries.shape, jnp.bfloat16),
            jax.ShapeDtypeStruct((heads, 1, tokens), jnp.float32),
        ],
        compiler_params=pltpu.CompilerParams(vmem_limit_bytes=32 << 20),
        cost_estimate=pl.CostEstimate(
            flops=16 * HD * pairs, bytes_accessed=8 * width * tokens, transcendentals=pairs
        ),
        name="attention",
    )(side, start, queries, far_keys, own_keys, far_values, own_values)


def attention_back(
    side, start, queries, far_keys, own_keys, far_values, own_values, mixed, grads, lse
):
    width, tokens = queries.shape
    heads = width // HD
    pairs = heads * tokens * (tokens + PROMPT_DEV)
    far, own = (width, PROMPT_DEV), (width, tokens)
    return pl.pallas_call(
        backward_kernel,
        grid=(heads,),
        in_specs=attention_specs(tokens)
        + [
            head_block(tokens),
            head_block(tokens),
            pl.BlockSpec((None, 1, tokens), lambda head: (head, 0, 0)),
        ],
        out_specs=[head_block(count) for count in (tokens, PROMPT_DEV, tokens, PROMPT_DEV, tokens)],
        out_shape=[jax.ShapeDtypeStruct(own, jnp.float32)]
        + [jax.ShapeDtypeStruct(shape, jnp.bfloat16) for shape in (far, own, far, own)],
        scratch_shapes=[
            pltpu.VMEM((HD, count), jnp.float32)
            for count in (PROMPT_DEV, tokens, PROMPT_DEV, tokens)
        ],
        compiler_params=pltpu.CompilerParams(vmem_limit_bytes=32 << 20),
        cost_estimate=pl.CostEstimate(
            flops=32 * HD * pairs, bytes_accessed=20 * width * tokens, transcendentals=pairs
        ),
        name="attention_back",
    )(side, start, queries, far_keys, own_keys, far_values, own_values, mixed, grads, lse)


def segment_starts(lengths_row, tokens):
    place = jnp.arange(tokens, dtype=jnp.int32) - PROMPT_DEV
    bounds = jnp.cumsum(lengths_row)
    passed = jnp.where(place[:, None] >= bounds[None, :], bounds[None, :], 0)
    return (PROMPT_DEV + jnp.max(passed, axis=1))[None, :]


def body(
    inputs,
    cotangent,
    query_weight,
    key_weight,
    value_weight,
    output_weight,
    up_weight,
    down_weight,
    attention_gain,
    feed_gain,
    query_scale,
    cont_lengths,
):
    tokens = inputs.shape[0] * lax.axis_size("tensor")
    heads = query_weight.shape[2] // HD
    order_a, order_b, order_c, order_d = exchange_orders(lax.axis_size("dp"))
    side = (lax.axis_index("dp") % 2).astype(jnp.int32)[None]
    start = segment_starts(cont_lengths[0], tokens)

    def gathered(order, *members):
        return doubled_gather(jnp.stack(members), order)

    weights = []
    for layer in range(LAYERS):
        out_shard, down_shard = output_weight[layer].T, down_weight[layer].T
        if layer == 0:
            (wk,) = gathered(order_a, key_weight[layer])
            (wv,) = gathered(order_c, value_weight[layer])
            (wq,) = gathered(order_d, query_weight[layer])
            (wo,) = gathered(order_b, out_shard)
            (wu,) = gathered(order_c, up_weight[layer])
            (wd,) = gathered(order_d, down_shard)
        else:
            wk, wv = gathered(order_c, key_weight[layer], value_weight[layer])
            wq, wo = gathered(order_d, query_weight[layer], out_shard)
            wu, wd = gathered(order_b, up_weight[layer], down_shard)
        weights.append((wq, wk, wv, wo, wu, wd))

    gains, stored = [], []
    current = inputs.T
    for layer in range(LAYERS):
        wq, wk, wv, wo, wu, wd = weights[layer]
        attn_gain, ff_gain = attention_gain[layer][:, None], feed_gain[layer][:, None]
        inverse_attn = inverse_root(current)
        normed = gather_tokens(lowered(current * inverse_attn * attn_gain))
        keys = lowered(dot_tn(wk, normed))
        far_keys = pair_swap(keys[:, :PROMPT_DEV], "dp", 1)
        values = lowered(dot_tn(wv, normed))
        far_values = pair_swap(values[:, :PROMPT_DEV], "dp", 1)
        gain_q = softplus(query_scale[layer]) * LOG_TWO_E / math.sqrt(HD)
        gain_rows = jnp.tile(gain_q, heads)[:, None]
        queries = lowered(dot_tn(wq, normed) * (gain_rows * LOG_TWO_E))
        seen = (side, start, queries, far_keys, keys, far_values, values)
        mixed, lse = attention(*seen)
        middle = current + scatter_tokens(lambda rows: dot_nn(wo, rows), mixed)
        inverse_feed = inverse_root(middle)
        feed = lowered(middle * inverse_feed * ff_gain)
        wu, wd = feed_gather(wu), feed_gather(wd)
        upper = dot_tn(wu, feed)
        hidden = lowered(upper * jax.nn.sigmoid(upper))
        stored.append(
            (
                (current, inverse_attn, attn_gain, normed),
                (gain_q, gain_rows, seen, mixed, lse),
                (middle, inverse_feed, ff_gain, feed, upper, hidden),
                (wq, wk, wv, wo, wu, wd),
            )
        )
        current = middle + dot_nn(wd, hidden)

    layer_grads = [None] * LAYERS
    small_grads = [None] * LAYERS
    grad = cotangent.T
    for layer in reversed(range(LAYERS)):
        (
            (source, inverse_attn, attn_gain, normed),
            (gain_q, gain_rows, seen, mixed, lse),
            (middle, inverse_feed, ff_gain, feed, upper, hidden),
            (wq, wk, wv, wo, wu, wd),
        ) = stored[layer]
        grad_low = lowered(grad)
        down_grad = feed_scatter(dot_nt(grad_low, hidden))
        d_hidden = lowered(dot_tn(wd, grad_low)).astype(jnp.float32)
        sigmoid = jax.nn.sigmoid(upper)
        d_upper = lowered(d_hidden * (sigmoid * (1.0 + upper * (1.0 - sigmoid))))
        up_grad = feed_scatter(dot_nt(feed, d_upper))
        feed_gain_grad, part = norm_backward(middle, inverse_feed, ff_gain, dot_nn(wu, d_upper))
        grad_middle = grad + part
        middle_low = gather_tokens(lowered(grad_middle))
        d_mixed = lowered(dot_tn(wo, middle_low))
        out_grad = lowered(dot_nt(middle_low, mixed))
        dq, far_dk, own_dk, far_dv, own_dv = attention_back(*seen, mixed, d_mixed, lse)
        back_keys = pair_swap(far_dk, "dp", 1).astype(jnp.float32)
        back_values = pair_swap(far_dv, "dp", 1).astype(jnp.float32)
        pad = ((0, 0), (0, tokens - PROMPT_DEV))
        d_keys = lowered(own_dk.astype(jnp.float32) + jnp.pad(back_keys, pad))
        d_values = lowered(own_dv.astype(jnp.float32) + jnp.pad(back_values, pad))
        scale_raw = jnp.sum((dq * seen[2].astype(jnp.float32)).reshape(heads, HD, tokens), (0, 2))
        scale_raw = scale_raw / (gain_q * LOG_TWO_E)
        scale_grad = scale_raw * jax.nn.sigmoid(query_scale[layer]) * LOG_TWO_E / math.sqrt(HD)
        d_raw = lowered(dq * gain_rows)
        d_normed = scatter_tokens(
            lambda dq, dk, dv: dot_nn(wq, dq) + dot_nn(wk, dk) + dot_nn(wv, dv),
            d_raw,
            d_keys,
            d_values,
        )
        query_grad = lowered(dot_nt(normed, d_raw))
        key_grad = lowered(dot_nt(normed, d_keys))
        value_grad = lowered(dot_nt(normed, d_values))
        attn_gain_grad, part = norm_backward(source, inverse_attn, attn_gain, d_normed)
        grad = grad_middle + part
        small_grads[layer] = (attn_gain_grad, feed_gain_grad, scale_grad)

        def scattered(order, *members):
            return halved_scatter(jnp.stack(members), order)

        if layer == 0:
            (up_grad,) = scattered(order_c, up_grad)
            (down_grad,) = scattered(order_d, down_grad)
            (out_grad,) = scattered(order_b, out_grad)
            (query_grad,) = scattered(order_d, query_grad)
            (key_grad,) = scattered(order_a, key_grad)
            (value_grad,) = scattered(order_c, value_grad)
        else:
            up_grad, down_grad = scattered(order_b, up_grad, down_grad)
            query_grad, out_grad = scattered(order_d, query_grad, out_grad)
            key_grad, value_grad = scattered(order_c, key_grad, value_grad)
        layer_grads[layer] = (query_grad, key_grad, value_grad, out_grad.T, up_grad, down_grad.T)

    summed = [jnp.stack(members) for members in zip(*layer_grads)]
    small = lax.psum(tuple(jnp.stack(members) for members in zip(*small_grads)), ("dp", "tensor"))
    return (current.T, grad.T, *summed, *small)


def solution(mesh):
    in_specs = (
        P(("dp", "tensor"), None),
        P(("dp", "tensor"), None),
        P(None, "dp", "tensor"),
        P(None, "dp", "tensor"),
        P(None, "dp", "tensor"),
        P(None, "tensor", "dp"),
        P(None, "dp", "tensor"),
        P(None, "tensor", "dp"),
        P(),
        P(),
        P(),
        P("dp", None),
    )
    out_specs = (
        P(("dp", "tensor"), None),
        P(("dp", "tensor"), None),
        P(None, "dp", "tensor"),
        P(None, "dp", "tensor"),
        P(None, "dp", "tensor"),
        P(None, "tensor", "dp"),
        P(None, "dp", "tensor"),
        P(None, "tensor", "dp"),
        P(),
        P(),
        P(),
    )
    return jax.shard_map(body, mesh=mesh, in_specs=in_specs, out_specs=out_specs, check_vma=False)
```

```python
from functools import partial
import math

import jax
import jax.numpy as jnp
from jax import lax
from jax.experimental import pallas as pl
from jax.experimental.pallas import tpu as pltpu
from jax.sharding import PartitionSpec as P

HD = 80
LAYERS = 2
PROMPT_DEV = 512
TILE = 256

EPSILON = 1e-06
LOG_TWO_E = 1.4426950408889634
LN_TWO = 0.6931471805599453
NEGATIVE = -1e30


def lowered(values):
    return values.astype(jnp.bfloat16)


def dot_nn(former, latter):
    return jnp.dot(former, latter, preferred_element_type=jnp.float32)


def dot_tn(former, latter):
    return lax.dot_general(
        former, latter, (((0,), (0,)), ((), ())), preferred_element_type=jnp.float32
    )


def dot_nt(former, latter):
    return lax.dot_general(
        former, latter, (((1,), (1,)), ((), ())), preferred_element_type=jnp.float32
    )


def inverse_root(source):
    return lax.rsqrt(jnp.mean(source * source, axis=0, keepdims=True) + EPSILON)


def softplus(values):
    return jnp.log1p(jnp.exp(values))


def norm_backward(source, inverse, gain, incoming):
    unit = source * inverse
    gain_grad = jnp.sum(incoming * unit, axis=1)
    scaled = incoming * gain
    return (
        gain_grad,
        inverse * (scaled - unit * jnp.mean(scaled * unit, axis=0, keepdims=True)),
    )


def pair_swap(values, axis, bit):
    size = lax.axis_size(axis)
    return lax.ppermute(values, axis, [(i, i ^ bit) for i in range(size)])


def my_bit(axis, bit):
    return (lax.axis_index(axis) & bit) != 0


def exchange_orders(size):
    if size == 16:
        return (8, 4, 2, 1), (8, 4, 1, 2), (1, 2, 8, 4)
    bits = tuple(1 << k for k in reversed(range(size.bit_length() - 1)))
    return (bits,) * 3


def zero_after(values):
    corner = values[(0,) * values.ndim]
    return jnp.minimum((corner.astype(jnp.float32) > 3e38).astype(jnp.int32), 0)


def doubled_gather(shard, order):
    values, done, marks = shard, [], []
    for bit in order:
        other = pair_swap(values, "dp", bit)
        marks.append(other)
        upper = my_bit("dp", bit)
        at = sum(1 for earlier in done if earlier > bit)
        values = jnp.stack(
            [jnp.where(upper, other, values), jnp.where(upper, values, other)], axis=at
        )
        done.append(bit)
    return values.reshape((-1, shard.shape[1])), zero_after(marks[-2])


def halved_scatter(values, order):
    rows, width = values.shape
    left = sorted(order, reverse=True)
    values = values.reshape((2,) * len(order) + (rows >> len(order), width))
    for bit in reversed(order):
        at = left.index(bit)
        left.remove(bit)
        upper = my_bit("dp", bit).astype(jnp.int32)
        keep = lax.dynamic_index_in_dim(values, upper, at, keepdims=False)
        send = lax.dynamic_index_in_dim(values, 1 - upper, at, keepdims=False)
        got = pair_swap(send, "dp", bit)
        values = keep.astype(jnp.float32) + got.astype(jnp.float32)
        if left:
            values = lowered(values)
    return values


def total_sum(values):
    for axis in ("tensor", "dp"):
        bit = 1
        while bit < lax.axis_size(axis):
            values = values + pair_swap(values, axis, bit)
            bit *= 2
    return values


def gather_tokens(local):
    if lax.axis_size("tensor") != 2:
        return lax.all_gather(local, "tensor", axis=1, tiled=True)
    other = pair_swap(local, "tensor", 1)
    upper = my_bit("tensor", 1)
    return jnp.concatenate([jnp.where(upper, other, local), jnp.where(upper, local, other)], axis=1)


def far_tokens(normed):
    part = PROMPT_DEV // lax.axis_size("tensor")
    place = lax.axis_index("tensor") * part
    return gather_tokens(pair_swap(lax.dynamic_slice_in_dim(normed, place, part, 1), "dp", 1))


def scatter_tokens(product, *values):
    if lax.axis_size("tensor") != 2:
        return lax.psum_scatter(
            lowered(product(*values)), "tensor", scatter_dimension=1, tiled=True
        ).astype(jnp.float32)
    count = values[0].shape[1] // 2
    place = lax.axis_index("tensor")
    theirs = [lax.dynamic_slice_in_dim(v, (1 - place) * count, count, 1) for v in values]
    got = pair_swap(lowered(product(*theirs)), "tensor", 1)
    mine = [lax.dynamic_slice_in_dim(v, place * count, count, 1) for v in values]
    return product(*mine) + got.astype(jnp.float32)


def feed_gather(values):
    if lax.axis_size("tensor") != 2:
        return lax.all_gather(values, "tensor", axis=1, tiled=True)
    return jnp.concatenate([values, pair_swap(values, "tensor", 1)], axis=1)


def feed_scatter(values):
    if lax.axis_size("tensor") != 2:
        return lax.psum_scatter(lowered(values), "tensor", scatter_dimension=1, tiled=True)
    count = values.shape[1] // 2
    got = pair_swap(lowered(values[:, count:]), "tensor", 1)
    return lowered(values[:, :count] + got.astype(jnp.float32))


def key_parts(tile):
    first = tile * TILE
    if first < PROMPT_DEV:
        return ([(0, first, "free")] if first else []) + [(first, TILE, "earlier")]
    return [(0, PROMPT_DEV, "free"), (PROMPT_DEV, first - PROMPT_DEV + TILE, "segment")]


def masked(scores, kind, first_key, first_query, start):
    if kind == "free":
        return scores
    key = lax.broadcasted_iota(jnp.int32, scores.shape, 0) + first_key
    query = lax.broadcasted_iota(jnp.int32, scores.shape, 1) + first_query
    allowed = key <= query
    if kind == "segment":
        allowed = allowed & (key >= start)
    return jnp.where(allowed, scores, NEGATIVE)


def spans(reference):
    tokens = reference.shape[1]
    return [(tile, slice(tile * TILE, tile * TILE + TILE)) for tile in range(tokens // TILE)]


def by_side(side_ref, reference, meets, skips):
    prompt = [at for tile, at in spans(reference) if tile * TILE < PROMPT_DEV]

    @pl.when(side_ref[0] == 0)
    def _():
        for at in prompt:
            skips(at)

    @pl.when(side_ref[0] != 0)
    def _():
        for at in prompt:
            meets(at)

    for tile, at in spans(reference):
        if at not in prompt:
            meets(at)


def own_forward(start_ref, q_ref, k_ref, v_ref, sum_ref, top_ref, total_ref):
    keys = k_ref[...].T
    for tile, at in spans(q_ref):
        query, start = q_ref[:, at], start_ref[:, at]
        parts = []
        for key, count, kind in key_parts(tile):
            scores = dot_nn(keys[key : key + count], query)
            scores = masked(scores, kind, key, tile * TILE, start)
            parts.append((scores, v_ref[:, key : key + count]))
        highest = jnp.max(parts[0][0], axis=0, keepdims=True)
        for scores, _ in parts[1:]:
            highest = jnp.maximum(highest, jnp.max(scores, axis=0, keepdims=True))
        total, mixed = 0.0, 0.0
        for scores, value in parts:
            weights = jnp.exp2(scores - highest)
            total = total + jnp.sum(weights, axis=0, keepdims=True)
            mixed = mixed + dot_nn(value, lowered(weights))
        sum_ref[:, at] = mixed
        top_ref[:, at] = highest
        total_ref[:, at] = total


def far_forward(
    side_ref, q_ref, k_ref, v_ref, sum_ref, top_ref, total_ref, out_ref, lse_ref
):
    keys = k_ref[...].T

    def meets(at):
        scores = dot_nn(keys, q_ref[:, at])
        highest = jnp.maximum(top_ref[:, at], jnp.max(scores, axis=0, keepdims=True))
        weights = jnp.exp2(scores - highest)
        scale = jnp.exp2(top_ref[:, at] - highest)
        total = total_ref[:, at] * scale + jnp.sum(weights, axis=0, keepdims=True)
        mixed = sum_ref[:, at] * scale + dot_nn(v_ref[...], lowered(weights))
        out_ref[:, at] = lowered(mixed / total)
        lse_ref[:, at] = highest + jnp.log2(total)

    def skips(at):
        out_ref[:, at] = lowered(sum_ref[:, at] / total_ref[:, at])
        lse_ref[:, at] = top_ref[:, at] + jnp.log2(total_ref[:, at])

    by_side(side_ref, q_ref, meets, skips)


def score_grads(scores, lse, d_shares, delta):
    shares = jnp.exp2(scores - lse)
    return lowered(shares), lowered(shares * (d_shares - delta))


def far_backward(
    side_ref, q_ref, k_ref, v_ref, out_ref, grad_ref, lse_ref, dq_ref, delta_ref, dk_ref, dv_ref
):
    keys, values = k_ref[...].T, v_ref[...].T
    delta_ref[...] = jnp.sum(
        out_ref[...].astype(jnp.float32) * grad_ref[...].astype(jnp.float32), axis=0, keepdims=True
    )

    def terms(at):
        query, grad = q_ref[:, at], grad_ref[:, at]
        shares, d_scores = score_grads(
            dot_nn(keys, query), lse_ref[:, at], dot_nn(values, grad), delta_ref[:, at]
        )
        dq_ref[:, at] = dot_nn(k_ref[...], d_scores)
        return dot_nt(query, d_scores), dot_nt(grad, shares)

    def close(tiles):
        dk, dv = 0.0, 0.0
        for at in tiles:
            k_term, v_term = terms(at)
            dk, dv = dk + k_term, dv + v_term
        dk_ref[...] = lowered(dk * LN_TWO)
        dv_ref[...] = lowered(dv)

    tiles = [at for _, at in spans(q_ref)]
    conts = [at for tile, at in spans(q_ref) if tile * TILE >= PROMPT_DEV]

    @pl.when(side_ref[0] == 0)
    def _():
        for at in tiles:
            if at not in conts:
                dq_ref[:, at] = jnp.zeros_like(dq_ref[:, at])
        close(conts)

    @pl.when(side_ref[0] != 0)
    def _():
        close(tiles)


def own_backward(
    start_ref,
    gain_ref,
    q_ref,
    k_ref,
    v_ref,
    grad_ref,
    lse_ref,
    delta_ref,
    far_dq_ref,
    dq_ref,
    dk_ref,
    dv_ref,
    scale_ref,
    k_total,
    v_total,
):
    keys, values = k_ref[...].T, v_ref[...].T
    seen = set()
    scale = 0.0
    for tile, at in spans(q_ref):
        query, grad = q_ref[:, at], grad_ref[:, at]
        dq = far_dq_ref[:, at]
        for key, count, kind in key_parts(tile):
            scores = dot_nn(keys[key : key + count], query)
            scores = masked(scores, kind, key, tile * TILE, start_ref[:, at])
            shares, d_scores = score_grads(
                scores, lse_ref[:, at], dot_nn(values[key : key + count], grad), delta_ref[:, at]
            )
            dv = dot_nt(grad, shares)
            dk = dot_nt(query, d_scores)
            dq = dq + dot_nn(k_ref[:, key : key + count], d_scores)
            for offset in range(0, count, TILE):
                there = slice(key + offset, key + offset + TILE)
                here = slice(offset, offset + TILE)
                if key + offset in seen:
                    k_total[:, there] += dk[:, here]
                    v_total[:, there] += dv[:, here]
                else:
                    seen.add(key + offset)
                    k_total[:, there] = dk[:, here]
                    v_total[:, there] = dv[:, here]
        dq_ref[:, at] = lowered(dq * gain_ref[...])
        scale = scale + jnp.sum(dq * query.astype(jnp.float32), axis=1, keepdims=True)
    dk_ref[...] = lowered(k_total[...] * LN_TWO)
    dv_ref[...] = lowered(v_total[...])
    scale_ref[...] = scale


SCALAR = pl.BlockSpec(memory_space=pltpu.SMEM)


def rows_block(count):
    return pl.BlockSpec((HD, count), lambda head: (head, 0))


def flat_block(count):
    return pl.BlockSpec((None, 1, count), lambda head: (head, 0, 0))


def same_block(*shape):
    return pl.BlockSpec(shape, lambda head: (0, 0))


def per_head(kernel, name, heads, area, products, ins, outs, scratch=()):
    flops = 2 * 256 * area * heads * products
    moved = sum(array.size * array.dtype.itemsize for _, array in ins)
    return pl.pallas_call(
        kernel,
        grid=(heads,),
        in_specs=[spec for spec, _ in ins],
        out_specs=[spec for spec, _, _ in outs],
        out_shape=[jax.ShapeDtypeStruct(shape, kind) for _, shape, kind in outs],
        scratch_shapes=list(scratch),
        compiler_params=pltpu.CompilerParams(vmem_limit_bytes=32 << 20),
        cost_estimate=pl.CostEstimate(
            flops=flops, bytes_accessed=moved, transcendentals=area * heads
        ),
        name=name,
    )(*[array for _, array in ins])


def attention_own(start, queries, keys, values):
    width, tokens = queries.shape
    heads = width // HD
    all_rows, flat = rows_block(tokens), flat_block(tokens)
    return per_head(
        own_forward,
        "attention_own",
        heads,
        tokens * tokens * 5 // 8,
        3,
        [
            (same_block(1, tokens), start),
            (all_rows, queries),
            (all_rows, keys),
            (all_rows, values),
        ],
        [
            (all_rows, (width, tokens), jnp.float32),
            (flat, (heads, 1, tokens), jnp.float32),
            (flat, (heads, 1, tokens), jnp.float32),
        ],
    )


def attention_far(side, queries, keys, values, partial_sum, top, total):
    width, tokens = queries.shape
    heads = width // HD
    all_rows, flat, far_rows = rows_block(tokens), flat_block(tokens), rows_block(PROMPT_DEV)
    return per_head(
        far_forward,
        "attention_far",
        heads,
        tokens * PROMPT_DEV,
        3,
        [
            (SCALAR, side),
            (all_rows, queries),
            (far_rows, keys),
            (far_rows, values),
            (all_rows, partial_sum),
            (flat, top),
            (flat, total),
        ],
        [
            (all_rows, (width, tokens), jnp.bfloat16),
            (flat, (heads, 1, tokens), jnp.float32),
        ],
    )


def attention_far_back(side, queries, keys, values, mixed, grads, lse):
    width, tokens = queries.shape
    heads = width // HD
    all_rows, flat, far_rows = rows_block(tokens), flat_block(tokens), rows_block(PROMPT_DEV)
    return per_head(
        far_backward,
        "attention_far_back",
        heads,
        tokens * PROMPT_DEV,
        6,
        [
            (SCALAR, side),
            (all_rows, queries),
            (far_rows, keys),
            (far_rows, values),
            (all_rows, mixed),
            (all_rows, grads),
            (flat, lse),
        ],
        [
            (all_rows, (width, tokens), jnp.float32),
            (flat, (heads, 1, tokens), jnp.float32),
            (far_rows, (width, PROMPT_DEV), jnp.bfloat16),
            (far_rows, (width, PROMPT_DEV), jnp.bfloat16),
        ],
    )


def attention_own_back(start, gain, queries, keys, values, grads, lse, delta, far_dq):
    width, tokens = queries.shape
    heads = width // HD
    all_rows, flat = rows_block(tokens), flat_block(tokens)
    return per_head(
        own_backward,
        "attention_own_back",
        heads,
        tokens * tokens * 5 // 8,
        6,
        [
            (same_block(1, tokens), start),
            (same_block(HD, 1), gain),
            (all_rows, queries),
            (all_rows, keys),
            (all_rows, values),
            (all_rows, grads),
            (flat, lse),
            (flat, delta),
            (all_rows, far_dq),
        ],
        [
            (all_rows, (width, tokens), jnp.bfloat16),
            (all_rows, (width, tokens), jnp.bfloat16),
            (all_rows, (width, tokens), jnp.bfloat16),
            (pl.BlockSpec((HD, 1), lambda head: (head, 0)), (width, 1), jnp.float32),
        ],
        [pltpu.VMEM((HD, tokens), jnp.float32)] * 2,
    )


def segment_starts(lengths_row, tokens):
    place = jnp.arange(tokens, dtype=jnp.int32) - PROMPT_DEV
    bounds = jnp.cumsum(lengths_row)
    passed = jnp.where(place[:, None] >= bounds[None, :], bounds[None, :], 0)
    return (PROMPT_DEV + jnp.max(passed, axis=1))[None, :]


def body(
    inputs,
    cotangent,
    query_weight,
    key_weight,
    value_weight,
    output_weight,
    up_weight,
    down_weight,
    attention_gain,
    feed_gain,
    query_scale,
    cont_lengths,
):
    tokens = inputs.shape[0] * lax.axis_size("tensor")
    heads = query_weight.shape[2] // HD
    orders = exchange_orders(lax.axis_size("dp"))
    side = (lax.axis_index("dp") % 2).astype(jnp.int32)[None]
    start = segment_starts(cont_lengths[0], tokens)

    weights = []
    waits = [jnp.int32(0)] * 3
    for layer in range(LAYERS):
        members = (
            (key_weight, False),
            (value_weight, False),
            (query_weight, False),
            (output_weight, True),
            (up_weight, False),
            (down_weight, True),
        )
        full = []
        for place, (member, flip) in enumerate(members):
            lane = place % 3
            shard = lax.dynamic_index_in_dim(member, layer + waits[lane], 0, keepdims=False)
            whole, waits[lane] = doubled_gather(shard.T if flip else shard, orders[lane])
            full.append(whole)
        weights.append(full)

    stored = []
    current = inputs.T
    for layer in range(LAYERS):
        wk, wv, wq, wo, wu, wd = weights[layer]
        attn_gain, ff_gain = attention_gain[layer][:, None], feed_gain[layer][:, None]
        inverse_attn = inverse_root(current)
        normed = gather_tokens(lowered(current * inverse_attn * attn_gain))
        far_normed = far_tokens(normed)
        keys = lowered(dot_tn(wk, normed))
        values = lowered(dot_tn(wv, normed))
        gain_q = softplus(query_scale[layer]) * LOG_TWO_E / math.sqrt(HD)
        gain_rows = jnp.tile(gain_q, heads)[:, None]
        queries = lowered(dot_tn(wq, normed) * (gain_rows * LOG_TWO_E))
        partial_sum = attention_own(start, queries, keys, values)
        far_keys = lowered(dot_tn(wk, far_normed))
        far_values = lowered(dot_tn(wv, far_normed))
        mixed, lse = attention_far(side, queries, far_keys, far_values, *partial_sum)
        middle = current + scatter_tokens(lambda rows: dot_nn(wo, rows), mixed)
        inverse_feed = inverse_root(middle)
        feed = lowered(middle * inverse_feed * ff_gain)
        wu, wd = feed_gather(wu), feed_gather(wd)
        upper = dot_tn(wu, feed)
        hidden = lowered(upper * jax.nn.sigmoid(upper))
        stored.append(
            (
                (current, inverse_attn, attn_gain, normed),
                (gain_q, queries, keys, values, far_keys, far_values, mixed, lse),
                (middle, inverse_feed, ff_gain, feed, upper, hidden),
                (wk, wv, wq, wo, wu, wd),
            )
        )
        current = middle + dot_nn(wd, hidden)

    layer_grads = [None] * LAYERS
    small_grads = [None] * LAYERS
    grad = cotangent.T
    for layer in reversed(range(LAYERS)):
        (
            (source, inverse_attn, attn_gain, normed),
            (gain_q, queries, keys, values, far_keys, far_values, mixed, lse),
            (middle, inverse_feed, ff_gain, feed, upper, hidden),
            (wk, wv, wq, wo, wu, wd),
        ) = stored[layer]
        grad_low = lowered(grad)
        down_grad = feed_scatter(dot_nt(grad_low, hidden))
        d_hidden = lowered(dot_tn(wd, grad_low)).astype(jnp.float32)
        sigmoid = jax.nn.sigmoid(upper)
        d_upper = lowered(d_hidden * (sigmoid * (1.0 + upper * (1.0 - sigmoid))))
        up_grad = feed_scatter(dot_nt(feed, d_upper))
        feed_gain_grad, part = norm_backward(middle, inverse_feed, ff_gain, dot_nn(wu, d_upper))
        grad_middle = grad + part
        middle_low = gather_tokens(lowered(grad_middle))
        d_mixed = lowered(dot_tn(wo, middle_low))
        far_dq, delta, far_dk, far_dv = attention_far_back(
            side, queries, far_keys, far_values, mixed, d_mixed, lse
        )
        back_keys = pair_swap(far_dk, "dp", 1).astype(jnp.float32)
        back_values = pair_swap(far_dv, "dp", 1).astype(jnp.float32)
        out_grad = lowered(dot_nt(middle_low, mixed))
        d_raw, own_dk, own_dv, scale_rows = attention_own_back(
            start, gain_q[:, None], queries, keys, values, d_mixed, lse, delta, far_dq
        )
        pad = ((0, 0), (0, tokens - PROMPT_DEV))
        d_keys = lowered(own_dk.astype(jnp.float32) + jnp.pad(back_keys, pad))
        d_values = lowered(own_dv.astype(jnp.float32) + jnp.pad(back_values, pad))
        scale_raw = jnp.sum(scale_rows.reshape(heads, HD), 0) / (gain_q * LOG_TWO_E)
        scale_grad = scale_raw * jax.nn.sigmoid(query_scale[layer]) * LOG_TWO_E / math.sqrt(HD)
        d_normed = scatter_tokens(
            lambda dq, dk, dv: dot_nn(wq, dq) + dot_nn(wk, dk) + dot_nn(wv, dv),
            d_raw,
            d_keys,
            d_values,
        )
        query_grad = lowered(dot_nt(normed, d_raw))
        key_grad = lowered(dot_nt(normed, d_keys))
        value_grad = lowered(dot_nt(normed, d_values))
        attn_gain_grad, part = norm_backward(source, inverse_attn, attn_gain, d_normed)
        grad = grad_middle + part
        small_grads[layer] = jnp.concatenate([attn_gain_grad, feed_gain_grad, scale_grad])
        down_grad, up_grad, out_grad, query_grad, key_grad, value_grad = [
            halved_scatter(member, orders[place % 3])
            for place, member in enumerate(
                (down_grad, up_grad, out_grad, query_grad, key_grad, value_grad)
            )
        ]
        layer_grads[layer] = (query_grad, key_grad, value_grad, out_grad.T, up_grad, down_grad.T)

    summed = [jnp.stack(members) for members in zip(*layer_grads)]
    small = total_sum(jnp.stack(small_grads))
    width = current.shape[0]
    return (
        current.T,
        grad.T,
        *summed,
        small[:, :width],
        small[:, width : 2 * width],
        small[:, 2 * width :],
    )


def solution(mesh):
    in_specs = (
        P(("dp", "tensor"), None),
        P(("dp", "tensor"), None),
        P(None, "dp", "tensor"),
        P(None, "dp", "tensor"),
        P(None, "dp", "tensor"),
        P(None, "tensor", "dp"),
        P(None, "dp", "tensor"),
        P(None, "tensor", "dp"),
        P(),
        P(),
        P(),
        P("dp", None),
    )
    out_specs = (
        P(("dp", "tensor"), None),
        P(("dp", "tensor"), None),
        P(None, "dp", "tensor"),
        P(None, "dp", "tensor"),
        P(None, "dp", "tensor"),
        P(None, "tensor", "dp"),
        P(None, "dp", "tensor"),
        P(None, "tensor", "dp"),
        P(),
        P(),
        P(),
    )
    return jax.shard_map(body, mesh=mesh, in_specs=in_specs, out_specs=out_specs, check_vma=False)
```

```python
from functools import partial
import math

import jax
import jax.numpy as jnp
from jax import lax
from jax.experimental import pallas as pl
from jax.experimental.pallas import tpu as pltpu
from jax.sharding import PartitionSpec as P

HD = 80
LAYERS = 2
PROMPT_DEV = 512
TILE = 256

EPSILON = 1e-06
LOG_TWO_E = 1.4426950408889634
LN_TWO = 0.6931471805599453
NEGATIVE = -1e30


def lowered(values):
    return values.astype(jnp.bfloat16)


def dot_nn(former, latter):
    return jnp.dot(former, latter, preferred_element_type=jnp.float32)


def dot_tn(former, latter):
    return lax.dot_general(
        former, latter, (((0,), (0,)), ((), ())), preferred_element_type=jnp.float32
    )


def dot_nt(former, latter):
    return lax.dot_general(
        former, latter, (((1,), (1,)), ((), ())), preferred_element_type=jnp.float32
    )


def inverse_root(source):
    return lax.rsqrt(jnp.mean(source * source, axis=0, keepdims=True) + EPSILON)


def softplus(values):
    return jnp.log1p(jnp.exp(values))


def norm_backward(source, inverse, gain, incoming):
    unit = source * inverse
    gain_grad = jnp.sum(incoming * unit, axis=1)
    scaled = incoming * gain
    return (
        gain_grad,
        inverse * (scaled - unit * jnp.mean(scaled * unit, axis=0, keepdims=True)),
    )


def pair_swap(values, axis, bit):
    size = lax.axis_size(axis)
    return lax.ppermute(values, axis, [(i, i ^ bit) for i in range(size)])


def exchange_orders(size):
    if size == 16:
        return (8, 4), ((2, 1), (1, 2))
    bits = tuple(1 << k for k in reversed(range(size.bit_length() - 1)))
    first, rest = bits[:1], bits[1:]
    half = len(rest) // 2
    return first, (rest, rest[half:] + rest[:half])


WHOLE = pl.BlockSpec(memory_space=pltpu.VMEM)
SCALAR = pl.BlockSpec(memory_space=pltpu.SMEM)
UNREAD = pl.BlockSpec(memory_space=pl.ANY)


def dp_bits(bits):
    place = lax.axis_index("dp")
    return jnp.stack([((place & bit) != 0).astype(jnp.int32) for bit in bits])


def quick_call(kernel, name, arrays, after, out_shape):
    out = pl.pallas_call(
        kernel,
        in_specs=[SCALAR] + [WHOLE] * (len(arrays) - 1) + [UNREAD] * len(after),
        out_specs=[WHOLE] * len(out_shape),
        out_shape=out_shape,
        compiler_params=pltpu.CompilerParams(vmem_limit_bytes=48 << 20),
        cost_estimate=pl.CostEstimate(flops=1, bytes_accessed=1, transcendentals=0),
        name=name,
    )(*arrays, *after)
    return list(out)


class Gather:
    def __init__(self, pairs, orders):
        self.first, self.rest = orders
        self.queue = [jnp.stack(pair)[:, None] for pair in pairs]
        self.early, self.early_at = None, 0
        self.late, self.late_at = None, 0
        self.ready = []

    def tick(self, *after):
        if self.early is None and self.queue:
            self.early, self.early_at = self.queue.pop(0), 0
        if self.late is None and self.early is not None and self.early_at == len(self.first):
            self.late, self.late_at = self.early, 0
            self.early, self.early_at = (self.queue.pop(0), 0) if self.queue else (None, 0)
        jobs = []
        early = self.early is not None and self.early_at < len(self.first)
        if early:
            jobs.append((self.early, self.first[: self.early_at + 1]))
        if self.late is not None:
            for values, order in zip(self.late, self.rest):
                jobs.append((values, self.first + order[: self.late_at + 1]))
        if not jobs:
            return []
        got = [pair_swap(values, "dp", done[-1]) for values, done in jobs]
        plans, shapes = [], []
        for values, done in jobs:
            members, blocks, rows, width = values.shape
            before = 1 << sum(1 for bit in done[:-1] if bit > done[-1])
            parts = members if members > 1 and len(done) == len(self.first) else 1
            plans.append((members, before, blocks // before, parts, len(shapes)))
            shapes += [(members // parts, 2 * blocks, rows, width)] * parts
        count = len(jobs)

        def join(bit_ref, *refs):
            outs = refs[len(refs) - len(shapes) :]
            for job, (members, before, blocks, parts, at) in enumerate(plans):
                bit = bit_ref[job]
                for member in range(members):
                    out, row = (outs[at + member], 0) if parts > 1 else (outs[at], member)
                    for step in range(before):
                        here = pl.ds(step * blocks, blocks)
                        place = 2 * step * blocks
                        ours, theirs = place + bit * blocks, place + (1 - bit) * blocks
                        out[row, pl.ds(ours, blocks)] = refs[job][member, here]
                        out[row, pl.ds(theirs, blocks)] = refs[count + job][member, here]

        outs = quick_call(
            join,
            "join_halves",
            [dp_bits([done[-1] for _, done in jobs]), *[values for values, _ in jobs], *got],
            after,
            [jax.ShapeDtypeStruct(shape, jnp.bfloat16) for shape in shapes],
        )
        if early:
            self.early_at += 1
            done = self.early_at == len(self.first)
            self.early = outs[:2] if done else outs[0]
        if self.late is not None:
            self.late, self.late_at = outs[-2:], self.late_at + 1
            if self.late_at == len(self.rest[0]):
                width = self.late[0].shape[-1]
                self.ready.append([values.reshape((-1, width)) for values in self.late])
                self.late = None
        return outs

    def take(self):
        while not self.ready:
            self.tick()
        return self.ready.pop(0)


class Scatter:
    def __init__(self, orders):
        self.first, self.rest = orders
        self.bits = sorted(self.first + self.rest[0], reverse=True)
        self.queue, self.late, self.early, self.done = [], None, None, []

    def push(self, *pair):
        rows = pair[0].shape[0] >> len(self.bits)
        shape = (1, 1 << len(self.bits), rows, pair[0].shape[1])
        self.queue.append([values.reshape(shape) for values in pair])

    def run(self, jobs, after):
        plans, ins, shapes, bits = [], [], [], []
        for held, got, left, bit, joined in jobs:
            blocks, rows, width = held[0].shape[1:]
            members = sum(values.shape[0] for values in held)
            at = left.index(bit) if bit else 0
            behind = blocks // 2 >> at if bit else blocks
            plans.append((len(held), len(ins), bool(got), 1 << at, behind, bit, joined, len(shapes)))
            ins += held + (got or [])
            bits.append(bit or 1)
            if bit:
                groups = 1 if joined else members
                shapes += [((members // groups, blocks // 2, rows, width), jnp.bfloat16)] * (
                    2 * groups
                )
            else:
                shapes += [((rows, width), jnp.float32)] * members
        inputs = len(ins)

        def add(bit_ref, *refs):
            sources, outs = refs[:inputs], refs[len(refs) - len(shapes) :]
            for job, (arrays, at, come, before, behind, bit, joined, out_at) in enumerate(plans):
                mine = bit_ref[job]
                member = 0
                for array in range(arrays):
                    held = sources[at + array]
                    for row in range(held.shape[0]):

                        def total(start):
                            values = held[row, pl.ds(start, behind)]
                            if come:
                                other = sources[at + arrays + array][row, pl.ds(start, behind)]
                                values = values.astype(jnp.float32) + other.astype(jnp.float32)
                            return values

                        if bit is None:
                            outs[out_at + member][...] = total(0)[0]
                        else:
                            keep, send, place = (
                                (outs[out_at], outs[out_at + 1], member)
                                if joined
                                else (outs[out_at + 2 * member], outs[out_at + 2 * member + 1], 0)
                            )
                            for step in range(before):
                                start = 2 * step * behind
                                there = pl.ds(step * behind, behind)
                                keep[place, there] = lowered(total(start + mine * behind))
                                send[place, there] = lowered(total(start + (1 - mine) * behind))
                        member += 1

        return quick_call(
            add,
            "add_halves",
            [dp_bits(bits), *ins],
            after,
            [jax.ShapeDtypeStruct(shape, kind) for shape, kind in shapes],
        )

    def enter(self):
        if self.late is not None or not self.queue:
            return []
        pair = self.queue.pop(0)
        jobs = [
            ([values], None, self.bits, order[-1], False) for values, order in zip(pair, self.rest)
        ]
        outs = self.run(jobs, ())
        self.late = (outs[0::2], outs[1::2], 1)
        return outs

    def tick(self, *after):
        self.enter()
        jobs, steps = [], len(self.rest[0])
        if self.early is not None:
            keep, send, at = self.early
            bits = self.first[: len(self.first) - at + 1]
            left = sorted(bits[:-1], reverse=True)
            got = [pair_swap(send, "dp", bits[-1])]
            jobs.append(([keep], got, left, bits[-2] if left else None, True))
        if self.late is not None:
            keeps, sends, at = self.late
            got = [
                pair_swap(send, "dp", order[steps - at]) for send, order in zip(sends, self.rest)
            ]
            for keep, come, order in zip(keeps, got, self.rest):
                left = sorted(self.first + order[: steps - at], reverse=True)
                if at < steps:
                    jobs.append(([keep], [come], left, order[steps - at - 1], False))
            if at == steps:
                jobs.append((keeps, got, left, self.first[-1], True))
        if not jobs:
            return []
        outs = self.run(jobs, after)
        rest = outs
        if self.early is not None:
            if at_end(self.early[2], self.first):
                self.done.append(rest[:2])
                self.early = None
            else:
                self.early = (rest[0], rest[1], self.early[2] + 1)
            rest = rest[2:]
        if self.late is not None:
            if self.late[2] == steps:
                self.early, self.late = (rest[0], rest[1], 1), None
            else:
                self.late = (rest[0::2], rest[1::2], self.late[2] + 1)
        return outs

    def finish(self):
        while self.queue or self.late or self.early:
            self.tick()
        return self.done


def at_end(step, bits):
    return step == len(bits)


def total_sum(values):
    for axis in ("tensor", "dp"):
        bit = 1
        while bit < lax.axis_size(axis):
            values = values + pair_swap(values, axis, bit)
            bit *= 2
    return values


def gather_tokens(local):
    if lax.axis_size("tensor") != 2:
        return lax.all_gather(local, "tensor", axis=1, tiled=True)
    other = pair_swap(local, "tensor", 1)
    upper = lax.axis_index("tensor") != 0
    return jnp.concatenate([jnp.where(upper, other, local), jnp.where(upper, local, other)], axis=1)


def far_tokens(normed):
    part = PROMPT_DEV // lax.axis_size("tensor")
    place = lax.axis_index("tensor") * part
    return gather_tokens(pair_swap(lax.dynamic_slice_in_dim(normed, place, part, 1), "dp", 1))


def scatter_tokens(product, *values):
    if lax.axis_size("tensor") != 2:
        return lax.psum_scatter(
            lowered(product(*values)), "tensor", scatter_dimension=1, tiled=True
        ).astype(jnp.float32)
    count = values[0].shape[1] // 2
    place = lax.axis_index("tensor")
    theirs = [lax.dynamic_slice_in_dim(v, (1 - place) * count, count, 1) for v in values]
    got = pair_swap(lowered(product(*theirs)), "tensor", 1)
    mine = [lax.dynamic_slice_in_dim(v, place * count, count, 1) for v in values]
    return product(*mine) + got.astype(jnp.float32)


def feed_parts(values):
    if lax.axis_size("tensor") != 2:
        return [lax.all_gather(values, "tensor", axis=1, tiled=True)]
    return [values, pair_swap(values, "tensor", 1)]


def feed_total(parts):
    if lax.axis_size("tensor") != 2:
        return lax.psum_scatter(lowered(parts[0]), "tensor", scatter_dimension=1, tiled=True)
    got = pair_swap(lowered(parts[1]), "tensor", 1)
    return lowered(parts[0] + got.astype(jnp.float32))


def key_parts(tile):
    first = tile * TILE
    if first < PROMPT_DEV:
        return ([(0, first, "free")] if first else []) + [(first, TILE, "earlier")]
    return [(0, PROMPT_DEV, "free"), (PROMPT_DEV, first - PROMPT_DEV + TILE, "segment")]


def masked(scores, kind, first_key, first_query, start):
    if kind == "free":
        return scores
    key = lax.broadcasted_iota(jnp.int32, scores.shape, 0) + first_key
    query = lax.broadcasted_iota(jnp.int32, scores.shape, 1) + first_query
    allowed = key <= query
    if kind == "segment":
        allowed = allowed & (key >= start)
    return jnp.where(allowed, scores, NEGATIVE)


def spans(reference):
    tokens = reference.shape[1]
    return [(tile, slice(tile * TILE, tile * TILE + TILE)) for tile in range(tokens // TILE)]


def by_side(side_ref, reference, meets, skips):
    prompt = [at for tile, at in spans(reference) if tile * TILE < PROMPT_DEV]

    @pl.when(side_ref[0] == 0)
    def _():
        for at in prompt:
            skips(at)

    @pl.when(side_ref[0] != 0)
    def _():
        for at in prompt:
            meets(at)

    for tile, at in spans(reference):
        if at not in prompt:
            meets(at)


def own_forward(start_ref, q_ref, k_ref, v_ref, sum_ref, top_ref, total_ref):
    keys = k_ref[...].T
    for tile, at in spans(q_ref):
        query, start = q_ref[:, at], start_ref[:, at]
        parts = []
        for key, count, kind in key_parts(tile):
            scores = dot_nn(keys[key : key + count], query)
            scores = masked(scores, kind, key, tile * TILE, start)
            parts.append((scores, v_ref[:, key : key + count]))
        highest = jnp.max(parts[0][0], axis=0, keepdims=True)
        for scores, _ in parts[1:]:
            highest = jnp.maximum(highest, jnp.max(scores, axis=0, keepdims=True))
        total, mixed = 0.0, 0.0
        for scores, value in parts:
            weights = jnp.exp2(scores - highest)
            total = total + jnp.sum(weights, axis=0, keepdims=True)
            mixed = mixed + dot_nn(value, lowered(weights))
        sum_ref[:, at] = mixed
        top_ref[:, at] = highest
        total_ref[:, at] = total


def far_forward(
    side_ref, q_ref, k_ref, v_ref, sum_ref, top_ref, total_ref, out_ref, lse_ref
):
    keys = k_ref[...].T

    def meets(at):
        scores = dot_nn(keys, q_ref[:, at])
        highest = jnp.maximum(top_ref[:, at], jnp.max(scores, axis=0, keepdims=True))
        weights = jnp.exp2(scores - highest)
        scale = jnp.exp2(top_ref[:, at] - highest)
        total = total_ref[:, at] * scale + jnp.sum(weights, axis=0, keepdims=True)
        mixed = sum_ref[:, at] * scale + dot_nn(v_ref[...], lowered(weights))
        out_ref[:, at] = lowered(mixed / total)
        lse_ref[:, at] = highest + jnp.log2(total)

    def skips(at):
        out_ref[:, at] = lowered(sum_ref[:, at] / total_ref[:, at])
        lse_ref[:, at] = top_ref[:, at] + jnp.log2(total_ref[:, at])

    by_side(side_ref, q_ref, meets, skips)


def score_grads(scores, lse, d_shares, delta):
    shares = jnp.exp2(scores - lse)
    return lowered(shares), lowered(shares * (d_shares - delta))


def far_backward(
    side_ref, q_ref, k_ref, v_ref, out_ref, grad_ref, lse_ref, dq_ref, delta_ref, dkv_ref
):
    keys, values = k_ref[...].T, v_ref[...].T
    delta_ref[...] = jnp.sum(
        out_ref[...].astype(jnp.float32) * grad_ref[...].astype(jnp.float32), axis=0, keepdims=True
    )

    def terms(at):
        query, grad = q_ref[:, at], grad_ref[:, at]
        shares, d_scores = score_grads(
            dot_nn(keys, query), lse_ref[:, at], dot_nn(values, grad), delta_ref[:, at]
        )
        dq_ref[:, at] = dot_nn(k_ref[...], d_scores)
        return dot_nt(query, d_scores), dot_nt(grad, shares)

    def close(tiles):
        dk, dv = 0.0, 0.0
        for at in tiles:
            k_term, v_term = terms(at)
            dk, dv = dk + k_term, dv + v_term
        dkv_ref[0] = lowered(dk * LN_TWO)
        dkv_ref[1] = lowered(dv)

    tiles = [at for _, at in spans(q_ref)]
    conts = [at for tile, at in spans(q_ref) if tile * TILE >= PROMPT_DEV]

    @pl.when(side_ref[0] == 0)
    def _():
        for at in tiles:
            if at not in conts:
                dq_ref[:, at] = jnp.zeros_like(dq_ref[:, at])
        close(conts)

    @pl.when(side_ref[0] != 0)
    def _():
        close(tiles)


def own_backward(
    start_ref,
    gain_ref,
    q_ref,
    k_ref,
    v_ref,
    grad_ref,
    lse_ref,
    delta_ref,
    far_dq_ref,
    dq_ref,
    dk_ref,
    dv_ref,
    scale_ref,
    k_total,
    v_total,
):
    keys, values = k_ref[...].T, v_ref[...].T
    seen = set()
    scale = 0.0
    for tile, at in spans(q_ref):
        query, grad = q_ref[:, at], grad_ref[:, at]
        dq = far_dq_ref[:, at]
        for key, count, kind in key_parts(tile):
            scores = dot_nn(keys[key : key + count], query)
            scores = masked(scores, kind, key, tile * TILE, start_ref[:, at])
            shares, d_scores = score_grads(
                scores, lse_ref[:, at], dot_nn(values[key : key + count], grad), delta_ref[:, at]
            )
            dv = dot_nt(grad, shares)
            dk = dot_nt(query, d_scores)
            dq = dq + dot_nn(k_ref[:, key : key + count], d_scores)
            for offset in range(0, count, TILE):
                there = slice(key + offset, key + offset + TILE)
                here = slice(offset, offset + TILE)
                if key + offset in seen:
                    k_total[:, there] += dk[:, here]
                    v_total[:, there] += dv[:, here]
                else:
                    seen.add(key + offset)
                    k_total[:, there] = dk[:, here]
                    v_total[:, there] = dv[:, here]
        dq_ref[:, at] = lowered(dq * gain_ref[...])
        scale = scale + jnp.sum(dq * query.astype(jnp.float32), axis=1, keepdims=True)
    dk_ref[...] = lowered(k_total[...] * LN_TWO)
    dv_ref[...] = lowered(v_total[...])
    scale_ref[...] = scale


def rows_block(count):
    return pl.BlockSpec((HD, count), lambda head: (head, 0))


def flat_block(count):
    return pl.BlockSpec((None, 1, count), lambda head: (head, 0, 0))


def same_block(*shape):
    return pl.BlockSpec(shape, lambda head: (0, 0))


def per_head(kernel, name, heads, area, products, ins, outs, after=(), scratch=()):
    flops = 2 * 256 * area * heads * products
    moved = sum(array.size * array.dtype.itemsize for _, array in ins)
    count = len(ins)

    def work(*refs):
        kernel(*refs[:count], *refs[count + len(after) :])

    return pl.pallas_call(
        work,
        grid=(heads,),
        in_specs=[spec for spec, _ in ins] + [UNREAD] * len(after),
        out_specs=[spec for spec, _, _ in outs],
        out_shape=[jax.ShapeDtypeStruct(shape, kind) for _, shape, kind in outs],
        scratch_shapes=list(scratch),
        compiler_params=pltpu.CompilerParams(vmem_limit_bytes=32 << 20),
        cost_estimate=pl.CostEstimate(
            flops=flops, bytes_accessed=moved, transcendentals=area * heads
        ),
        name=name,
    )(*[array for _, array in ins], *after)


def attention_own(start, queries, keys, values, after):
    width, tokens = queries.shape
    heads = width // HD
    all_rows, flat = rows_block(tokens), flat_block(tokens)
    return per_head(
        own_forward,
        "attention_own",
        heads,
        tokens * tokens * 5 // 8,
        3,
        [
            (same_block(1, tokens), start),
            (all_rows, queries),
            (all_rows, keys),
            (all_rows, values),
        ],
        [
            (all_rows, (width, tokens), jnp.float32),
            (flat, (heads, 1, tokens), jnp.float32),
            (flat, (heads, 1, tokens), jnp.float32),
        ],
        after,
    )


def attention_far(side, queries, keys, values, partial_sum, top, total, after):
    width, tokens = queries.shape
    heads = width // HD
    all_rows, flat, far_rows = rows_block(tokens), flat_block(tokens), rows_block(PROMPT_DEV)
    return per_head(
        far_forward,
        "attention_far",
        heads,
        tokens * PROMPT_DEV,
        3,
        [
            (SCALAR, side),
            (all_rows, queries),
            (far_rows, keys),
            (far_rows, values),
            (all_rows, partial_sum),
            (flat, top),
            (flat, total),
        ],
        [
            (all_rows, (width, tokens), jnp.bfloat16),
            (flat, (heads, 1, tokens), jnp.float32),
        ],
        after,
    )


def attention_far_back(side, queries, keys, values, mixed, grads, lse, after):
    width, tokens = queries.shape
    heads = width // HD
    all_rows, flat, far_rows = rows_block(tokens), flat_block(tokens), rows_block(PROMPT_DEV)
    return per_head(
        far_backward,
        "attention_far_back",
        heads,
        tokens * PROMPT_DEV,
        6,
        [
            (SCALAR, side),
            (all_rows, queries),
            (far_rows, keys),
            (far_rows, values),
            (all_rows, mixed),
            (all_rows, grads),
            (flat, lse),
        ],
        [
            (all_rows, (width, tokens), jnp.float32),
            (flat, (heads, 1, tokens), jnp.float32),
            (
                pl.BlockSpec((2, HD, PROMPT_DEV), lambda head: (0, head, 0)),
                (2, width, PROMPT_DEV),
                jnp.bfloat16,
            ),
        ],
        after,
    )


def attention_own_back(start, gain, queries, keys, values, grads, lse, delta, far_dq, after):
    width, tokens = queries.shape
    heads = width // HD
    all_rows, flat = rows_block(tokens), flat_block(tokens)
    return per_head(
        own_backward,
        "attention_own_back",
        heads,
        tokens * tokens * 5 // 8,
        6,
        [
            (same_block(1, tokens), start),
            (same_block(HD, 1), gain),
            (all_rows, queries),
            (all_rows, keys),
            (all_rows, values),
            (all_rows, grads),
            (flat, lse),
            (flat, delta),
            (all_rows, far_dq),
        ],
        [
            (all_rows, (width, tokens), jnp.bfloat16),
            (all_rows, (width, tokens), jnp.bfloat16),
            (all_rows, (width, tokens), jnp.bfloat16),
            (pl.BlockSpec((HD, 1), lambda head: (head, 0)), (width, 1), jnp.float32),
        ],
        after,
        [pltpu.VMEM((HD, tokens), jnp.float32)] * 2,
    )


def segment_starts(lengths_row, tokens):
    place = jnp.arange(tokens, dtype=jnp.int32) - PROMPT_DEV
    bounds = jnp.cumsum(lengths_row)
    passed = jnp.where(place[:, None] >= bounds[None, :], bounds[None, :], 0)
    return (PROMPT_DEV + jnp.max(passed, axis=1))[None, :]


def body(
    inputs,
    cotangent,
    query_weight,
    key_weight,
    value_weight,
    output_weight,
    up_weight,
    down_weight,
    attention_gain,
    feed_gain,
    query_scale,
    cont_lengths,
):
    tokens = inputs.shape[0] * lax.axis_size("tensor")
    heads = query_weight.shape[2] // HD
    orders = exchange_orders(lax.axis_size("dp"))
    side = (lax.axis_index("dp") % 2).astype(jnp.int32)[None]
    start = segment_starts(cont_lengths[0], tokens)

    pairs = []
    for layer in range(LAYERS):
        pairs.append((key_weight[layer], value_weight[layer]))
        pairs.append((query_weight[layer], output_weight[layer].T))
        pairs.append((up_weight[layer], down_weight[layer].T))

    gather = Gather(pairs, orders)
    stored = []
    current = inputs.T
    for layer in range(LAYERS):
        attn_gain = attention_gain[layer][:, None]
        ff_gain = feed_gain[layer][:, None]
        inverse_attn = inverse_root(current)
        normed = gather_tokens(lowered(current * inverse_attn * attn_gain))
        far_normed = far_tokens(normed)
        wk, wv = gather.take()
        keys = lowered(dot_tn(wk, normed))
        values = lowered(dot_tn(wv, normed))
        gather.tick(keys, values)
        far_keys = lowered(dot_tn(wk, far_normed))
        far_values = lowered(dot_tn(wv, far_normed))
        gather.tick(far_keys, far_values)
        wq, wo = gather.take()
        gain_q = softplus(query_scale[layer]) * LOG_TWO_E / math.sqrt(HD)
        gain_rows = jnp.tile(gain_q, heads)[:, None]
        queries = lowered(dot_tn(wq, normed) * (gain_rows * LOG_TWO_E))
        own_sum, top, total = attention_own(start, queries, keys, values, ())
        ready = gather.tick(top)
        mixed, lse = attention_far(side, queries, far_keys, far_values, own_sum, top, total, ready)
        middle = current + scatter_tokens(lambda rows: dot_nn(wo, rows), mixed)
        gather.tick(middle)
        wu, wd = gather.take()
        inverse_feed = inverse_root(middle)
        feed = lowered(middle * inverse_feed * ff_gain)
        ups, downs = feed_parts(wu), feed_parts(wd)
        uppers = [dot_tn(w, feed) for w in ups]
        gather.tick(*uppers)
        hiddens = [lowered(upper * jax.nn.sigmoid(upper)) for upper in uppers]
        stored.append(
            (
                (current, inverse_attn, attn_gain, normed),
                (gain_q, queries, keys, values, far_keys, far_values, mixed, lse),
                (middle, inverse_feed, ff_gain, feed, uppers, hiddens),
                (wk, wv, wq, wo, ups, downs),
            )
        )
        current = middle + sum(dot_nn(w, hidden) for w, hidden in zip(downs, hiddens))
        gather.tick(current)

    sums = Scatter(orders)
    small_grads = [None] * LAYERS
    grad = cotangent.T
    for layer in reversed(range(LAYERS)):
        (
            (source, inverse_attn, attn_gain, normed),
            (gain_q, queries, keys, values, far_keys, far_values, mixed, lse),
            (middle, inverse_feed, ff_gain, feed, uppers, hiddens),
            (wk, wv, wq, wo, ups, downs),
        ) = stored[layer]
        grad_low = lowered(grad)
        d_uppers = []
        for w, upper in zip(downs, uppers):
            d_hidden = lowered(dot_tn(w, grad_low)).astype(jnp.float32)
            sigmoid = jax.nn.sigmoid(upper)
            d_uppers.append(lowered(d_hidden * (sigmoid * (1.0 + upper * (1.0 - sigmoid)))))
        d_feed = sum(dot_nn(w, d_upper) for w, d_upper in zip(ups, d_uppers))
        feed_gain_grad, part = norm_backward(middle, inverse_feed, ff_gain, d_feed)
        grad_middle = grad + part
        sums.tick(grad_middle)
        down_grad = feed_total([dot_nt(grad_low, hidden) for hidden in hiddens])
        up_grad = feed_total([dot_nt(feed, d_upper) for d_upper in d_uppers])
        sums.tick(down_grad, up_grad)
        sums.push(down_grad, up_grad)
        middle_low = gather_tokens(lowered(grad_middle))
        d_mixed = lowered(dot_tn(wo, middle_low))
        out_grad = lowered(dot_nt(middle_low, mixed))
        ready = sums.enter()
        far_dq, delta, far_dkv = attention_far_back(
            side, queries, far_keys, far_values, mixed, d_mixed, lse, ready
        )
        back = pair_swap(far_dkv, "dp", 1).astype(jnp.float32)
        ready = sums.tick(delta, out_grad)
        d_raw, own_dk, own_dv, scale_rows = attention_own_back(
            start,
            gain_q[:, None],
            queries,
            keys,
            values,
            d_mixed,
            lse,
            delta,
            far_dq,
            ready,
        )
        sums.tick(scale_rows)
        query_grad = lowered(dot_nt(normed, d_raw))
        sums.push(out_grad, query_grad)
        sums.enter()
        pad = ((0, 0), (0, tokens - PROMPT_DEV))
        d_keys = lowered(own_dk.astype(jnp.float32) + jnp.pad(back[0], pad))
        d_values = lowered(own_dv.astype(jnp.float32) + jnp.pad(back[1], pad))
        scale_raw = jnp.sum(scale_rows.reshape(heads, HD), 0) / (gain_q * LOG_TWO_E)
        scale_grad = scale_raw * jax.nn.sigmoid(query_scale[layer]) * LOG_TWO_E / math.sqrt(HD)
        d_normed = scatter_tokens(
            lambda dq, dk, dv: dot_nn(wq, dq) + dot_nn(wk, dk) + dot_nn(wv, dv),
            d_raw,
            d_keys,
            d_values,
        )
        sums.tick(d_normed)
        key_grad = lowered(dot_nt(normed, d_keys))
        value_grad = lowered(dot_nt(normed, d_values))
        sums.push(key_grad, value_grad)
        attn_gain_grad, part = norm_backward(source, inverse_attn, attn_gain, d_normed)
        grad = grad_middle + part
        sums.tick(grad)
        small_grads[layer] = jnp.concatenate([attn_gain_grad, feed_gain_grad, scale_grad])
    done = sums.finish()
    layer_grads = []
    for layer in range(LAYERS):
        at = 3 * (LAYERS - 1 - layer)
        (down_grad, up_grad), (out_grad, query_grad), (key_grad, value_grad) = done[at : at + 3]
        layer_grads.append(
            (query_grad, key_grad, value_grad, out_grad.T, up_grad, down_grad.T)
        )

    summed = [jnp.stack(members) for members in zip(*layer_grads)]
    small = total_sum(jnp.stack(small_grads))
    width = current.shape[0]
    return (
        current.T,
        grad.T,
        *summed,
        small[:, :width],
        small[:, width : 2 * width],
        small[:, 2 * width :],
    )


def solution(mesh):
    in_specs = (
        P(("dp", "tensor"), None),
        P(("dp", "tensor"), None),
        P(None, "dp", "tensor"),
        P(None, "dp", "tensor"),
        P(None, "dp", "tensor"),
        P(None, "tensor", "dp"),
        P(None, "dp", "tensor"),
        P(None, "tensor", "dp"),
        P(),
        P(),
        P(),
        P("dp", None),
    )
    out_specs = (
        P(("dp", "tensor"), None),
        P(("dp", "tensor"), None),
        P(None, "dp", "tensor"),
        P(None, "dp", "tensor"),
        P(None, "dp", "tensor"),
        P(None, "tensor", "dp"),
        P(None, "dp", "tensor"),
        P(None, "tensor", "dp"),
        P(),
        P(),
        P(),
    )
    return jax.shard_map(body, mesh=mesh, in_specs=in_specs, out_specs=out_specs, check_vma=False)
```

```python
from functools import partial
import math

import jax
import jax.numpy as jnp
from jax import lax
from jax.experimental import pallas as pl
from jax.experimental.pallas import tpu as pltpu
from jax.sharding import PartitionSpec as P

HD = 80
LAYERS = 2
PROMPT_DEV = 512
TILE = 256

EPSILON = 1e-06
LOG_TWO_E = 1.4426950408889634
LN_TWO = 0.6931471805599453
NEGATIVE = -1e30


def lowered(values):
    return values.astype(jnp.bfloat16)


def dot_nn(former, latter):
    return jnp.dot(former, latter, preferred_element_type=jnp.float32)


def dot_tn(former, latter):
    return lax.dot_general(
        former, latter, (((0,), (0,)), ((), ())), preferred_element_type=jnp.float32
    )


def dot_nt(former, latter):
    return lax.dot_general(
        former, latter, (((1,), (1,)), ((), ())), preferred_element_type=jnp.float32
    )


def softplus(values):
    return jnp.log1p(jnp.exp(values))


def pair_swap(values, axis, bit):
    size = lax.axis_size(axis)
    return lax.ppermute(values, axis, [(i, i ^ bit) for i in range(size)])


def exchange_orders(size):
    if size == 16:
        return (8, 4), ((2, 1), (1, 2))
    bits = tuple(1 << k for k in reversed(range(size.bit_length() - 1)))
    first, rest = bits[:1], bits[1:]
    half = len(rest) // 2
    return first, (rest, rest[half:] + rest[:half])


WHOLE = pl.BlockSpec(memory_space=pltpu.VMEM)
SCALAR = pl.BlockSpec(memory_space=pltpu.SMEM)
UNREAD = pl.BlockSpec(memory_space=pl.ANY)


def dp_bits(bits):
    place = lax.axis_index("dp")
    return jnp.stack([((place & bit) != 0).astype(jnp.int32) for bit in bits])


def quick_call(kernel, name, arrays, after, out_shape):
    out = pl.pallas_call(
        kernel,
        in_specs=[SCALAR] + [WHOLE] * (len(arrays) - 1) + [UNREAD] * len(after),
        out_specs=[WHOLE] * len(out_shape),
        out_shape=out_shape,
        compiler_params=pltpu.CompilerParams(vmem_limit_bytes=48 << 20),
        cost_estimate=pl.CostEstimate(flops=1, bytes_accessed=1, transcendentals=0),
        name=name,
    )(*arrays, *after)
    return list(out)


class Gather:
    def __init__(self, pairs, orders):
        self.first, self.rest = orders
        self.queue = [jnp.stack(pair)[:, None] for pair in pairs]
        self.left = len(pairs)
        self.early, self.early_at = None, 0
        self.late, self.late_at = None, 0
        self.ready = []

    def tick(self, *after):
        if self.early is None and self.queue:
            self.early, self.early_at = self.queue.pop(0), 0
        if self.late is None and self.early is not None and self.early_at == len(self.first):
            self.late, self.late_at = self.early, 0
            self.early, self.early_at = (self.queue.pop(0), 0) if self.queue else (None, 0)
        jobs = []
        early = self.early is not None and self.early_at < len(self.first)
        if early:
            jobs.append((self.early, self.first[: self.early_at + 1]))
        if self.late is not None:
            for values, order in zip(self.late, self.rest):
                jobs.append((values, self.first + order[: self.late_at + 1]))
        if not jobs:
            return []
        got = [pair_swap(values, "dp", done[-1]) for values, done in jobs]
        plans, shapes = [], []
        for values, done in jobs:
            members, blocks, rows, width = values.shape
            before = 1 << sum(1 for bit in done[:-1] if bit > done[-1])
            parts = members if members > 1 and len(done) == len(self.first) else 1
            plans.append((members, before, blocks // before, parts, len(shapes)))
            shapes += [(members // parts, 2 * blocks, rows, width)] * parts
        count = len(jobs)
        merged = self.late is not None and self.merges() and (
            self.late_at + 1 == len(self.rest[0])
        )
        if merged:
            at = plans[-2][-1]
            shapes[at:] = [(2,) + shapes[at][1:]]
        following = self.queue[:1]

        def join(bit_ref, *refs):
            outs = refs[len(refs) - len(shapes) - len(following) :]
            if following:
                outs[-1][...] = refs[2 * count][...]
            for job, (members, before, blocks, parts, at) in enumerate(plans):
                bit = bit_ref[job]
                for member in range(members):
                    if merged and job == count - 1:
                        out, row = outs[at - 1], 1
                    elif parts > 1:
                        out, row = outs[at + member], 0
                    else:
                        out, row = outs[at], member
                    for step in range(before):
                        here = pl.ds(step * blocks, blocks)
                        place = 2 * step * blocks
                        ours, theirs = place + bit * blocks, place + (1 - bit) * blocks
                        out[row, pl.ds(ours, blocks)] = refs[job][member, here]
                        out[row, pl.ds(theirs, blocks)] = refs[count + job][member, here]

        outs = quick_call(
            join,
            "join_halves",
            [
                dp_bits([done[-1] for _, done in jobs]),
                *[values for values, _ in jobs],
                *got,
                *following,
            ],
            after,
            [
                jax.ShapeDtypeStruct(shape, jnp.bfloat16)
                for shape in shapes + [values.shape for values in following]
            ],
        )
        if following:
            self.queue[0] = outs.pop()
        if early:
            self.early_at += 1
            done = self.early_at == len(self.first)
            self.early = outs[:2] if done else outs[0]
        if self.late is not None:
            self.late, self.late_at = outs[-1:] if merged else outs[-2:], self.late_at + 1
            if self.late_at == len(self.rest[0]):
                width = self.late[0].shape[-1]
                shape = (2, -1, width) if merged else (-1, width)
                self.ready.append([values.reshape(shape) for values in self.late])
                self.late = None
                self.left -= 1
        return outs

    def merges(self):
        return self.left % 3 == 1

    def take(self):
        while not self.ready:
            self.tick()
        return self.ready.pop(0)


class Scatter:
    def __init__(self, orders):
        self.first, self.rest = orders
        self.bits = sorted(self.first + self.rest[0], reverse=True)
        self.queue, self.late, self.early, self.done = [], None, None, []

    def push(self, *pair, came=(None, None)):
        rows = pair[0].shape[0] >> len(self.bits)
        shape = (1, 1 << len(self.bits), rows, pair[0].shape[1])
        self.queue.append(
            [
                ([values.reshape(shape)], None if more is None else [more.reshape(shape)], order)
                for values, more, order in zip(pair, came, self.rest)
            ]
        )

    def run(self, jobs, after):
        plans, ins, shapes, bits = [], [], [], []
        for held, got, left, bit, joined in jobs:
            blocks, rows, width = held[0].shape[1:]
            members = sum(values.shape[0] for values in held)
            at = left.index(bit) if bit else 0
            behind = blocks // 2 >> at if bit else blocks
            plans.append((len(held), len(ins), bool(got), 1 << at, behind, bit, joined, len(shapes)))
            ins += held + (got or [])
            bits.append(bit or 1)
            if bit:
                groups = 1 if joined else members
                shapes += [((members // groups, blocks // 2, rows, width), jnp.bfloat16)] * (
                    2 * groups
                )
            else:
                shapes += [((rows, width), jnp.float32)] * members
        inputs = len(ins)

        def add(bit_ref, *refs):
            sources, outs = refs[:inputs], refs[len(refs) - len(shapes) :]
            for job, (arrays, at, come, before, behind, bit, joined, out_at) in enumerate(plans):
                mine = bit_ref[job]
                member = 0
                for array in range(arrays):
                    held = sources[at + array]
                    for row in range(held.shape[0]):

                        def total(start):
                            values = held[row, pl.ds(start, behind)]
                            if come:
                                other = sources[at + arrays + array][row, pl.ds(start, behind)]
                                values = values.astype(jnp.float32) + other.astype(jnp.float32)
                            return values

                        if bit is None:
                            outs[out_at + member][...] = total(0)[0]
                        else:
                            keep, send, place = (
                                (outs[out_at], outs[out_at + 1], member)
                                if joined
                                else (outs[out_at + 2 * member], outs[out_at + 2 * member + 1], 0)
                            )
                            for step in range(before):
                                start = 2 * step * behind
                                there = pl.ds(step * behind, behind)
                                keep[place, there] = lowered(total(start + mine * behind))
                                send[place, there] = lowered(total(start + (1 - mine) * behind))
                        member += 1

        return quick_call(
            add,
            "add_halves",
            [dp_bits(bits), *ins],
            after,
            [jax.ShapeDtypeStruct(shape, kind) for shape, kind in shapes],
        )

    def enter(self):
        if self.late is not None or not self.queue:
            return []
        jobs = [
            (held, came, self.bits, order[-1], False) for held, came, order in self.queue.pop(0)
        ]
        outs = self.run(jobs, ())
        self.late = (outs[0::2], outs[1::2], 1)
        return outs

    def tick(self, *after):
        self.enter()
        jobs, steps = [], len(self.rest[0])
        if self.early is not None:
            keep, send, at = self.early
            bits = self.first[: len(self.first) - at + 1]
            left = sorted(bits[:-1], reverse=True)
            got = [pair_swap(send, "dp", bits[-1])]
            jobs.append(([keep], got, left, bits[-2] if left else None, True))
        if self.late is not None:
            keeps, sends, at = self.late
            got = [
                pair_swap(send, "dp", order[steps - at]) for send, order in zip(sends, self.rest)
            ]
            for keep, come, order in zip(keeps, got, self.rest):
                left = sorted(self.first + order[: steps - at], reverse=True)
                if at < steps:
                    jobs.append(([keep], [come], left, order[steps - at - 1], False))
            if at == steps:
                jobs.append((keeps, got, left, self.first[-1], True))
        if not jobs:
            return []
        outs = self.run(jobs, after)
        rest = outs
        if self.early is not None:
            if at_end(self.early[2], self.first):
                self.done.append(rest[:2])
                self.early = None
            else:
                self.early = (rest[0], rest[1], self.early[2] + 1)
            rest = rest[2:]
        if self.late is not None:
            if self.late[2] == steps:
                self.early, self.late = (rest[0], rest[1], 1), None
            else:
                self.late = (rest[0::2], rest[1::2], self.late[2] + 1)
        return outs

    def finish(self):
        while self.queue or self.late or self.early:
            self.tick()
        return self.done


def at_end(step, bits):
    return step == len(bits)


def gather_tokens(local):
    if lax.axis_size("tensor") != 2:
        values = lax.all_gather(local, "tensor", axis=1, tiled=True)
        return values, values
    other = pair_swap(local, "tensor", 1)
    upper = lax.axis_index("tensor") != 0
    values = [jnp.where(upper, other, local), jnp.where(upper, local, other)]
    return jnp.concatenate(values, axis=1), other


def far_part(normed):
    part = PROMPT_DEV // lax.axis_size("tensor")
    place = lax.axis_index("tensor") * part
    return pair_swap(lax.dynamic_slice_in_dim(normed, place, part, 1), "dp", 1)


def scatter_tokens(product, *values):
    if lax.axis_size("tensor") != 2:
        return [
            lax.psum_scatter(
                lowered(product(*values)), "tensor", scatter_dimension=1, tiled=True
            )
        ]
    count = values[0].shape[1] // 2
    place = lax.axis_index("tensor")
    theirs = [lax.dynamic_slice_in_dim(v, (1 - place) * count, count, 1) for v in values]
    got = pair_swap(lowered(product(*theirs)), "tensor", 1)
    mine = [lax.dynamic_slice_in_dim(v, place * count, count, 1) for v in values]
    return [lowered(product(*mine)), got]


def feed_parts(both):
    if lax.axis_size("tensor") != 2:
        whole = lax.all_gather(both, "tensor", axis=2, tiled=True)
        return [whole[0]], [whole[1]]
    other = pair_swap(both, "tensor", 1)
    return [both[0], other[0]], [both[1], other[1]]


def feed_total(parts):
    if lax.axis_size("tensor") != 2:
        whole = lax.psum_scatter(lowered(parts[0]), "tensor", scatter_dimension=1, tiled=True)
        return whole, None
    return lowered(parts[0]), pair_swap(lowered(parts[1]), "tensor", 1)


def tied(gain, after):
    if not after:
        return gain
    corner = after[0][(0,) * after[0].ndim].astype(jnp.float32)
    return gain + jnp.minimum((corner > 3e38).astype(jnp.int32), 0).astype(jnp.float32)


def norm(terms, gain, after=()):
    total = sum(term.astype(jnp.float32) for term in terms)
    inverse = lax.rsqrt(jnp.mean(total * total, axis=0, keepdims=True) + EPSILON)
    return total, inverse, lowered(total * inverse * tied(gain, after))


def norm_back(source, inverse, gain, grad, terms, after=()):
    incoming = sum(term.astype(jnp.float32) for term in terms)
    unit = source * inverse
    gain_grad = jnp.sum(incoming * unit, axis=1)
    scaled = incoming * tied(gain, after)
    total = grad + inverse * (scaled - unit * jnp.mean(scaled * unit, axis=0, keepdims=True))
    return total, lowered(total), gain_grad


def first_slot(_):
    return jnp.zeros((1,), jnp.int32)


def add_back(own_keys, own_values, back, after):
    def kernel(_, keys_ref, values_ref, back_ref, *refs):
        for place, (ref, out) in enumerate(zip((keys_ref, values_ref), refs[-2:])):
            prompt = ref[:, :PROMPT_DEV].astype(jnp.float32) + back_ref[place].astype(jnp.float32)
            out[:, :PROMPT_DEV] = lowered(prompt)
            out[:, PROMPT_DEV:] = ref[:, PROMPT_DEV:]

    out = [jax.ShapeDtypeStruct(own_keys.shape, jnp.bfloat16)] * 2
    arrays = [first_slot(back), own_keys, own_values, back]
    return quick_call(kernel, "add_back", arrays, after, out)


def key_parts(tile):
    first = tile * TILE
    if first < PROMPT_DEV:
        return ([(0, first, "free")] if first else []) + [(first, TILE, "earlier")]
    return [(0, PROMPT_DEV, "free"), (PROMPT_DEV, first - PROMPT_DEV + TILE, "segment")]


def masked(scores, kind, first_key, first_query, start):
    if kind == "free":
        return scores
    key = lax.broadcasted_iota(jnp.int32, scores.shape, 0) + first_key
    query = lax.broadcasted_iota(jnp.int32, scores.shape, 1) + first_query
    allowed = key <= query
    if kind == "segment":
        allowed = allowed & (key >= start)
    return jnp.where(allowed, scores, NEGATIVE)


def spans(reference):
    tokens = reference.shape[1]
    return [(tile, slice(tile * TILE, tile * TILE + TILE)) for tile in range(tokens // TILE)]


def ahead(items, first, second):
    items = list(items)
    held = first(items[0])
    for place, item in enumerate(items):
        following = first(items[place + 1]) if place + 1 < len(items) else None
        second(item, held)
        held = following


def own_forward(start_ref, q_ref, k_ref, v_ref, sum_ref, top_ref, total_ref):
    keys = k_ref[...].T

    def scores_of(item):
        tile, at = item
        query, start = q_ref[:, at], start_ref[:, at]
        return [
            masked(dot_nn(keys[key : key + count], query), kind, key, tile * TILE, start)
            for key, count, kind in key_parts(tile)
        ]

    def mix(item, parts):
        tile, at = item
        highest = jnp.max(parts[0], axis=0, keepdims=True)
        for scores in parts[1:]:
            highest = jnp.maximum(highest, jnp.max(scores, axis=0, keepdims=True))
        total, mixed = 0.0, 0.0
        for scores, (key, count, _) in zip(parts, key_parts(tile)):
            weights = jnp.exp2(scores - highest)
            total = total + jnp.sum(weights, axis=0, keepdims=True)
            mixed = mixed + dot_nn(v_ref[:, key : key + count], lowered(weights))
        sum_ref[:, at] = mixed
        top_ref[:, at] = highest
        total_ref[:, at] = total

    ahead(spans(q_ref), scores_of, mix)


def far_forward(
    side_ref, q_ref, k_ref, v_ref, sum_ref, top_ref, total_ref, out_ref, lse_ref
):
    keys = k_ref[...].T

    def scores_of(at):
        return dot_nn(keys, q_ref[:, at])

    def mix(at, scores):
        highest = jnp.maximum(top_ref[:, at], jnp.max(scores, axis=0, keepdims=True))
        weights = jnp.exp2(scores - highest)
        scale = jnp.exp2(top_ref[:, at] - highest)
        total = total_ref[:, at] * scale + jnp.sum(weights, axis=0, keepdims=True)
        mixed = sum_ref[:, at] * scale + dot_nn(v_ref[...], lowered(weights))
        out_ref[:, at] = lowered(mixed / total)
        lse_ref[:, at] = highest + jnp.log2(total)

    tiles = [at for _, at in spans(q_ref)]
    conts = [at for tile, at in spans(q_ref) if tile * TILE >= PROMPT_DEV]

    @pl.when(side_ref[0] == 0)
    def _():
        for at in tiles:
            if at not in conts:
                out_ref[:, at] = lowered(sum_ref[:, at] / total_ref[:, at])
                lse_ref[:, at] = top_ref[:, at] + jnp.log2(total_ref[:, at])
        ahead(conts, scores_of, mix)

    @pl.when(side_ref[0] != 0)
    def _():
        ahead(tiles, scores_of, mix)


def score_grads(scores, lse, d_shares, delta):
    shares = jnp.exp2(scores - lse)
    return lowered(shares), lowered(shares * (d_shares - delta))


def far_backward(
    side_ref, q_ref, k_ref, v_ref, out_ref, grad_ref, lse_ref, dq_ref, delta_ref, dkv_ref
):
    keys, values = k_ref[...].T, v_ref[...].T
    delta_ref[...] = jnp.sum(
        out_ref[...].astype(jnp.float32) * grad_ref[...].astype(jnp.float32), axis=0, keepdims=True
    )

    def begin(at):
        return dot_nn(keys, q_ref[:, at]), dot_nn(values, grad_ref[:, at])

    def close(tiles):
        sums = [0.0, 0.0]

        def terms(at, held):
            scores, d_shares = held
            shares, d_scores = score_grads(scores, lse_ref[:, at], d_shares, delta_ref[:, at])
            dq_ref[:, at] = dot_nn(k_ref[...], d_scores)
            sums[0] = sums[0] + dot_nt(q_ref[:, at], d_scores)
            sums[1] = sums[1] + dot_nt(grad_ref[:, at], shares)

        ahead(tiles, begin, terms)
        dkv_ref[0] = lowered(sums[0] * LN_TWO)
        dkv_ref[1] = lowered(sums[1])

    tiles = [at for _, at in spans(q_ref)]
    conts = [at for tile, at in spans(q_ref) if tile * TILE >= PROMPT_DEV]

    @pl.when(side_ref[0] == 0)
    def _():
        for at in tiles:
            if at not in conts:
                dq_ref[:, at] = jnp.zeros_like(dq_ref[:, at])
        close(conts)

    @pl.when(side_ref[0] != 0)
    def _():
        close(tiles)


def own_backward(
    start_ref,
    gain_ref,
    q_ref,
    k_ref,
    v_ref,
    grad_ref,
    lse_ref,
    delta_ref,
    far_dq_ref,
    dq_ref,
    dk_ref,
    dv_ref,
    scale_ref,
    k_total,
    v_total,
):
    keys, values = k_ref[...].T, v_ref[...].T
    seen, dqs, scales = set(), {}, [0.0]

    def begin(item):
        (tile, at), (key, count, kind), _ = item
        scores = dot_nn(keys[key : key + count], q_ref[:, at])
        scores = masked(scores, kind, key, tile * TILE, start_ref[:, at])
        return scores, dot_nn(values[key : key + count], grad_ref[:, at])

    def terms(item, held):
        (tile, at), (key, count, _), last = item
        scores, d_shares = held
        query, grad = q_ref[:, at], grad_ref[:, at]
        shares, d_scores = score_grads(scores, lse_ref[:, at], d_shares, delta_ref[:, at])
        dv = dot_nt(grad, shares)
        dk = dot_nt(query, d_scores)
        dq = dqs.get(tile, far_dq_ref[:, at]) + dot_nn(k_ref[:, key : key + count], d_scores)
        dqs[tile] = dq
        for offset in range(0, count, TILE):
            there = slice(key + offset, key + offset + TILE)
            here = slice(offset, offset + TILE)
            if key + offset in seen:
                k_total[:, there] += dk[:, here]
                v_total[:, there] += dv[:, here]
            else:
                seen.add(key + offset)
                k_total[:, there] = dk[:, here]
                v_total[:, there] = dv[:, here]
        if last:
            dq_ref[:, at] = lowered(dq * gain_ref[...])
            product = jnp.sum(dq * query.astype(jnp.float32), axis=1, keepdims=True)
            scales[0] = scales[0] + product

    items = []
    for tile, at in spans(q_ref):
        parts = key_parts(tile)
        items += [((tile, at), part, part is parts[-1]) for part in parts]
    ahead(items, begin, terms)
    dk_ref[...] = lowered(k_total[...] * LN_TWO)
    dv_ref[...] = lowered(v_total[...])
    scale_ref[...] = scales[0]


def rows_block(count):
    return pl.BlockSpec((HD, count), lambda head: (head, 0))


def flat_block(count):
    return pl.BlockSpec((None, 1, count), lambda head: (head, 0, 0))


def same_block(*shape):
    return pl.BlockSpec(shape, lambda head: (0, 0))


def per_head(kernel, name, heads, area, products, ins, outs, after=(), scratch=()):
    flops = 40 * area * heads * products
    moved = sum(array.size * array.dtype.itemsize for _, array in ins)
    count = len(ins)

    def work(*refs):
        kernel(*refs[:count], *refs[count + len(after) :])

    return pl.pallas_call(
        work,
        grid=(heads,),
        in_specs=[spec for spec, _ in ins] + [UNREAD] * len(after),
        out_specs=[spec for spec, _, _ in outs],
        out_shape=[jax.ShapeDtypeStruct(shape, kind) for _, shape, kind in outs],
        scratch_shapes=list(scratch),
        compiler_params=pltpu.CompilerParams(vmem_limit_bytes=32 << 20),
        cost_estimate=pl.CostEstimate(
            flops=flops, bytes_accessed=moved, transcendentals=area * heads
        ),
        name=name,
    )(*[array for _, array in ins], *after)


def attention_own(start, queries, keys, values, after):
    width, tokens = queries.shape
    heads = width // HD
    all_rows, flat = rows_block(tokens), flat_block(tokens)
    return per_head(
        own_forward,
        "attention_own",
        heads,
        tokens * tokens * 5 // 8,
        3,
        [
            (same_block(1, tokens), start),
            (all_rows, queries),
            (all_rows, keys),
            (all_rows, values),
        ],
        [
            (all_rows, (width, tokens), jnp.float32),
            (flat, (heads, 1, tokens), jnp.float32),
            (flat, (heads, 1, tokens), jnp.float32),
        ],
        after,
    )


def attention_far(side, queries, keys, values, partial_sum, top, total, after):
    width, tokens = queries.shape
    heads = width // HD
    all_rows, flat, far_rows = rows_block(tokens), flat_block(tokens), rows_block(PROMPT_DEV)
    return per_head(
        far_forward,
        "attention_far",
        heads,
        tokens * PROMPT_DEV,
        2,
        [
            (SCALAR, side),
            (all_rows, queries),
            (far_rows, keys),
            (far_rows, values),
            (all_rows, partial_sum),
            (flat, top),
            (flat, total),
        ],
        [
            (all_rows, (width, tokens), jnp.bfloat16),
            (flat, (heads, 1, tokens), jnp.float32),
        ],
        after,
    )


def attention_far_back(side, queries, keys, values, mixed, grads, lse, after):
    width, tokens = queries.shape
    heads = width // HD
    all_rows, flat, far_rows = rows_block(tokens), flat_block(tokens), rows_block(PROMPT_DEV)
    return per_head(
        far_backward,
        "attention_far_back",
        heads,
        tokens * PROMPT_DEV,
        3,
        [
            (SCALAR, side),
            (all_rows, queries),
            (far_rows, keys),
            (far_rows, values),
            (all_rows, mixed),
            (all_rows, grads),
            (flat, lse),
        ],
        [
            (all_rows, (width, tokens), jnp.float32),
            (flat, (heads, 1, tokens), jnp.float32),
            (
                pl.BlockSpec((2, HD, PROMPT_DEV), lambda head: (0, head, 0)),
                (2, width, PROMPT_DEV),
                jnp.bfloat16,
            ),
        ],
        after,
    )


def attention_own_back(start, gain, queries, keys, values, grads, lse, delta, far_dq, after):
    width, tokens = queries.shape
    heads = width // HD
    all_rows, flat = rows_block(tokens), flat_block(tokens)
    return per_head(
        own_backward,
        "attention_own_back",
        heads,
        tokens * tokens * 5 // 8,
        4,
        [
            (same_block(1, tokens), start),
            (same_block(HD, 1), gain),
            (all_rows, queries),
            (all_rows, keys),
            (all_rows, values),
            (all_rows, grads),
            (flat, lse),
            (flat, delta),
            (all_rows, far_dq),
        ],
        [
            (all_rows, (width, tokens), jnp.bfloat16),
            (all_rows, (width, tokens), jnp.bfloat16),
            (all_rows, (width, tokens), jnp.bfloat16),
            (pl.BlockSpec((HD, 1), lambda head: (head, 0)), (width, 1), jnp.float32),
        ],
        after,
        [pltpu.VMEM((HD, tokens), jnp.float32)] * 2,
    )


def segment_starts(lengths_row, tokens):
    place = jnp.arange(tokens, dtype=jnp.int32) - PROMPT_DEV
    bounds = jnp.cumsum(lengths_row)
    passed = jnp.where(place[:, None] >= bounds[None, :], bounds[None, :], 0)
    return (PROMPT_DEV + jnp.max(passed, axis=1))[None, :]


def body(
    inputs,
    cotangent,
    query_weight,
    key_weight,
    value_weight,
    output_weight,
    up_weight,
    down_weight,
    attention_gain,
    feed_gain,
    query_scale,
    cont_lengths,
):
    tokens = inputs.shape[0] * lax.axis_size("tensor")
    heads = query_weight.shape[2] // HD
    orders = exchange_orders(lax.axis_size("dp"))
    side = (lax.axis_index("dp") % 2).astype(jnp.int32)[None]
    start = segment_starts(cont_lengths[0], tokens)

    pairs = []
    for layer in range(LAYERS):
        pairs.append((key_weight[layer], value_weight[layer]))
        pairs.append((query_weight[layer], output_weight[layer].T))
        pairs.append((up_weight[layer], down_weight[layer].T))

    gather = Gather(pairs, orders)
    stored = []
    terms = [inputs.T]
    ready = ()
    for layer in range(LAYERS):
        attn_gain = attention_gain[layer][:, None]
        ff_gain = feed_gain[layer][:, None]
        current, inverse_attn, low = norm(terms, attn_gain, ready)
        normed, came = gather_tokens(low)
        gather.tick(came)
        if layer == 0:
            far = far_part(normed)
            gather.tick(far)
            far_normed, came = gather_tokens(far)
            gather.tick(came)
            wk, wv = gather.take()
            gather.tick()
        keys = lowered(dot_tn(wk, normed))
        values = lowered(dot_tn(wv, normed))
        gather.tick(keys, values)
        wq, wo = gather.take()
        gain_q = softplus(query_scale[layer]) * LOG_TWO_E / math.sqrt(HD)
        gain_rows = jnp.tile(gain_q, heads)[:, None]
        queries = lowered(dot_tn(wq, normed) * (gain_rows * LOG_TWO_E))
        own_sum, top, total = attention_own(start, queries, keys, values, ())
        if layer:
            far = far_part(normed)
            ready = gather.tick(top, far)
            far_normed, _ = gather_tokens(far)
        far_keys = lowered(dot_tn(wk, far_normed))
        far_values = lowered(dot_tn(wv, far_normed))
        if not layer:
            ready = gather.tick(top, far_keys, far_values)
        mixed, lse = attention_far(side, queries, far_keys, far_values, own_sum, top, total, ready)
        gather.tick(lse)
        (both,) = gather.take()
        terms = scatter_tokens(lambda rows: dot_nn(wo, rows), mixed)
        ups, downs = feed_parts(both)
        ready = gather.tick(terms[-1])
        middle, inverse_feed, feed = norm([current, *terms], ff_gain, ready)
        uppers = [dot_tn(w, feed) for w in ups]
        ready = gather.tick(*uppers)
        if layer + 1 < LAYERS:
            following = gather.take()
        hiddens = [lowered(upper * jax.nn.sigmoid(upper)) for upper in uppers]
        stored.append(
            (
                (current, inverse_attn, attn_gain, normed),
                (gain_q, queries, keys, values, far_keys, far_values, mixed, lse),
                (middle, inverse_feed, ff_gain, feed, uppers, hiddens),
                (wk, wv, wq, wo, ups, downs),
            )
        )
        terms = [middle, sum(dot_nn(w, hidden) for w, hidden in zip(downs, hiddens))]
        if layer + 1 < LAYERS:
            wk, wv = following
    current = terms[0] + terms[1]

    sums = Scatter(orders)
    small_grads = [None] * LAYERS
    grad = cotangent.T
    grad_low = lowered(grad)
    for layer in reversed(range(LAYERS)):
        (
            (source, inverse_attn, attn_gain, normed),
            (gain_q, queries, keys, values, far_keys, far_values, mixed, lse),
            (middle, inverse_feed, ff_gain, feed, uppers, hiddens),
            (wk, wv, wq, wo, ups, downs),
        ) = stored[layer]
        d_uppers = []
        for w, upper in zip(downs, uppers):
            d_hidden = lowered(dot_tn(w, grad_low)).astype(jnp.float32)
            sigmoid = jax.nn.sigmoid(upper)
            d_uppers.append(lowered(d_hidden * (sigmoid * (1.0 + upper * (1.0 - sigmoid)))))
        d_feed = sum(dot_nn(w, d_upper) for w, d_upper in zip(ups, d_uppers))
        ready = sums.tick(d_feed)
        grad_middle, low, feed_gain_grad = norm_back(
            middle, inverse_feed, ff_gain, grad, [d_feed], ready
        )
        middle_low, came = gather_tokens(low)
        down_grad, down_came = feed_total([dot_nt(grad_low, hidden) for hidden in hiddens])
        up_grad, up_came = feed_total([dot_nt(feed, d_upper) for d_upper in d_uppers])
        if down_came is None:
            stepped = sums.tick(came, down_grad, up_grad)
            sums.push(down_grad, up_grad)
        else:
            stepped = sums.tick(came, down_came, up_came)
            sums.push(down_grad, up_grad, came=(down_came, up_came))
        d_mixed = lowered(dot_tn(wo, middle_low))
        out_grad = lowered(dot_nt(middle_low, mixed))
        ready = [*sums.enter(), *stepped]
        far_dq, delta, far_dkv = attention_far_back(
            side, queries, far_keys, far_values, mixed, d_mixed, lse, ready
        )
        back = pair_swap(far_dkv, "dp", 1)
        ready = sums.tick(delta)
        d_raw, own_dk, own_dv, scale_rows = attention_own_back(
            start,
            gain_q[:, None],
            queries,
            keys,
            values,
            d_mixed,
            lse,
            delta,
            far_dq,
            ready,
        )
        ready = sums.tick(scale_rows)
        query_grad = lowered(dot_nt(normed, d_raw))
        sums.push(out_grad, query_grad)
        sums.enter()
        d_keys, d_values = add_back(own_dk, own_dv, back, ready)
        scale_raw = jnp.sum(scale_rows.reshape(heads, HD), 0) / (gain_q * LOG_TWO_E)
        scale_grad = scale_raw * jax.nn.sigmoid(query_scale[layer]) * LOG_TWO_E / math.sqrt(HD)
        terms = scatter_tokens(
            lambda dq, dk, dv: dot_nn(wq, dq) + dot_nn(wk, dk) + dot_nn(wv, dv),
            d_raw,
            d_keys,
            d_values,
        )
        ready = sums.tick(terms[-1])
        grad, grad_low, attn_gain_grad = norm_back(
            source, inverse_attn, attn_gain, grad_middle, terms, ready
        )
        key_grad = lowered(dot_nt(normed, d_keys))
        value_grad = lowered(dot_nt(normed, d_values))
        sums.push(key_grad, value_grad)
        sums.tick(grad, key_grad, value_grad)
        small_grads[layer] = jnp.concatenate([attn_gain_grad, feed_gain_grad, scale_grad])
    small = jnp.stack(small_grads)
    for axis in ("tensor", "dp"):
        bit = 1
        while bit < lax.axis_size(axis):
            came = pair_swap(small, axis, bit)
            after = sums.tick(came) if axis == "dp" else ()
            small, bit = tied(small + came, after), 2 * bit
    done = sums.finish()
    layer_grads = []
    for layer in range(LAYERS):
        at = 3 * (LAYERS - 1 - layer)
        (down_grad, up_grad), (out_grad, query_grad), (key_grad, value_grad) = done[at : at + 3]
        layer_grads.append(
            (query_grad, key_grad, value_grad, out_grad.T, up_grad, down_grad.T)
        )

    summed = [jnp.stack(members) for members in zip(*layer_grads)]
    width = current.shape[0]
    return (
        current.T,
        grad.T,
        *summed,
        small[:, :width],
        small[:, width : 2 * width],
        small[:, 2 * width :],
    )


def solution(mesh):
    in_specs = (
        P(("dp", "tensor"), None),
        P(("dp", "tensor"), None),
        P(None, "dp", "tensor"),
        P(None, "dp", "tensor"),
        P(None, "dp", "tensor"),
        P(None, "tensor", "dp"),
        P(None, "dp", "tensor"),
        P(None, "tensor", "dp"),
        P(),
        P(),
        P(),
        P("dp", None),
    )
    out_specs = (
        P(("dp", "tensor"), None),
        P(("dp", "tensor"), None),
        P(None, "dp", "tensor"),
        P(None, "dp", "tensor"),
        P(None, "dp", "tensor"),
        P(None, "tensor", "dp"),
        P(None, "dp", "tensor"),
        P(None, "tensor", "dp"),
        P(),
        P(),
        P(),
    )
    return jax.shard_map(body, mesh=mesh, in_specs=in_specs, out_specs=out_specs, check_vma=False)
```

```python
from functools import partial
import math

import jax
import jax.numpy as jnp
from jax import lax
from jax.experimental import pallas as pl
from jax.experimental.pallas import tpu as pltpu
from jax.sharding import PartitionSpec as P

HD = 80
LAYERS = 2
PROMPT_DEV = 512
TILE = 256

EPSILON = 1e-06
LOG_TWO_E = 1.4426950408889634
LN_TWO = 0.6931471805599453
NEGATIVE = -1e30


def lowered(values):
    return values.astype(jnp.bfloat16)


def dot_nn(former, latter):
    return jnp.dot(former, latter, preferred_element_type=jnp.float32)


def dot_tn(former, latter):
    return lax.dot_general(
        former, latter, (((0,), (0,)), ((), ())), preferred_element_type=jnp.float32
    )


def dot_nt(former, latter):
    return lax.dot_general(
        former, latter, (((1,), (1,)), ((), ())), preferred_element_type=jnp.float32
    )


def softplus(values):
    return jnp.log1p(jnp.exp(values))


def pair_swap(values, axis, bit):
    size = lax.axis_size(axis)
    return lax.ppermute(values, axis, [(i, i ^ bit) for i in range(size)])


def exchange_orders(size):
    if size == 16:
        return (8, 4), ((2, 1), (1, 2))
    bits = tuple(1 << k for k in reversed(range(size.bit_length() - 1)))
    first, rest = bits[:1], bits[1:]
    half = len(rest) // 2
    return first, (rest, rest[half:] + rest[:half])


WHOLE = pl.BlockSpec(memory_space=pltpu.VMEM)
SCALAR = pl.BlockSpec(memory_space=pltpu.SMEM)
UNREAD = pl.BlockSpec(memory_space=pl.ANY)


def dp_bits(bits):
    place = lax.axis_index("dp")
    return jnp.stack([((place & bit) != 0).astype(jnp.int32) for bit in bits])


def quick_call(kernel, name, arrays, after, out_shape):
    out = pl.pallas_call(
        kernel,
        in_specs=[SCALAR] + [WHOLE] * (len(arrays) - 1) + [UNREAD] * len(after),
        out_specs=[WHOLE] * len(out_shape),
        out_shape=out_shape,
        compiler_params=pltpu.CompilerParams(vmem_limit_bytes=48 << 20),
        cost_estimate=pl.CostEstimate(flops=1, bytes_accessed=1, transcendentals=0),
        name=name,
    )(*arrays, *after)
    return list(out)


class Gather:
    def __init__(self, pairs, orders):
        self.first, self.rest = orders
        self.queue = [jnp.stack(pair)[:, None] for pair in pairs]
        self.left = len(pairs)
        self.early, self.early_at = None, 0
        self.late, self.late_at = None, 0
        self.ready = []

    def tick(self, *after):
        if self.early is None and self.queue:
            self.early, self.early_at = self.queue.pop(0), 0
        if self.late is None and self.early is not None and self.early_at == len(self.first):
            self.late, self.late_at = self.early, 0
            self.early, self.early_at = (self.queue.pop(0), 0) if self.queue else (None, 0)
        jobs = []
        early = self.early is not None and self.early_at < len(self.first)
        if early:
            jobs.append((self.early, self.first[: self.early_at + 1]))
        if self.late is not None:
            for values, order in zip(self.late, self.rest):
                jobs.append((values, self.first + order[: self.late_at + 1]))
        if not jobs:
            return []
        got = [pair_swap(values, "dp", done[-1]) for values, done in jobs]
        plans, shapes = [], []
        for values, done in jobs:
            members, blocks, rows, width = values.shape
            before = 1 << sum(1 for bit in done[:-1] if bit > done[-1])
            parts = members if members > 1 and len(done) == len(self.first) else 1
            plans.append((members, before, blocks // before, parts, len(shapes)))
            shapes += [(members // parts, 2 * blocks, rows, width)] * parts
        count = len(jobs)
        merged = self.late is not None and self.merges() and (
            self.late_at + 1 == len(self.rest[0])
        )
        if merged:
            at = plans[-2][-1]
            shapes[at:] = [(2,) + shapes[at][1:]]
        following = self.queue[:1]

        def join(bit_ref, *refs):
            outs = refs[len(refs) - len(shapes) - len(following) :]
            if following:
                outs[-1][...] = refs[2 * count][...]
            for job, (members, before, blocks, parts, at) in enumerate(plans):
                bit = bit_ref[job]
                for member in range(members):
                    if merged and job == count - 1:
                        out, row = outs[at - 1], 1
                    elif parts > 1:
                        out, row = outs[at + member], 0
                    else:
                        out, row = outs[at], member
                    for step in range(before):
                        here = pl.ds(step * blocks, blocks)
                        place = 2 * step * blocks
                        ours, theirs = place + bit * blocks, place + (1 - bit) * blocks
                        out[row, pl.ds(ours, blocks)] = refs[job][member, here]
                        out[row, pl.ds(theirs, blocks)] = refs[count + job][member, here]

        outs = quick_call(
            join,
            "join_halves",
            [
                dp_bits([done[-1] for _, done in jobs]),
                *[values for values, _ in jobs],
                *got,
                *following,
            ],
            after,
            [
                jax.ShapeDtypeStruct(shape, jnp.bfloat16)
                for shape in shapes + [values.shape for values in following]
            ],
        )
        if following:
            self.queue[0] = outs.pop()
        if early:
            self.early_at += 1
            done = self.early_at == len(self.first)
            self.early = outs[:2] if done else outs[0]
        if self.late is not None:
            self.late, self.late_at = outs[-1:] if merged else outs[-2:], self.late_at + 1
            if self.late_at == len(self.rest[0]):
                width = self.late[0].shape[-1]
                shape = (2, -1, width) if merged else (-1, width)
                self.ready.append([values.reshape(shape) for values in self.late])
                self.late = None
                self.left -= 1
        return outs

    def merges(self):
        return self.left % 3 == 1

    def take(self):
        while not self.ready:
            self.tick()
        return self.ready.pop(0)


class Scatter:
    def __init__(self, orders):
        self.first, self.rest = orders
        self.bits = sorted(self.first + self.rest[0], reverse=True)
        self.queue, self.late, self.early, self.done = [], None, None, []

    def push(self, *pair, came=(None, None)):
        rows = pair[0].shape[0] >> len(self.bits)
        shape = (1, 1 << len(self.bits), rows, pair[0].shape[1])
        self.queue.append(
            [
                ([values.reshape(shape)], None if more is None else [more.reshape(shape)], order)
                for values, more, order in zip(pair, came, self.rest)
            ]
        )

    def run(self, jobs, after):
        plans, ins, shapes, bits = [], [], [], []
        for held, got, left, bit, joined in jobs:
            blocks, rows, width = held[0].shape[1:]
            members = sum(values.shape[0] for values in held)
            at = left.index(bit) if bit else 0
            behind = blocks // 2 >> at if bit else blocks
            plans.append((len(held), len(ins), bool(got), 1 << at, behind, bit, joined, len(shapes)))
            ins += held + (got or [])
            bits.append(bit or 1)
            if bit:
                groups = 1 if joined else members
                shapes += [((members // groups, blocks // 2, rows, width), jnp.bfloat16)] * (
                    2 * groups
                )
            else:
                shapes += [((rows, width), jnp.float32)] * members
        inputs = len(ins)

        def add(bit_ref, *refs):
            sources, outs = refs[:inputs], refs[len(refs) - len(shapes) :]
            for job, (arrays, at, come, before, behind, bit, joined, out_at) in enumerate(plans):
                mine = bit_ref[job]
                member = 0
                for array in range(arrays):
                    held = sources[at + array]
                    for row in range(held.shape[0]):

                        def total(start):
                            values = held[row, pl.ds(start, behind)]
                            if come:
                                other = sources[at + arrays + array][row, pl.ds(start, behind)]
                                values = values.astype(jnp.float32) + other.astype(jnp.float32)
                            return values

                        if bit is None:
                            outs[out_at + member][...] = total(0)[0]
                        else:
                            keep, send, place = (
                                (outs[out_at], outs[out_at + 1], member)
                                if joined
                                else (outs[out_at + 2 * member], outs[out_at + 2 * member + 1], 0)
                            )
                            for step in range(before):
                                start = 2 * step * behind
                                there = pl.ds(step * behind, behind)
                                keep[place, there] = lowered(total(start + mine * behind))
                                send[place, there] = lowered(total(start + (1 - mine) * behind))
                        member += 1

        return quick_call(
            add,
            "add_halves",
            [dp_bits(bits), *ins],
            after,
            [jax.ShapeDtypeStruct(shape, kind) for shape, kind in shapes],
        )

    def enter(self):
        if self.late is not None or not self.queue:
            return []
        jobs = [
            (held, came, self.bits, order[-1], False) for held, came, order in self.queue.pop(0)
        ]
        outs = self.run(jobs, ())
        self.late = (outs[0::2], outs[1::2], 1)
        return outs

    def tick(self, *after):
        self.enter()
        jobs, steps = [], len(self.rest[0])
        if self.early is not None:
            keep, send, at = self.early
            bits = self.first[: len(self.first) - at + 1]
            left = sorted(bits[:-1], reverse=True)
            got = [pair_swap(send, "dp", bits[-1])]
            jobs.append(([keep], got, left, bits[-2] if left else None, True))
        if self.late is not None:
            keeps, sends, at = self.late
            got = [
                pair_swap(send, "dp", order[steps - at]) for send, order in zip(sends, self.rest)
            ]
            for keep, come, order in zip(keeps, got, self.rest):
                left = sorted(self.first + order[: steps - at], reverse=True)
                if at < steps:
                    jobs.append(([keep], [come], left, order[steps - at - 1], False))
            if at == steps:
                jobs.append((keeps, got, left, self.first[-1], True))
        if not jobs:
            return []
        outs = self.run(jobs, after)
        rest = outs
        if self.early is not None:
            if at_end(self.early[2], self.first):
                self.done.append(rest[:2])
                self.early = None
            else:
                self.early = (rest[0], rest[1], self.early[2] + 1)
            rest = rest[2:]
        if self.late is not None:
            if self.late[2] == steps:
                self.early, self.late = (rest[0], rest[1], 1), None
            else:
                self.late = (rest[0::2], rest[1::2], self.late[2] + 1)
        return outs

    def finish(self):
        while self.queue or self.late or self.early:
            self.tick()
        return self.done


def at_end(step, bits):
    return step == len(bits)


def gather_tokens(local):
    if lax.axis_size("tensor") != 2:
        values = lax.all_gather(local, "tensor", axis=1, tiled=True)
        return values, values
    other = pair_swap(local, "tensor", 1)
    upper = lax.axis_index("tensor") != 0
    values = [jnp.where(upper, other, local), jnp.where(upper, local, other)]
    return jnp.concatenate(values, axis=1), other


def far_part(normed):
    part = PROMPT_DEV // lax.axis_size("tensor")
    place = lax.axis_index("tensor") * part
    return pair_swap(lax.dynamic_slice_in_dim(normed, place, part, 1), "dp", 1)


def scatter_tokens(product, *values):
    if lax.axis_size("tensor") != 2:
        return [
            lax.psum_scatter(
                lowered(product(*values)), "tensor", scatter_dimension=1, tiled=True
            )
        ]
    count = values[0].shape[1] // 2
    place = lax.axis_index("tensor")
    theirs = [lax.dynamic_slice_in_dim(v, (1 - place) * count, count, 1) for v in values]
    got = pair_swap(lowered(product(*theirs)), "tensor", 1)
    mine = [lax.dynamic_slice_in_dim(v, place * count, count, 1) for v in values]
    return [lowered(product(*mine)), got]


def feed_parts(both):
    if lax.axis_size("tensor") != 2:
        whole = lax.all_gather(both, "tensor", axis=2, tiled=True)
        return [whole[0]], [whole[1]]
    other = pair_swap(both, "tensor", 1)
    return [both[0], other[0]], [both[1], other[1]]


def feed_total(parts):
    if lax.axis_size("tensor") != 2:
        whole = lax.psum_scatter(lowered(parts[0]), "tensor", scatter_dimension=1, tiled=True)
        return whole, None
    return lowered(parts[0]), pair_swap(lowered(parts[1]), "tensor", 1)


def exchange_sum(values, axis, bit, bits, exchange):
    wide = bits == 2 and 2 * bit < lax.axis_size(axis)
    came = [pair_swap(values, axis, bit * by) for by in ((1, 2, 3) if wide else (1,))]
    after = exchange.tick(*came)
    total = values + came[0]
    if wide:
        total = total + (came[1] + came[2])
    return tied(total, after)


def tied(gain, after):
    if not after:
        return gain
    corner = after[0][(0,) * after[0].ndim].astype(jnp.float32)
    return gain + jnp.minimum((corner > 3e38).astype(jnp.int32), 0).astype(jnp.float32)


def norm(terms, gain, after=()):
    total = sum(term.astype(jnp.float32) for term in terms)
    inverse = lax.rsqrt(jnp.mean(total * total, axis=0, keepdims=True) + EPSILON)
    return total, inverse, lowered(total * inverse * tied(gain, after))


def norm_back(source, inverse, gain, grad, terms, after=()):
    incoming = sum(term.astype(jnp.float32) for term in terms)
    unit = source * inverse
    gain_grad = jnp.sum(incoming * unit, axis=1)
    scaled = incoming * tied(gain, after)
    total = grad + inverse * (scaled - unit * jnp.mean(scaled * unit, axis=0, keepdims=True))
    return total, lowered(total), gain_grad


def first_slot(_):
    return jnp.zeros((1,), jnp.int32)


def add_back(own_keys, own_values, back, after):
    def kernel(_, keys_ref, values_ref, back_ref, *refs):
        for place, (ref, out) in enumerate(zip((keys_ref, values_ref), refs[-2:])):
            prompt = ref[:, :PROMPT_DEV].astype(jnp.float32) + back_ref[place].astype(jnp.float32)
            out[:, :PROMPT_DEV] = lowered(prompt)
            out[:, PROMPT_DEV:] = ref[:, PROMPT_DEV:]

    out = [jax.ShapeDtypeStruct(own_keys.shape, jnp.bfloat16)] * 2
    arrays = [first_slot(back), own_keys, own_values, back]
    return quick_call(kernel, "add_back", arrays, after, out)


def key_parts(tile):
    first = tile * TILE
    if first < PROMPT_DEV:
        return ([(0, first, "free")] if first else []) + [(first, TILE, "earlier")]
    return [(0, PROMPT_DEV, "free"), (PROMPT_DEV, first - PROMPT_DEV + TILE, "segment")]


def masked(scores, kind, first_key, first_query, start):
    if kind == "free":
        return scores
    key = lax.broadcasted_iota(jnp.int32, scores.shape, 0) + first_key
    query = lax.broadcasted_iota(jnp.int32, scores.shape, 1) + first_query
    allowed = key <= query
    if kind == "segment":
        allowed = allowed & (key >= start)
    return jnp.where(allowed, scores, NEGATIVE)


def spans(reference):
    tokens = reference.shape[1]
    return [(tile, slice(tile * TILE, tile * TILE + TILE)) for tile in range(tokens // TILE)]


def ahead(items, first, second):
    items = list(items)
    held = first(items[0])
    for place, item in enumerate(items):
        following = first(items[place + 1]) if place + 1 < len(items) else None
        second(item, held)
        held = following


def own_forward(start_ref, q_ref, k_ref, v_ref, sum_ref, top_ref, total_ref):
    keys = k_ref[...].T

    def scores_of(item):
        tile, at = item
        query, start = q_ref[:, at], start_ref[:, at]
        return [
            masked(dot_nn(keys[key : key + count], query), kind, key, tile * TILE, start)
            for key, count, kind in key_parts(tile)
        ]

    def mix(item, parts):
        tile, at = item
        highest = jnp.max(parts[0], axis=0, keepdims=True)
        for scores in parts[1:]:
            highest = jnp.maximum(highest, jnp.max(scores, axis=0, keepdims=True))
        total, mixed = 0.0, 0.0
        for scores, (key, count, _) in zip(parts, key_parts(tile)):
            weights = jnp.exp2(scores - highest)
            total = total + jnp.sum(weights, axis=0, keepdims=True)
            mixed = mixed + dot_nn(v_ref[:, key : key + count], lowered(weights))
        sum_ref[:, at] = mixed
        top_ref[:, at] = highest
        total_ref[:, at] = total

    ahead(spans(q_ref), scores_of, mix)


def far_forward(
    side_ref, q_ref, k_ref, v_ref, sum_ref, top_ref, total_ref, out_ref, lse_ref
):
    keys = k_ref[...].T

    def scores_of(at):
        return dot_nn(keys, q_ref[:, at])

    def mix(at, scores):
        highest = jnp.maximum(top_ref[:, at], jnp.max(scores, axis=0, keepdims=True))
        weights = jnp.exp2(scores - highest)
        scale = jnp.exp2(top_ref[:, at] - highest)
        total = total_ref[:, at] * scale + jnp.sum(weights, axis=0, keepdims=True)
        mixed = sum_ref[:, at] * scale + dot_nn(v_ref[...], lowered(weights))
        out_ref[:, at] = lowered(mixed / total)
        lse_ref[:, at] = highest + jnp.log2(total)

    tiles = [at for _, at in spans(q_ref)]
    conts = [at for tile, at in spans(q_ref) if tile * TILE >= PROMPT_DEV]

    @pl.when(side_ref[0] == 0)
    def _():
        for at in tiles:
            if at not in conts:
                out_ref[:, at] = lowered(sum_ref[:, at] / total_ref[:, at])
                lse_ref[:, at] = top_ref[:, at] + jnp.log2(total_ref[:, at])
        ahead(conts, scores_of, mix)

    @pl.when(side_ref[0] != 0)
    def _():
        ahead(tiles, scores_of, mix)


def score_grads(scores, lse, d_shares, delta):
    shares = jnp.exp2(scores - lse)
    return lowered(shares), lowered(shares * (d_shares - delta))


def far_backward(
    side_ref, q_ref, k_ref, v_ref, out_ref, grad_ref, lse_ref, dq_ref, delta_ref, dkv_ref
):
    keys, values = k_ref[...].T, v_ref[...].T
    delta_ref[...] = jnp.sum(
        out_ref[...].astype(jnp.float32) * grad_ref[...].astype(jnp.float32), axis=0, keepdims=True
    )

    def begin(at):
        return dot_nn(keys, q_ref[:, at]), dot_nn(values, grad_ref[:, at])

    def close(tiles):
        sums = [0.0, 0.0]

        def terms(at, held):
            scores, d_shares = held
            shares, d_scores = score_grads(scores, lse_ref[:, at], d_shares, delta_ref[:, at])
            dq_ref[:, at] = dot_nn(k_ref[...], d_scores)
            sums[0] = sums[0] + dot_nt(q_ref[:, at], d_scores)
            sums[1] = sums[1] + dot_nt(grad_ref[:, at], shares)

        ahead(tiles, begin, terms)
        dkv_ref[0] = lowered(sums[0] * LN_TWO)
        dkv_ref[1] = lowered(sums[1])

    tiles = [at for _, at in spans(q_ref)]
    conts = [at for tile, at in spans(q_ref) if tile * TILE >= PROMPT_DEV]

    @pl.when(side_ref[0] == 0)
    def _():
        for at in tiles:
            if at not in conts:
                dq_ref[:, at] = jnp.zeros_like(dq_ref[:, at])
        close(conts)

    @pl.when(side_ref[0] != 0)
    def _():
        close(tiles)


def own_backward(
    start_ref,
    gain_ref,
    q_ref,
    k_ref,
    v_ref,
    grad_ref,
    lse_ref,
    delta_ref,
    far_dq_ref,
    dq_ref,
    dk_ref,
    dv_ref,
    scale_ref,
    k_total,
    v_total,
):
    keys, values = k_ref[...].T, v_ref[...].T
    seen, dqs, scales = set(), {}, [0.0]

    def begin(item):
        (tile, at), (key, count, kind), _ = item
        scores = dot_nn(keys[key : key + count], q_ref[:, at])
        scores = masked(scores, kind, key, tile * TILE, start_ref[:, at])
        return scores, dot_nn(values[key : key + count], grad_ref[:, at])

    def terms(item, held):
        (tile, at), (key, count, _), last = item
        scores, d_shares = held
        query, grad = q_ref[:, at], grad_ref[:, at]
        shares, d_scores = score_grads(scores, lse_ref[:, at], d_shares, delta_ref[:, at])
        dv = dot_nt(grad, shares)
        dk = dot_nt(query, d_scores)
        dq = dqs.get(tile, far_dq_ref[:, at]) + dot_nn(k_ref[:, key : key + count], d_scores)
        dqs[tile] = dq
        for offset in range(0, count, TILE):
            there = slice(key + offset, key + offset + TILE)
            here = slice(offset, offset + TILE)
            if key + offset in seen:
                k_total[:, there] += dk[:, here]
                v_total[:, there] += dv[:, here]
            else:
                seen.add(key + offset)
                k_total[:, there] = dk[:, here]
                v_total[:, there] = dv[:, here]
        if last:
            dq_ref[:, at] = lowered(dq * gain_ref[...])
            product = jnp.sum(dq * query.astype(jnp.float32), axis=1, keepdims=True)
            scales[0] = scales[0] + product

    items = []
    for tile, at in spans(q_ref):
        parts = key_parts(tile)
        items += [((tile, at), part, part is parts[-1]) for part in parts]
    ahead(items, begin, terms)
    dk_ref[...] = lowered(k_total[...] * LN_TWO)
    dv_ref[...] = lowered(v_total[...])
    scale_ref[...] = scales[0]


def rows_block(count):
    return pl.BlockSpec((HD, count), lambda head: (head, 0))


def flat_block(count):
    return pl.BlockSpec((None, 1, count), lambda head: (head, 0, 0))


def same_block(*shape):
    return pl.BlockSpec(shape, lambda head: (0, 0))


def per_head(kernel, name, heads, area, products, ins, outs, after=(), scratch=()):
    flops = 40 * area * heads * products
    moved = sum(array.size * array.dtype.itemsize for _, array in ins)
    count = len(ins)

    def work(*refs):
        kernel(*refs[:count], *refs[count + len(after) :])

    return pl.pallas_call(
        work,
        grid=(heads,),
        in_specs=[spec for spec, _ in ins] + [UNREAD] * len(after),
        out_specs=[spec for spec, _, _ in outs],
        out_shape=[jax.ShapeDtypeStruct(shape, kind) for _, shape, kind in outs],
        scratch_shapes=list(scratch),
        compiler_params=pltpu.CompilerParams(vmem_limit_bytes=32 << 20),
        cost_estimate=pl.CostEstimate(
            flops=flops, bytes_accessed=moved, transcendentals=area * heads
        ),
        name=name,
    )(*[array for _, array in ins], *after)


def attention_own(start, queries, keys, values, after):
    width, tokens = queries.shape
    heads = width // HD
    all_rows, flat = rows_block(tokens), flat_block(tokens)
    return per_head(
        own_forward,
        "attention_own",
        heads,
        tokens * tokens * 5 // 8,
        3,
        [
            (same_block(1, tokens), start),
            (all_rows, queries),
            (all_rows, keys),
            (all_rows, values),
        ],
        [
            (all_rows, (width, tokens), jnp.float32),
            (flat, (heads, 1, tokens), jnp.float32),
            (flat, (heads, 1, tokens), jnp.float32),
        ],
        after,
    )


def attention_far(side, queries, keys, values, partial_sum, top, total, after):
    width, tokens = queries.shape
    heads = width // HD
    all_rows, flat, far_rows = rows_block(tokens), flat_block(tokens), rows_block(PROMPT_DEV)
    return per_head(
        far_forward,
        "attention_far",
        heads,
        tokens * PROMPT_DEV,
        2,
        [
            (SCALAR, side),
            (all_rows, queries),
            (far_rows, keys),
            (far_rows, values),
            (all_rows, partial_sum),
            (flat, top),
            (flat, total),
        ],
        [
            (all_rows, (width, tokens), jnp.bfloat16),
            (flat, (heads, 1, tokens), jnp.float32),
        ],
        after,
    )


def attention_far_back(side, queries, keys, values, mixed, grads, lse, after):
    width, tokens = queries.shape
    heads = width // HD
    all_rows, flat, far_rows = rows_block(tokens), flat_block(tokens), rows_block(PROMPT_DEV)
    return per_head(
        far_backward,
        "attention_far_back",
        heads,
        tokens * PROMPT_DEV,
        3,
        [
            (SCALAR, side),
            (all_rows, queries),
            (far_rows, keys),
            (far_rows, values),
            (all_rows, mixed),
            (all_rows, grads),
            (flat, lse),
        ],
        [
            (all_rows, (width, tokens), jnp.float32),
            (flat, (heads, 1, tokens), jnp.float32),
            (
                pl.BlockSpec((2, HD, PROMPT_DEV), lambda head: (0, head, 0)),
                (2, width, PROMPT_DEV),
                jnp.bfloat16,
            ),
        ],
        after,
    )


def attention_own_back(start, gain, queries, keys, values, grads, lse, delta, far_dq, after):
    width, tokens = queries.shape
    heads = width // HD
    all_rows, flat = rows_block(tokens), flat_block(tokens)
    return per_head(
        own_backward,
        "attention_own_back",
        heads,
        tokens * tokens * 5 // 8,
        76,
        [
            (same_block(1, tokens), start),
            (same_block(HD, 1), gain),
            (all_rows, queries),
            (all_rows, keys),
            (all_rows, values),
            (all_rows, grads),
            (flat, lse),
            (flat, delta),
            (all_rows, far_dq),
        ],
        [
            (all_rows, (width, tokens), jnp.bfloat16),
            (all_rows, (width, tokens), jnp.bfloat16),
            (all_rows, (width, tokens), jnp.bfloat16),
            (pl.BlockSpec((HD, 1), lambda head: (head, 0)), (width, 1), jnp.float32),
        ],
        after,
        [pltpu.VMEM((HD, tokens), jnp.float32)] * 2,
    )


def segment_starts(lengths_row, tokens):
    place = jnp.arange(tokens, dtype=jnp.int32) - PROMPT_DEV
    bounds = jnp.cumsum(lengths_row)
    passed = jnp.where(place[:, None] >= bounds[None, :], bounds[None, :], 0)
    return (PROMPT_DEV + jnp.max(passed, axis=1))[None, :]


def body(
    inputs,
    cotangent,
    query_weight,
    key_weight,
    value_weight,
    output_weight,
    up_weight,
    down_weight,
    attention_gain,
    feed_gain,
    query_scale,
    cont_lengths,
):
    tokens = inputs.shape[0] * lax.axis_size("tensor")
    heads = query_weight.shape[2] // HD
    orders = exchange_orders(lax.axis_size("dp"))
    side = (lax.axis_index("dp") % 2).astype(jnp.int32)[None]
    start = segment_starts(cont_lengths[0], tokens)

    pairs = []
    for layer in range(LAYERS):
        pairs.append((key_weight[layer], value_weight[layer]))
        pairs.append((query_weight[layer], output_weight[layer].T))
        pairs.append((up_weight[layer], down_weight[layer].T))

    gather = Gather(pairs, orders)
    stored = []
    terms = [inputs.T]
    ready = ()
    grad = cotangent.T
    for layer in range(LAYERS):
        attn_gain = attention_gain[layer][:, None]
        ff_gain = feed_gain[layer][:, None]
        current, inverse_attn, low = norm(terms, attn_gain, ready)
        normed, came = gather_tokens(low)
        gather.tick(came)
        if layer == 0:
            far = far_part(normed)
            gather.tick(far)
            far_normed, came = gather_tokens(far)
            gather.tick(came)
            gather.tick(grad)
            wk, wv = gather.take()
            gather.tick()
        keys = lowered(dot_tn(wk, normed))
        values = lowered(dot_tn(wv, normed))
        gather.tick(keys, values)
        wq, wo = gather.take()
        gain_q = softplus(query_scale[layer]) * LOG_TWO_E / math.sqrt(HD)
        gain_rows = jnp.tile(gain_q, heads)[:, None]
        queries = lowered(dot_tn(wq, normed) * (gain_rows * LOG_TWO_E))
        own_sum, top, total = attention_own(start, queries, keys, values, ())
        if layer:
            far = far_part(normed)
            ready = gather.tick(top, far)
            far_normed, _ = gather_tokens(far)
        far_keys = lowered(dot_tn(wk, far_normed))
        far_values = lowered(dot_tn(wv, far_normed))
        if not layer:
            ready = gather.tick(top, far_keys, far_values)
        mixed, lse = attention_far(side, queries, far_keys, far_values, own_sum, top, total, ready)
        gather.tick(lse)
        (both,) = gather.take()
        terms = scatter_tokens(lambda rows: dot_nn(wo, rows), mixed)
        ups, downs = feed_parts(both)
        ready = gather.tick(terms[-1])
        middle, inverse_feed, feed = norm([current, *terms], ff_gain, ready)
        uppers = [dot_tn(w, feed) for w in ups]
        ready = gather.tick(*uppers)
        if layer + 1 < LAYERS:
            following = gather.take()
        hiddens = [lowered(upper * jax.nn.sigmoid(upper)) for upper in uppers]
        stored.append(
            (
                (current, inverse_attn, attn_gain, normed),
                (gain_q, queries, keys, values, far_keys, far_values, mixed, lse),
                (middle, inverse_feed, ff_gain, feed, uppers, hiddens),
                (wk, wv, wq, wo, ups, downs),
            )
        )
        terms = [middle, sum(dot_nn(w, hidden) for w, hidden in zip(downs, hiddens))]
        if layer + 1 < LAYERS:
            wk, wv = following
    current = terms[0] + terms[1]

    sums = Scatter(orders)
    small_grads = [None] * LAYERS
    grad_low = lowered(grad)
    for layer in reversed(range(LAYERS)):
        (
            (source, inverse_attn, attn_gain, normed),
            (gain_q, queries, keys, values, far_keys, far_values, mixed, lse),
            (middle, inverse_feed, ff_gain, feed, uppers, hiddens),
            (wk, wv, wq, wo, ups, downs),
        ) = stored[layer]
        d_uppers = []
        for w, upper in zip(downs, uppers):
            d_hidden = lowered(dot_tn(w, grad_low)).astype(jnp.float32)
            sigmoid = jax.nn.sigmoid(upper)
            d_uppers.append(lowered(d_hidden * (sigmoid * (1.0 + upper * (1.0 - sigmoid)))))
        d_feed = sum(dot_nn(w, d_upper) for w, d_upper in zip(ups, d_uppers))
        ready = sums.tick(d_feed)
        grad_middle, low, feed_gain_grad = norm_back(
            middle, inverse_feed, ff_gain, grad, [d_feed], ready
        )
        middle_low, came = gather_tokens(low)
        down_grad, down_came = feed_total([dot_nt(grad_low, hidden) for hidden in hiddens])
        up_grad, up_came = feed_total([dot_nt(feed, d_upper) for d_upper in d_uppers])
        if down_came is None:
            stepped = sums.tick(came, down_grad, up_grad)
            sums.push(down_grad, up_grad)
        else:
            stepped = sums.tick(came, down_came, up_came)
            sums.push(down_grad, up_grad, came=(down_came, up_came))
        d_mixed = lowered(dot_tn(wo, middle_low))
        out_grad = lowered(dot_nt(middle_low, mixed))
        ready = [*sums.enter(), *stepped]
        far_dq, delta, far_dkv = attention_far_back(
            side, queries, far_keys, far_values, mixed, d_mixed, lse, ready
        )
        back = pair_swap(far_dkv, "dp", 1)
        ready = sums.tick(delta)
        d_raw, own_dk, own_dv, scale_rows = attention_own_back(
            start,
            gain_q[:, None],
            queries,
            keys,
            values,
            d_mixed,
            lse,
            delta,
            far_dq,
            ready,
        )
        ready = sums.tick(scale_rows)
        query_grad = lowered(dot_nt(normed, d_raw))
        sums.push(out_grad, query_grad)
        ready = [*ready, *sums.enter()]
        d_keys, d_values = add_back(own_dk, own_dv, back, ready)
        scale_raw = jnp.sum(scale_rows.reshape(heads, HD), 0) / (gain_q * LOG_TWO_E)
        scale_grad = scale_raw * jax.nn.sigmoid(query_scale[layer]) * LOG_TWO_E / math.sqrt(HD)
        if not layer:
            key_grad, value_grad = [lowered(dot_nt(normed, d)) for d in (d_keys, d_values)]
            ready = sums.tick(key_grad, value_grad)
            last = Scatter(orders)
            last.push(key_grad, value_grad)
            last.enter()
        terms = scatter_tokens(
            lambda dq, dk, dv: dot_nn(wq, dq) + dot_nn(wk, dk) + dot_nn(wv, dv),
            d_raw,
            d_keys,
            d_values,
        )
        if layer:
            ready = sums.tick(terms[-1])
        else:
            sums.tick(terms[-1])
            ready = last.tick(terms[-1])
        grad, grad_low, attn_gain_grad = norm_back(
            source, inverse_attn, attn_gain, grad_middle, terms, ready
        )
        if layer:
            key_grad, value_grad = [lowered(dot_nt(normed, d)) for d in (d_keys, d_values)]
            sums.push(key_grad, value_grad)
            sums.tick(grad, key_grad, value_grad)
        small_grads[layer] = jnp.concatenate([attn_gain_grad, feed_gain_grad, scale_grad])
    small = jnp.stack(small_grads)
    for axis, bits in (("tensor", 1), ("dp", 2)):
        bit = 1
        while bit < lax.axis_size(axis):
            small, bit = exchange_sum(small, axis, bit, bits, last), bit << bits
    done = sums.finish() + last.finish()
    layer_grads = []
    for layer in range(LAYERS):
        at = 3 * (LAYERS - 1 - layer)
        (down_grad, up_grad), (out_grad, query_grad), (key_grad, value_grad) = done[at : at + 3]
        layer_grads.append(
            (query_grad, key_grad, value_grad, out_grad.T, up_grad, down_grad.T)
        )

    summed = [jnp.stack(members) for members in zip(*layer_grads)]
    width = current.shape[0]
    return (
        current.T,
        grad.T,
        *summed,
        small[:, :width],
        small[:, width : 2 * width],
        small[:, 2 * width :],
    )


def solution(mesh):
    in_specs = (
        P(("dp", "tensor"), None),
        P(("dp", "tensor"), None),
        P(None, "dp", "tensor"),
        P(None, "dp", "tensor"),
        P(None, "dp", "tensor"),
        P(None, "tensor", "dp"),
        P(None, "dp", "tensor"),
        P(None, "tensor", "dp"),
        P(),
        P(),
        P(),
        P("dp", None),
    )
    out_specs = (
        P(("dp", "tensor"), None),
        P(("dp", "tensor"), None),
        P(None, "dp", "tensor"),
        P(None, "dp", "tensor"),
        P(None, "dp", "tensor"),
        P(None, "tensor", "dp"),
        P(None, "dp", "tensor"),
        P(None, "tensor", "dp"),
        P(),
        P(),
        P(),
    )
    return jax.shard_map(body, mesh=mesh, in_specs=in_specs, out_specs=out_specs, check_vma=False)
```

```python
from functools import partial
import math

import jax
import jax.numpy as jnp
from jax import lax
from jax.experimental.layout import Layout, with_layout_constraint
from jax.experimental import pallas as pl
from jax.experimental.pallas import tpu as pltpu
from jax.sharding import PartitionSpec as P

HD = 80
LAYERS = 2
PROMPT_DEV = 512
TILE = 256

EPSILON = 1e-06
LOG_TWO_E = 1.4426950408889634
LN_TWO = 0.6931471805599453
NEGATIVE = -1e30


def lowered(values):
    return values.astype(jnp.bfloat16)


def dot_nn(former, latter):
    return jnp.dot(former, latter, preferred_element_type=jnp.float32)


def dot_tn(former, latter):
    return lax.dot_general(
        former, latter, (((0,), (0,)), ((), ())), preferred_element_type=jnp.float32
    )


def dot_nt(former, latter):
    return lax.dot_general(
        former, latter, (((1,), (1,)), ((), ())), preferred_element_type=jnp.float32
    )


def softplus(values):
    return jnp.log1p(jnp.exp(values))


def pair_swap(values, axis, bit):
    size = lax.axis_size(axis)
    return lax.ppermute(values, axis, [(i, i ^ bit) for i in range(size)])


def exchange_orders(size):
    if size == 16:
        return (8, 4), ((2, 1), (1, 2))
    bits = tuple(1 << k for k in reversed(range(size.bit_length() - 1)))
    first, rest = bits[:1], bits[1:]
    half = len(rest) // 2
    return first, (rest, rest[half:] + rest[:half])


WHOLE = pl.BlockSpec(memory_space=pltpu.VMEM)
SCALAR = pl.BlockSpec(memory_space=pltpu.SMEM)
UNREAD = pl.BlockSpec(memory_space=pl.ANY)


def dp_bits(bits):
    place = lax.axis_index("dp")
    return jnp.stack([((place & bit) != 0).astype(jnp.int32) for bit in bits])


def quick_call(kernel, name, arrays, after, out_shape):
    out = pl.pallas_call(
        kernel,
        in_specs=[SCALAR] + [WHOLE] * (len(arrays) - 1) + [UNREAD] * len(after),
        out_specs=[WHOLE] * len(out_shape),
        out_shape=out_shape,
        compiler_params=pltpu.CompilerParams(vmem_limit_bytes=48 << 20),
        cost_estimate=pl.CostEstimate(flops=1, bytes_accessed=1, transcendentals=0),
        name=name,
    )(*arrays, *after)
    return list(out)


class Gather:
    def __init__(self, pairs, orders):
        self.first, self.rest = orders
        self.queue = [jnp.stack(pair)[:, None] for pair in pairs]
        self.left = len(pairs)
        self.early, self.early_at = None, 0
        self.late, self.late_at = None, 0
        self.ready = []

    def tick(self, *after):
        if self.early is None and self.queue:
            self.early, self.early_at = self.queue.pop(0), 0
        if self.late is None and self.early is not None and self.early_at == len(self.first):
            self.late, self.late_at = self.early, 0
            self.early, self.early_at = (self.queue.pop(0), 0) if self.queue else (None, 0)
        jobs = []
        early = self.early is not None and self.early_at < len(self.first)
        if early:
            jobs.append((self.early, self.first[: self.early_at + 1]))
        if self.late is not None:
            for values, order in zip(self.late, self.rest):
                jobs.append((values, self.first + order[: self.late_at + 1]))
        if not jobs:
            return []
        got = [pair_swap(values, "dp", done[-1]) for values, done in jobs]
        plans, shapes = [], []
        for values, done in jobs:
            members, blocks, rows, width = values.shape
            before = 1 << sum(1 for bit in done[:-1] if bit > done[-1])
            parts = members if members > 1 and len(done) == len(self.first) else 1
            plans.append((members, before, blocks // before, parts, len(shapes)))
            shapes += [(members // parts, 2 * blocks, rows, width)] * parts
        count = len(jobs)
        merged = self.late is not None and self.merges() and (
            self.late_at + 1 == len(self.rest[0])
        )
        if merged:
            at = plans[-2][-1]
            shapes[at:] = [(2,) + shapes[at][1:]]
        following = self.queue[:1]

        def join(bit_ref, *refs):
            outs = refs[len(refs) - len(shapes) - len(following) :]
            if following:
                outs[-1][...] = refs[2 * count][...]
            for job, (members, before, blocks, parts, at) in enumerate(plans):
                bit = bit_ref[job]
                for member in range(members):
                    if merged and job == count - 1:
                        out, row = outs[at - 1], 1
                    elif parts > 1:
                        out, row = outs[at + member], 0
                    else:
                        out, row = outs[at], member
                    for step in range(before):
                        here = pl.ds(step * blocks, blocks)
                        place = 2 * step * blocks
                        ours, theirs = place + bit * blocks, place + (1 - bit) * blocks
                        out[row, pl.ds(ours, blocks)] = refs[job][member, here]
                        out[row, pl.ds(theirs, blocks)] = refs[count + job][member, here]

        outs = quick_call(
            join,
            "join_halves",
            [
                dp_bits([done[-1] for _, done in jobs]),
                *[values for values, _ in jobs],
                *got,
                *following,
            ],
            after,
            [
                jax.ShapeDtypeStruct(shape, jnp.bfloat16)
                for shape in shapes + [values.shape for values in following]
            ],
        )
        if following:
            self.queue[0] = outs.pop()
        if early:
            self.early_at += 1
            done = self.early_at == len(self.first)
            self.early = outs[:2] if done else outs[0]
        if self.late is not None:
            self.late, self.late_at = outs[-1:] if merged else outs[-2:], self.late_at + 1
            if self.late_at == len(self.rest[0]):
                width = self.late[0].shape[-1]
                shape = (2, -1, width) if merged else (-1, width)
                self.ready.append([values.reshape(shape) for values in self.late])
                self.late = None
                self.left -= 1
        return outs

    def merges(self):
        return self.left % 3 == 1

    def take(self):
        while not self.ready:
            self.tick()
        return self.ready.pop(0)


class Scatter:
    def __init__(self, orders):
        self.first, self.rest = orders
        self.bits = sorted(self.first + self.rest[0], reverse=True)
        self.queue, self.late, self.early, self.done = [], None, None, []

    def push(self, *pair, came=(None, None)):
        rows = pair[0].shape[0] >> len(self.bits)
        shape = (1, 1 << len(self.bits), rows, pair[0].shape[1])
        self.queue.append(
            [
                ([values.reshape(shape)], None if more is None else [more.reshape(shape)], order)
                for values, more, order in zip(pair, came, self.rest)
            ]
        )

    def run(self, jobs, after):
        plans, ins, shapes, bits = [], [], [], []
        for held, got, left, bit, joined in jobs:
            blocks, rows, width = held[0].shape[1:]
            members = sum(values.shape[0] for values in held)
            at = left.index(bit) if bit else 0
            behind = blocks // 2 >> at if bit else blocks
            plans.append((len(held), len(ins), bool(got), 1 << at, behind, bit, joined, len(shapes)))
            ins += held + (got or [])
            bits.append(bit or 1)
            if bit:
                groups = 1 if joined else members
                shapes += [((members // groups, blocks // 2, rows, width), jnp.bfloat16)] * (
                    2 * groups
                )
            else:
                shapes += [((rows, width), jnp.float32)] * members
        inputs = len(ins)

        def add(bit_ref, *refs):
            sources, outs = refs[:inputs], refs[len(refs) - len(shapes) :]
            for job, (arrays, at, come, before, behind, bit, joined, out_at) in enumerate(plans):
                mine = bit_ref[job]
                member = 0
                for array in range(arrays):
                    held = sources[at + array]
                    for row in range(held.shape[0]):

                        def total(start):
                            values = held[row, pl.ds(start, behind)]
                            if come:
                                other = sources[at + arrays + array][row, pl.ds(start, behind)]
                                values = values.astype(jnp.float32) + other.astype(jnp.float32)
                            return values

                        if bit is None:
                            outs[out_at + member][...] = total(0)[0]
                        else:
                            keep, send, place = (
                                (outs[out_at], outs[out_at + 1], member)
                                if joined
                                else (outs[out_at + 2 * member], outs[out_at + 2 * member + 1], 0)
                            )
                            for step in range(before):
                                start = 2 * step * behind
                                there = pl.ds(step * behind, behind)
                                keep[place, there] = lowered(total(start + mine * behind))
                                send[place, there] = lowered(total(start + (1 - mine) * behind))
                        member += 1

        return quick_call(
            add,
            "add_halves",
            [dp_bits(bits), *ins],
            after,
            [jax.ShapeDtypeStruct(shape, kind) for shape, kind in shapes],
        )

    def enter(self):
        if self.late is not None or not self.queue:
            return []
        jobs = [
            (held, came, self.bits, order[-1], False) for held, came, order in self.queue.pop(0)
        ]
        outs = self.run(jobs, ())
        self.late = (outs[0::2], outs[1::2], 1)
        return outs

    def tick(self, *after):
        self.enter()
        jobs, steps = [], len(self.rest[0])
        if self.early is not None:
            keep, send, at = self.early
            bits = self.first[: len(self.first) - at + 1]
            left = sorted(bits[:-1], reverse=True)
            got = [pair_swap(send, "dp", bits[-1])]
            jobs.append(([keep], got, left, bits[-2] if left else None, True))
        if self.late is not None:
            keeps, sends, at = self.late
            got = [
                pair_swap(send, "dp", order[steps - at]) for send, order in zip(sends, self.rest)
            ]
            for keep, come, order in zip(keeps, got, self.rest):
                left = sorted(self.first + order[: steps - at], reverse=True)
                if at < steps:
                    jobs.append(([keep], [come], left, order[steps - at - 1], False))
            if at == steps:
                jobs.append((keeps, got, left, self.first[-1], True))
        if not jobs:
            return []
        outs = self.run(jobs, after)
        rest = outs
        if self.early is not None:
            if at_end(self.early[2], self.first):
                self.done.append(rest[:2])
                self.early = None
            else:
                self.early = (rest[0], rest[1], self.early[2] + 1)
            rest = rest[2:]
        if self.late is not None:
            if self.late[2] == steps:
                self.early, self.late = (rest[0], rest[1], 1), None
            else:
                self.late = (rest[0::2], rest[1::2], self.late[2] + 1)
        return outs

    def finish(self):
        while self.queue or self.late or self.early:
            self.tick()
        return self.done


def at_end(step, bits):
    return step == len(bits)


def gather_tokens(local):
    if lax.axis_size("tensor") != 2:
        values = lax.all_gather(local, "tensor", axis=1, tiled=True)
        return values, values
    other = pair_swap(local, "tensor", 1)
    upper = lax.axis_index("tensor") != 0
    values = [jnp.where(upper, other, local), jnp.where(upper, local, other)]
    return jnp.concatenate(values, axis=1), other


def far_part(normed):
    part = PROMPT_DEV // lax.axis_size("tensor")
    place = lax.axis_index("tensor") * part
    return pair_swap(lax.dynamic_slice_in_dim(normed, place, part, 1), "dp", 1)


def scatter_tokens(product, *values):
    if lax.axis_size("tensor") != 2:
        return [
            lax.psum_scatter(
                lowered(product(*values)), "tensor", scatter_dimension=1, tiled=True
            )
        ]
    count = values[0].shape[1] // 2
    place = lax.axis_index("tensor")
    theirs = [lax.dynamic_slice_in_dim(v, (1 - place) * count, count, 1) for v in values]
    got = pair_swap(lowered(product(*theirs)), "tensor", 1)
    mine = [lax.dynamic_slice_in_dim(v, place * count, count, 1) for v in values]
    return [lowered(product(*mine)), got]


def feed_parts(both):
    if lax.axis_size("tensor") != 2:
        whole = lax.all_gather(both, "tensor", axis=2, tiled=True)
        return [whole[0]], [whole[1]]
    other = pair_swap(both, "tensor", 1)
    return [both[0], other[0]], [both[1], other[1]]


def feed_total(parts):
    if lax.axis_size("tensor") != 2:
        whole = lax.psum_scatter(lowered(parts[0]), "tensor", scatter_dimension=1, tiled=True)
        return whole, None
    mine, theirs = [with_layout_constraint(lowered(part), Layout((0, 1))) for part in parts]
    return mine, pair_swap(theirs, "tensor", 1)


def exchange_sum(values, axis, bit, bits, exchange):
    wide = bits == 2 and 2 * bit < lax.axis_size(axis)
    came = [pair_swap(values, axis, bit * by) for by in ((1, 2, 3) if wide else (1,))]
    after = exchange.tick(*came)
    total = values + came[0]
    if wide:
        total = total + (came[1] + came[2])
    return tied(total, after)


def tied(gain, after):
    if not after:
        return gain
    corner = after[0][(0,) * after[0].ndim].astype(jnp.float32)
    return gain + jnp.minimum((corner > 3e38).astype(jnp.int32), 0).astype(jnp.float32)


def norm(terms, gain, after=()):
    total = sum(term.astype(jnp.float32) for term in terms)
    inverse = lax.rsqrt(jnp.mean(total * total, axis=0, keepdims=True) + EPSILON)
    return total, inverse, lowered(total * inverse * tied(gain, after))


def norm_back(source, inverse, gain, grad, terms, after=()):
    incoming = sum(term.astype(jnp.float32) for term in terms)
    unit = source * inverse
    gain_grad = jnp.sum(incoming * unit, axis=1)
    scaled = incoming * tied(gain, after)
    total = grad + inverse * (scaled - unit * jnp.mean(scaled * unit, axis=0, keepdims=True))
    return total, lowered(total), gain_grad


def first_slot(_):
    return jnp.zeros((1,), jnp.int32)


def add_back(own_keys, own_values, back, after):
    def kernel(_, keys_ref, values_ref, back_ref, *refs):
        for place, (ref, out) in enumerate(zip((keys_ref, values_ref), refs[-2:])):
            prompt = ref[:, :PROMPT_DEV].astype(jnp.float32) + back_ref[place].astype(jnp.float32)
            out[:, :PROMPT_DEV] = lowered(prompt)
            out[:, PROMPT_DEV:] = ref[:, PROMPT_DEV:]

    out = [jax.ShapeDtypeStruct(own_keys.shape, jnp.bfloat16)] * 2
    arrays = [first_slot(back), own_keys, own_values, back]
    return quick_call(kernel, "add_back", arrays, after, out)


def key_parts(tile):
    first = tile * TILE
    if first < PROMPT_DEV:
        return ([(0, first, "free")] if first else []) + [(first, TILE, "earlier")]
    return [(0, PROMPT_DEV, "free"), (PROMPT_DEV, first - PROMPT_DEV + TILE, "segment")]


def masked(scores, kind, first_key, first_query, start):
    if kind == "free":
        return scores
    key = lax.broadcasted_iota(jnp.int32, scores.shape, 0) + first_key
    query = lax.broadcasted_iota(jnp.int32, scores.shape, 1) + first_query
    allowed = key <= query
    if kind == "segment":
        allowed = allowed & (key >= start)
    return jnp.where(allowed, scores, NEGATIVE)


def spans(reference):
    tokens = reference.shape[1]
    return [(tile, slice(tile * TILE, tile * TILE + TILE)) for tile in range(tokens // TILE)]


def ahead(steps):
    held = steps[0][0]()
    for place, (_, second) in enumerate(steps):
        following = steps[place + 1][0]() if place + 1 < len(steps) else None
        second(held)
        held = following


def own_forward(heads):
    def steps(start_ref, q_ref, k_ref, v_ref, sum_ref, top_ref, total_ref):
        keys = k_ref[...].T

        def scores_of(tile, at):
            query, start = q_ref[:, at], start_ref[:, at]
            return [
                masked(dot_nn(keys[key : key + count], query), kind, key, tile * TILE, start)
                for key, count, kind in key_parts(tile)
            ]

        def mix(tile, at, parts):
            highest = jnp.max(parts[0], axis=0, keepdims=True)
            for scores in parts[1:]:
                highest = jnp.maximum(highest, jnp.max(scores, axis=0, keepdims=True))
            total, mixed = 0.0, 0.0
            for scores, (key, count, _) in zip(parts, key_parts(tile)):
                weights = jnp.exp2(scores - highest)
                total = total + jnp.sum(weights, axis=0, keepdims=True)
                mixed = mixed + dot_nn(v_ref[:, key : key + count], lowered(weights))
            sum_ref[:, at] = mixed
            top_ref[:, at] = highest
            total_ref[:, at] = total

        return [(partial(scores_of, *item), partial(mix, *item)) for item in spans(q_ref)]

    ahead([step for refs in heads for step in steps(*refs)])


def sides(side_ref, q_ref, run):
    tiles = [at for _, at in spans(q_ref)]
    conts = [at for tile, at in spans(q_ref) if tile * TILE >= PROMPT_DEV]

    @pl.when(side_ref[0] == 0)
    def _():
        run(conts, [at for at in tiles if at not in conts])

    @pl.when(side_ref[0] != 0)
    def _():
        run(tiles, [])


def far_forward(heads):
    def steps(tiles, _, q_ref, k_ref, v_ref, sum_ref, top_ref, total_ref, out_ref, lse_ref):
        keys = k_ref[...].T

        def scores_of(at):
            return dot_nn(keys, q_ref[:, at])

        def mix(at, scores):
            highest = jnp.maximum(top_ref[:, at], jnp.max(scores, axis=0, keepdims=True))
            weights = jnp.exp2(scores - highest)
            scale = jnp.exp2(top_ref[:, at] - highest)
            total = total_ref[:, at] * scale + jnp.sum(weights, axis=0, keepdims=True)
            mixed = sum_ref[:, at] * scale + dot_nn(v_ref[...], lowered(weights))
            out_ref[:, at] = lowered(mixed / total)
            lse_ref[:, at] = highest + jnp.log2(total)

        return [(partial(scores_of, at), partial(mix, at)) for at in tiles]

    def run(tiles, others):
        for _, _, _, _, sum_ref, top_ref, total_ref, out_ref, lse_ref in heads:
            for at in others:
                out_ref[:, at] = lowered(sum_ref[:, at] / total_ref[:, at])
                lse_ref[:, at] = top_ref[:, at] + jnp.log2(total_ref[:, at])
        ahead([step for refs in heads for step in steps(tiles, *refs)])

    sides(heads[0][0], heads[0][1], run)


def score_grads(scores, lse, d_shares, delta):
    shares = jnp.exp2(scores - lse)
    return lowered(shares), lowered(shares * (d_shares - delta))


def far_backward(heads):
    def steps(
        tiles, _, q_ref, k_ref, v_ref, out_ref, grad_ref, lse_ref, dq_ref, delta_ref, dkv_ref
    ):
        keys, values = k_ref[...].T, v_ref[...].T
        delta_ref[...] = jnp.sum(
            out_ref[...].astype(jnp.float32) * grad_ref[...].astype(jnp.float32),
            axis=0,
            keepdims=True,
        )
        sums = [0.0, 0.0]

        def begin(at):
            return dot_nn(keys, q_ref[:, at]), dot_nn(values, grad_ref[:, at])

        def terms(at, held):
            scores, d_shares = held
            shares, d_scores = score_grads(scores, lse_ref[:, at], d_shares, delta_ref[:, at])
            dq_ref[:, at] = dot_nn(k_ref[...], d_scores)
            sums[0] = sums[0] + dot_nt(q_ref[:, at], d_scores)
            sums[1] = sums[1] + dot_nt(grad_ref[:, at], shares)
            if at is tiles[-1]:
                dkv_ref[0] = lowered(sums[0] * LN_TWO)
                dkv_ref[1] = lowered(sums[1])

        return [(partial(begin, at), partial(terms, at)) for at in tiles]

    def run(tiles, others):
        for refs in heads:
            for at in others:
                refs[7][:, at] = jnp.zeros_like(refs[7][:, at])
        ahead([step for refs in heads for step in steps(tiles, *refs)])

    sides(heads[0][0], heads[0][1], run)


def own_backward(heads):
    def steps(
        start_ref,
        gain_ref,
        q_ref,
        k_ref,
        v_ref,
        grad_ref,
        lse_ref,
        delta_ref,
        far_dq_ref,
        dq_ref,
        dk_ref,
        dv_ref,
        scale_ref,
        k_total,
        v_total,
    ):
        keys, values = k_ref[...].T, v_ref[...].T
        seen, dqs, scales = set(), {}, [0.0]
        final = spans(q_ref)[-1][0]

        def begin(tile, at, part, last):
            key, count, kind = part
            scores = dot_nn(keys[key : key + count], q_ref[:, at])
            scores = masked(scores, kind, key, tile * TILE, start_ref[:, at])
            return scores, dot_nn(values[key : key + count], grad_ref[:, at])

        def terms(tile, at, part, last, held):
            key, count, _ = part
            scores, d_shares = held
            query, grad = q_ref[:, at], grad_ref[:, at]
            shares, d_scores = score_grads(scores, lse_ref[:, at], d_shares, delta_ref[:, at])
            dv = dot_nt(grad, shares)
            dk = dot_nt(query, d_scores)
            dq = dqs.get(tile, far_dq_ref[:, at])
            dqs[tile] = dq = dq + dot_nn(k_ref[:, key : key + count], d_scores)
            for offset in range(0, count, TILE):
                there = slice(key + offset, key + offset + TILE)
                here = slice(offset, offset + TILE)
                if key + offset in seen:
                    k_total[:, there] += dk[:, here]
                    v_total[:, there] += dv[:, here]
                else:
                    seen.add(key + offset)
                    k_total[:, there] = dk[:, here]
                    v_total[:, there] = dv[:, here]
            if last:
                dq_ref[:, at] = lowered(dq * gain_ref[...])
                product = jnp.sum(dq * query.astype(jnp.float32), axis=1, keepdims=True)
                scales[0] = scales[0] + product
                if tile == final:
                    dk_ref[...] = lowered(k_total[...] * LN_TWO)
                    dv_ref[...] = lowered(v_total[...])
                    scale_ref[...] = scales[0]

        items = []
        for tile, at in spans(q_ref):
            parts = key_parts(tile)
            items += [(tile, at, part, part is parts[-1]) for part in parts]
        return [(partial(begin, *item), partial(terms, *item)) for item in items]

    ahead([step for refs in heads for step in steps(*refs)])


def per_head(kernel, name, heads, area, products, ins, outs, after=(), scratch=()):
    group = 2 - heads % 2
    moved = sum(array.size * array.dtype.itemsize for _, array in ins)

    def spec(kind, shape):
        if kind == "rows":
            return pl.BlockSpec((group * HD, shape[1]), lambda step: (step, 0))
        if kind == "flat":
            return pl.BlockSpec((group, 1, shape[2]), lambda step: (step, 0, 0))
        if kind == "pair":
            return pl.BlockSpec((2, group * HD, shape[2]), lambda step: (0, step, 0))
        return pl.BlockSpec(shape, lambda step: (0, 0)) if kind == "same" else SCALAR

    def view(kind, ref, head):
        rows = pl.ds(head * HD, HD)
        if kind == "rows":
            return ref.at[rows]
        if kind == "flat":
            return ref.at[head]
        return ref.at[:, rows] if kind == "pair" else ref

    count = len(ins)
    kinds = [kind for kind, _ in ins] + [out[0] for out in outs] + ["rows"] * len(scratch)

    def work(*refs):
        refs = refs[:count] + refs[count + len(after) :]
        kernel(
            [[view(kind, ref, head) for kind, ref in zip(kinds, refs)] for head in range(group)]
        )

    return pl.pallas_call(
        work,
        grid=(heads // group,),
        in_specs=[spec(kind, array.shape) for kind, array in ins] + [UNREAD] * len(after),
        out_specs=[spec(kind, shape) for kind, shape, _ in outs],
        out_shape=[jax.ShapeDtypeStruct(shape, kind) for _, shape, kind in outs],
        scratch_shapes=[pltpu.VMEM((group * HD, tokens), jnp.float32) for tokens in scratch],
        compiler_params=pltpu.CompilerParams(vmem_limit_bytes=40 << 20),
        cost_estimate=pl.CostEstimate(
            flops=40 * area * heads * products,
            bytes_accessed=moved,
            transcendentals=area * heads,
        ),
        name=name,
    )(*[array for _, array in ins], *after)


def attention_own(start, queries, keys, values, after):
    width, tokens = queries.shape
    heads = width // HD
    flat = ("flat", (heads, 1, tokens), jnp.float32)
    return per_head(
        own_forward,
        "attention_own",
        heads,
        tokens * tokens * 5 // 8,
        3,
        [("same", start), ("rows", queries), ("rows", keys), ("rows", values)],
        [("rows", (width, tokens), jnp.float32), flat, flat],
        after,
    )


def attention_far(side, queries, keys, values, partial_sum, top, total, after):
    width, tokens = queries.shape
    heads = width // HD
    return per_head(
        far_forward,
        "attention_far",
        heads,
        tokens * PROMPT_DEV,
        2,
        [
            ("scalar", side),
            ("rows", queries),
            ("rows", keys),
            ("rows", values),
            ("rows", partial_sum),
            ("flat", top),
            ("flat", total),
        ],
        [
            ("rows", (width, tokens), jnp.bfloat16),
            ("flat", (heads, 1, tokens), jnp.float32),
        ],
        after,
    )


def attention_far_back(side, queries, keys, values, mixed, grads, lse, after):
    width, tokens = queries.shape
    heads = width // HD
    return per_head(
        far_backward,
        "attention_far_back",
        heads,
        tokens * PROMPT_DEV,
        3,
        [
            ("scalar", side),
            ("rows", queries),
            ("rows", keys),
            ("rows", values),
            ("rows", mixed),
            ("rows", grads),
            ("flat", lse),
        ],
        [
            ("rows", (width, tokens), jnp.float32),
            ("flat", (heads, 1, tokens), jnp.float32),
            ("pair", (2, width, PROMPT_DEV), jnp.bfloat16),
        ],
        after,
    )


def attention_own_back(start, gain, queries, keys, values, grads, lse, delta, far_dq, after):
    width, tokens = queries.shape
    heads = width // HD
    return per_head(
        own_backward,
        "attention_own_back",
        heads,
        tokens * tokens * 5 // 8,
        76,
        [
            ("same", start),
            ("same", gain),
            ("rows", queries),
            ("rows", keys),
            ("rows", values),
            ("rows", grads),
            ("flat", lse),
            ("flat", delta),
            ("rows", far_dq),
        ],
        [
            ("rows", (width, tokens), jnp.bfloat16),
            ("rows", (width, tokens), jnp.bfloat16),
            ("rows", (width, tokens), jnp.bfloat16),
            ("rows", (width, 1), jnp.float32),
        ],
        after,
        (tokens, tokens),
    )


def segment_starts(lengths_row, tokens):
    place = jnp.arange(tokens, dtype=jnp.int32) - PROMPT_DEV
    bounds = jnp.cumsum(lengths_row)
    passed = jnp.where(place[:, None] >= bounds[None, :], bounds[None, :], 0)
    return (PROMPT_DEV + jnp.max(passed, axis=1))[None, :]


def body(
    inputs,
    cotangent,
    query_weight,
    key_weight,
    value_weight,
    output_weight,
    up_weight,
    down_weight,
    attention_gain,
    feed_gain,
    query_scale,
    cont_lengths,
):
    tokens = inputs.shape[0] * lax.axis_size("tensor")
    heads = query_weight.shape[2] // HD
    orders = exchange_orders(lax.axis_size("dp"))
    side = (lax.axis_index("dp") % 2).astype(jnp.int32)[None]
    start = segment_starts(cont_lengths[0], tokens)

    pairs = []
    for layer in range(LAYERS):
        pairs.append((key_weight[layer], value_weight[layer]))
        pairs.append((query_weight[layer], output_weight[layer].T))
        pairs.append((up_weight[layer], down_weight[layer].T))

    gather = Gather(pairs, orders)
    stored = []
    terms = [inputs.T]
    ready = ()
    grad = cotangent.T
    for layer in range(LAYERS):
        attn_gain = attention_gain[layer][:, None]
        ff_gain = feed_gain[layer][:, None]
        current, inverse_attn, low = norm(terms, attn_gain, ready)
        normed, came = gather_tokens(low)
        gather.tick(came)
        if layer == 0:
            far = far_part(normed)
            gather.tick(far)
            far_normed, came = gather_tokens(far)
            gather.tick(came)
            gather.tick(grad)
            wk, wv = gather.take()
            gather.tick()
        keys = lowered(dot_tn(wk, normed))
        values = lowered(dot_tn(wv, normed))
        gather.tick(keys, values)
        wq, wo = gather.take()
        gain_q = softplus(query_scale[layer]) * LOG_TWO_E / math.sqrt(HD)
        gain_rows = jnp.tile(gain_q, heads)[:, None]
        queries = lowered(dot_tn(wq, normed) * (gain_rows * LOG_TWO_E))
        own_sum, top, total = attention_own(start, queries, keys, values, ())
        if layer:
            far = far_part(normed)
            ready = gather.tick(top, far)
            far_normed, _ = gather_tokens(far)
        far_keys = lowered(dot_tn(wk, far_normed))
        far_values = lowered(dot_tn(wv, far_normed))
        if not layer:
            ready = gather.tick(top, far_keys, far_values)
        mixed, lse = attention_far(side, queries, far_keys, far_values, own_sum, top, total, ready)
        gather.tick(lse)
        (both,) = gather.take()
        terms = scatter_tokens(lambda rows: dot_nn(wo, rows), mixed)
        ups, downs = feed_parts(both)
        ready = gather.tick(terms[-1])
        middle, inverse_feed, feed = norm([current, *terms], ff_gain, ready)
        uppers = [dot_tn(w, feed) for w in ups]
        ready = gather.tick(*uppers)
        if layer + 1 < LAYERS:
            following = gather.take()
        hiddens = [lowered(upper * jax.nn.sigmoid(upper)) for upper in uppers]
        stored.append(
            (
                (current, inverse_attn, attn_gain, normed),
                (gain_q, queries, keys, values, far_keys, far_values, mixed, lse),
                (middle, inverse_feed, ff_gain, feed, uppers, hiddens),
                (wk, wv, wq, wo, ups, downs),
            )
        )
        terms = [middle, sum(dot_nn(w, hidden) for w, hidden in zip(downs, hiddens))]
        if layer + 1 < LAYERS:
            wk, wv = following
    current = terms[0] + terms[1]

    sums = Scatter(orders)
    small_grads = [None] * LAYERS
    grad_low = lowered(grad)
    for layer in reversed(range(LAYERS)):
        (
            (source, inverse_attn, attn_gain, normed),
            (gain_q, queries, keys, values, far_keys, far_values, mixed, lse),
            (middle, inverse_feed, ff_gain, feed, uppers, hiddens),
            (wk, wv, wq, wo, ups, downs),
        ) = stored[layer]
        d_uppers = []
        for w, upper in zip(downs, uppers):
            d_hidden = lowered(dot_tn(w, grad_low)).astype(jnp.float32)
            sigmoid = jax.nn.sigmoid(upper)
            d_uppers.append(lowered(d_hidden * (sigmoid * (1.0 + upper * (1.0 - sigmoid)))))
        d_feed = sum(dot_nn(w, d_upper) for w, d_upper in zip(ups, d_uppers))
        ready = sums.tick(d_feed)
        grad_middle, low, feed_gain_grad = norm_back(
            middle, inverse_feed, ff_gain, grad, [d_feed], ready
        )
        middle_low, came = gather_tokens(low)
        down_grad, down_came = feed_total([dot_nt(grad_low, hidden) for hidden in hiddens])
        up_grad, up_came = feed_total([dot_nt(feed, d_upper) for d_upper in d_uppers])
        if down_came is None:
            stepped = sums.tick(came, down_grad, up_grad)
            sums.push(down_grad, up_grad)
        else:
            stepped = sums.tick(came, down_came, up_came)
            sums.push(down_grad, up_grad, came=(down_came, up_came))
        d_mixed = lowered(dot_tn(wo, middle_low))
        out_grad = lowered(dot_nt(middle_low, mixed))
        ready = [*sums.enter(), *stepped]
        far_dq, delta, far_dkv = attention_far_back(
            side, queries, far_keys, far_values, mixed, d_mixed, lse, ready
        )
        back = pair_swap(far_dkv, "dp", 1)
        ready = sums.tick(delta)
        d_raw, own_dk, own_dv, scale_rows = attention_own_back(
            start,
            gain_q[:, None],
            queries,
            keys,
            values,
            d_mixed,
            lse,
            delta,
            far_dq,
            ready,
        )
        ready = sums.tick(scale_rows)
        query_grad = lowered(dot_nt(normed, d_raw))
        sums.push(out_grad, query_grad)
        ready = [*ready, *sums.enter()]
        d_keys, d_values = add_back(own_dk, own_dv, back, ready)
        scale_raw = jnp.sum(scale_rows.reshape(heads, HD), 0) / (gain_q * LOG_TWO_E)
        scale_grad = scale_raw * jax.nn.sigmoid(query_scale[layer]) * LOG_TWO_E / math.sqrt(HD)
        if not layer:
            key_grad, value_grad = [lowered(dot_nt(normed, d)) for d in (d_keys, d_values)]
            ready = sums.tick(key_grad, value_grad)
            last = Scatter(orders)
            last.push(key_grad, value_grad)
            last.enter()
        terms = scatter_tokens(
            lambda dq, dk, dv: dot_nn(wq, dq) + dot_nn(wk, dk) + dot_nn(wv, dv),
            d_raw,
            d_keys,
            d_values,
        )
        if layer:
            ready = sums.tick(terms[-1])
        else:
            sums.tick(terms[-1])
            ready = last.tick(terms[-1])
        grad, grad_low, attn_gain_grad = norm_back(
            source, inverse_attn, attn_gain, grad_middle, terms, ready
        )
        if layer:
            key_grad, value_grad = [lowered(dot_nt(normed, d)) for d in (d_keys, d_values)]
            sums.push(key_grad, value_grad)
            sums.tick(grad, key_grad, value_grad)
        small_grads[layer] = jnp.concatenate([attn_gain_grad, feed_gain_grad, scale_grad])
    small = jnp.stack(small_grads)
    for axis, bits in (("tensor", 1), ("dp", 2)):
        bit = 1
        while bit < lax.axis_size(axis):
            small, bit = exchange_sum(small, axis, bit, bits, last), bit << bits
    done = sums.finish() + last.finish()
    layer_grads = []
    for layer in range(LAYERS):
        at = 3 * (LAYERS - 1 - layer)
        (down_grad, up_grad), (out_grad, query_grad), (key_grad, value_grad) = done[at : at + 3]
        layer_grads.append(
            (query_grad, key_grad, value_grad, out_grad.T, up_grad, down_grad.T)
        )

    summed = [jnp.stack(members) for members in zip(*layer_grads)]
    width = current.shape[0]
    return (
        current.T,
        grad.T,
        *summed,
        small[:, :width],
        small[:, width : 2 * width],
        small[:, 2 * width :],
    )


def solution(mesh):
    in_specs = (
        P(("dp", "tensor"), None),
        P(("dp", "tensor"), None),
        P(None, "dp", "tensor"),
        P(None, "dp", "tensor"),
        P(None, "dp", "tensor"),
        P(None, "tensor", "dp"),
        P(None, "dp", "tensor"),
        P(None, "tensor", "dp"),
        P(),
        P(),
        P(),
        P("dp", None),
    )
    out_specs = (
        P(("dp", "tensor"), None),
        P(("dp", "tensor"), None),
        P(None, "dp", "tensor"),
        P(None, "dp", "tensor"),
        P(None, "dp", "tensor"),
        P(None, "tensor", "dp"),
        P(None, "dp", "tensor"),
        P(None, "tensor", "dp"),
        P(),
        P(),
        P(),
    )
    return jax.shard_map(body, mesh=mesh, in_specs=in_specs, out_specs=out_specs, check_vma=False)
```

```python
from functools import partial
import math

import jax
import jax.numpy as jnp
from jax import lax
from jax.experimental.layout import Layout, with_layout_constraint
from jax.experimental import pallas as pl
from jax.experimental.pallas import tpu as pltpu
from jax.sharding import PartitionSpec as P

HD = 80
LAYERS = 2
PROMPT_DEV = 512
TILE = 256

EPSILON = 1e-06
LOG_TWO_E = 1.4426950408889634
LN_TWO = 0.6931471805599453
NEGATIVE = -1e30


def lowered(values):
    return values.astype(jnp.bfloat16)


def dot_nn(former, latter):
    return jnp.dot(former, latter, preferred_element_type=jnp.float32)


def dot_tn(former, latter):
    return lax.dot_general(
        former, latter, (((0,), (0,)), ((), ())), preferred_element_type=jnp.float32
    )


def dot_nt(former, latter):
    return lax.dot_general(
        former, latter, (((1,), (1,)), ((), ())), preferred_element_type=jnp.float32
    )


def softplus(values):
    return jnp.log1p(jnp.exp(values))


def pair_swap(values, axis, bit):
    size = lax.axis_size(axis)
    return lax.ppermute(values, axis, [(i, i ^ bit) for i in range(size)])


def exchange_orders(size):
    if size == 16:
        return (8, 4), ((2, 1), (1, 2))
    bits = tuple(1 << k for k in reversed(range(size.bit_length() - 1)))
    first, rest = bits[:1], bits[1:]
    half = len(rest) // 2
    return first, (rest, rest[half:] + rest[:half])


WHOLE = pl.BlockSpec(memory_space=pltpu.VMEM)
SCALAR = pl.BlockSpec(memory_space=pltpu.SMEM)
UNREAD = pl.BlockSpec(memory_space=pl.ANY)


def dp_bits(bits):
    place = lax.axis_index("dp")
    return jnp.stack([((place & bit) != 0).astype(jnp.int32) for bit in bits])


def quick_call(kernel, name, arrays, after, out_shape):
    out = pl.pallas_call(
        kernel,
        in_specs=[SCALAR] + [WHOLE] * (len(arrays) - 1) + [UNREAD] * len(after),
        out_specs=[WHOLE] * len(out_shape),
        out_shape=out_shape,
        compiler_params=pltpu.CompilerParams(vmem_limit_bytes=48 << 20),
        cost_estimate=pl.CostEstimate(flops=1, bytes_accessed=1, transcendentals=0),
        name=name,
    )(*arrays, *after)
    return list(out)


class Gather:
    def __init__(self, pairs, orders):
        self.first, self.rest = orders
        self.queue = [jnp.stack(pair)[:, None] for pair in pairs]
        self.left = len(pairs)
        self.early, self.early_at = None, 0
        self.late, self.late_at = None, 0
        self.ready = []

    def tick(self, *after):
        if self.early is None and self.queue:
            self.early, self.early_at = self.queue.pop(0), 0
        if self.late is None and self.early is not None and self.early_at == len(self.first):
            self.late, self.late_at = self.early, 0
            self.early, self.early_at = (self.queue.pop(0), 0) if self.queue else (None, 0)
        jobs = []
        early = self.early is not None and self.early_at < len(self.first)
        if early:
            jobs.append((self.early, self.first[: self.early_at + 1]))
        if self.late is not None:
            for values, order in zip(self.late, self.rest):
                jobs.append((values, self.first + order[: self.late_at + 1]))
        if not jobs:
            return []
        got = [pair_swap(values, "dp", done[-1]) for values, done in jobs]
        plans, shapes = [], []
        for values, done in jobs:
            members, blocks, rows, width = values.shape
            before = 1 << sum(1 for bit in done[:-1] if bit > done[-1])
            parts = members if members > 1 and len(done) == len(self.first) else 1
            plans.append((members, before, blocks // before, parts, len(shapes)))
            shapes += [(members // parts, 2 * blocks, rows, width)] * parts
        count = len(jobs)
        merged = self.late is not None and self.merges() and (
            self.late_at + 1 == len(self.rest[0])
        )
        if merged:
            at = plans[-2][-1]
            shapes[at:] = [(2,) + shapes[at][1:]]
        following = self.queue[:1]

        def join(bit_ref, *refs):
            outs = refs[len(refs) - len(shapes) - len(following) :]
            if following:
                outs[-1][...] = refs[2 * count][...]
            for job, (members, before, blocks, parts, at) in enumerate(plans):
                bit = bit_ref[job]
                for member in range(members):
                    if merged and job == count - 1:
                        out, row = outs[at - 1], 1
                    elif parts > 1:
                        out, row = outs[at + member], 0
                    else:
                        out, row = outs[at], member
                    for step in range(before):
                        here = pl.ds(step * blocks, blocks)
                        place = 2 * step * blocks
                        ours, theirs = place + bit * blocks, place + (1 - bit) * blocks
                        out[row, pl.ds(ours, blocks)] = refs[job][member, here]
                        out[row, pl.ds(theirs, blocks)] = refs[count + job][member, here]

        outs = quick_call(
            join,
            "join_halves",
            [
                dp_bits([done[-1] for _, done in jobs]),
                *[values for values, _ in jobs],
                *got,
                *following,
            ],
            after,
            [
                jax.ShapeDtypeStruct(shape, jnp.bfloat16)
                for shape in shapes + [values.shape for values in following]
            ],
        )
        if following:
            self.queue[0] = outs.pop()
        if early:
            self.early_at += 1
            done = self.early_at == len(self.first)
            self.early = outs[:2] if done else outs[0]
        if self.late is not None:
            self.late, self.late_at = outs[-1:] if merged else outs[-2:], self.late_at + 1
            if self.late_at == len(self.rest[0]):
                width = self.late[0].shape[-1]
                shape = (2, -1, width) if merged else (-1, width)
                self.ready.append([values.reshape(shape) for values in self.late])
                self.late = None
                self.left -= 1
        return outs

    def merges(self):
        return self.left % 3 == 1

    def take(self):
        while not self.ready:
            self.tick()
        return self.ready.pop(0)


class Scatter:
    def __init__(self, orders):
        self.first, self.rest = orders
        self.bits = sorted(self.first + self.rest[0], reverse=True)
        self.queue, self.late, self.early, self.done = [], None, None, []

    def push(self, *pair, came=(None, None)):
        rows = pair[0].shape[0] >> len(self.bits)
        shape = (1, 1 << len(self.bits), rows, pair[0].shape[1])
        self.queue.append(
            [
                ([values.reshape(shape)], None if more is None else [more.reshape(shape)], order)
                for values, more, order in zip(pair, came, self.rest)
            ]
        )

    def run(self, jobs, after):
        plans, ins, shapes, bits = [], [], [], []
        for held, got, left, bit, joined in jobs:
            blocks, rows, width = held[0].shape[1:]
            members = sum(values.shape[0] for values in held)
            at = left.index(bit) if bit else 0
            behind = blocks // 2 >> at if bit else blocks
            plans.append((len(held), len(ins), bool(got), 1 << at, behind, bit, joined, len(shapes)))
            ins += held + (got or [])
            bits.append(bit or 1)
            if bit:
                groups = 1 if joined else members
                shapes += [((members // groups, blocks // 2, rows, width), jnp.bfloat16)] * (
                    2 * groups
                )
            else:
                shapes += [((rows, width), jnp.float32)] * members
        inputs = len(ins)

        def add(bit_ref, *refs):
            sources, outs = refs[:inputs], refs[len(refs) - len(shapes) :]
            for job, (arrays, at, come, before, behind, bit, joined, out_at) in enumerate(plans):
                mine = bit_ref[job]
                member = 0
                for array in range(arrays):
                    held = sources[at + array]
                    for row in range(held.shape[0]):

                        def total(start):
                            values = held[row, pl.ds(start, behind)]
                            if come:
                                other = sources[at + arrays + array][row, pl.ds(start, behind)]
                                values = values.astype(jnp.float32) + other.astype(jnp.float32)
                            return values

                        if bit is None:
                            outs[out_at + member][...] = total(0)[0]
                        else:
                            keep, send, place = (
                                (outs[out_at], outs[out_at + 1], member)
                                if joined
                                else (outs[out_at + 2 * member], outs[out_at + 2 * member + 1], 0)
                            )
                            for step in range(before):
                                start = 2 * step * behind
                                there = pl.ds(step * behind, behind)
                                keep[place, there] = lowered(total(start + mine * behind))
                                send[place, there] = lowered(total(start + (1 - mine) * behind))
                        member += 1

        return quick_call(
            add,
            "add_halves",
            [dp_bits(bits), *ins],
            after,
            [jax.ShapeDtypeStruct(shape, kind) for shape, kind in shapes],
        )

    def enter(self):
        if self.late is not None or not self.queue:
            return []
        jobs = [
            (held, came, self.bits, order[-1], False) for held, came, order in self.queue.pop(0)
        ]
        outs = self.run(jobs, ())
        self.late = (outs[0::2], outs[1::2], 1)
        return outs

    def tick(self, *after):
        self.enter()
        jobs, steps = [], len(self.rest[0])
        if self.early is not None:
            keep, send, at = self.early
            bits = self.first[: len(self.first) - at + 1]
            left = sorted(bits[:-1], reverse=True)
            got = [pair_swap(send, "dp", bits[-1])]
            jobs.append(([keep], got, left, bits[-2] if left else None, True))
        if self.late is not None:
            keeps, sends, at = self.late
            got = [
                pair_swap(send, "dp", order[steps - at]) for send, order in zip(sends, self.rest)
            ]
            for keep, come, order in zip(keeps, got, self.rest):
                left = sorted(self.first + order[: steps - at], reverse=True)
                if at < steps:
                    jobs.append(([keep], [come], left, order[steps - at - 1], False))
            if at == steps:
                jobs.append((keeps, got, left, self.first[-1], True))
        if not jobs:
            return []
        outs = self.run(jobs, after)
        rest = outs
        if self.early is not None:
            if at_end(self.early[2], self.first):
                self.done.append(rest[:2])
                self.early = None
            else:
                self.early = (rest[0], rest[1], self.early[2] + 1)
            rest = rest[2:]
        if self.late is not None:
            if self.late[2] == steps:
                self.early, self.late = (rest[0], rest[1], 1), None
            else:
                self.late = (rest[0::2], rest[1::2], self.late[2] + 1)
        return outs

    def finish(self):
        while self.queue or self.late or self.early:
            self.tick()
        return self.done


def at_end(step, bits):
    return step == len(bits)


def gather_tokens(local):
    if lax.axis_size("tensor") != 2:
        values = lax.all_gather(local, "tensor", axis=1, tiled=True)
        return values, values
    other = pair_swap(local, "tensor", 1)
    upper = lax.axis_index("tensor") != 0
    values = [jnp.where(upper, other, local), jnp.where(upper, local, other)]
    return jnp.concatenate(values, axis=1), other


def far_part(normed):
    part = PROMPT_DEV // lax.axis_size("tensor")
    place = lax.axis_index("tensor") * part
    return pair_swap(lax.dynamic_slice_in_dim(normed, place, part, 1), "dp", 1)


def scatter_tokens(product, *values):
    if lax.axis_size("tensor") != 2:
        return [
            lax.psum_scatter(
                lowered(product(*values)), "tensor", scatter_dimension=1, tiled=True
            )
        ]
    count = values[0].shape[1] // 2
    place = lax.axis_index("tensor")
    theirs = [lax.dynamic_slice_in_dim(v, (1 - place) * count, count, 1) for v in values]
    got = pair_swap(lowered(product(*theirs)), "tensor", 1)
    mine = [lax.dynamic_slice_in_dim(v, place * count, count, 1) for v in values]
    return [lowered(product(*mine)), got]


def feed_parts(both):
    if lax.axis_size("tensor") != 2:
        whole = lax.all_gather(both, "tensor", axis=2, tiled=True)
        return [whole[0]], [whole[1]]
    other = pair_swap(both, "tensor", 1)
    return [both[0], other[0]], [both[1], other[1]]


def feed_total(parts):
    if lax.axis_size("tensor") != 2:
        whole = lax.psum_scatter(lowered(parts[0]), "tensor", scatter_dimension=1, tiled=True)
        return whole, None
    mine, theirs = [with_layout_constraint(lowered(part), Layout((0, 1))) for part in parts]
    return mine, pair_swap(theirs, "tensor", 1)


def exchange_sum(values, axis, bit, bits, exchange):
    wide = bits == 2 and 2 * bit < lax.axis_size(axis)
    came = [pair_swap(values, axis, bit * by) for by in ((1, 2, 3) if wide else (1,))]
    after = exchange.tick(*came)
    total = values + came[0]
    if wide:
        total = total + (came[1] + came[2])
    return tied(total, after)


def tied(gain, after):
    if not after:
        return gain
    corner = after[0][(0,) * after[0].ndim].astype(jnp.float32)
    return gain + jnp.minimum((corner > 3e38).astype(jnp.int32), 0).astype(jnp.float32)


def norm(terms, gain, after=()):
    total = sum(term.astype(jnp.float32) for term in terms)
    inverse = lax.rsqrt(jnp.mean(total * total, axis=0, keepdims=True) + EPSILON)
    return total, inverse, lowered(total * inverse * tied(gain, after))


def norm_back(source, inverse, gain, grad, terms, after=()):
    incoming = sum(term.astype(jnp.float32) for term in terms)
    if len(terms) > 1:
        incoming = lax.optimization_barrier(lowered(incoming)).astype(jnp.float32)
    unit = source * inverse
    gain_grad = jnp.sum(incoming * unit, axis=1)
    scaled = incoming * tied(gain, after)
    total = grad + inverse * (scaled - unit * jnp.mean(scaled * unit, axis=0, keepdims=True))
    return total, lowered(total), gain_grad


def first_slot(_):
    return jnp.zeros((1,), jnp.int32)


def add_back(own_keys, own_values, back, after):
    def kernel(_, keys_ref, values_ref, back_ref, *refs):
        for place, (ref, out) in enumerate(zip((keys_ref, values_ref), refs[-2:])):
            prompt = ref[:, :PROMPT_DEV].astype(jnp.float32) + back_ref[place].astype(jnp.float32)
            out[:, :PROMPT_DEV] = lowered(prompt)
            out[:, PROMPT_DEV:] = ref[:, PROMPT_DEV:]

    out = [jax.ShapeDtypeStruct(own_keys.shape, jnp.bfloat16)] * 2
    arrays = [first_slot(back), own_keys, own_values, back]
    return quick_call(kernel, "add_back", arrays, after, out)


def key_parts(tile):
    first = tile * TILE
    if first < PROMPT_DEV:
        return ([(0, first, "free")] if first else []) + [(first, TILE, "earlier")]
    return [(0, PROMPT_DEV, "free"), (PROMPT_DEV, first - PROMPT_DEV + TILE, "segment")]


def masked(scores, kind, first_key, first_query, start):
    if kind == "free":
        return scores
    key = lax.broadcasted_iota(jnp.int32, scores.shape, 0) + first_key
    query = lax.broadcasted_iota(jnp.int32, scores.shape, 1) + first_query
    allowed = key <= query
    if kind == "segment":
        allowed = allowed & (key >= start)
    return jnp.where(allowed, scores, NEGATIVE)


def spans(reference):
    tokens = reference.shape[1]
    return [(tile, slice(tile * TILE, tile * TILE + TILE)) for tile in range(tokens // TILE)]


def ahead(steps):
    held = steps[0][0]()
    for place, (_, second) in enumerate(steps):
        following = steps[place + 1][0]() if place + 1 < len(steps) else None
        second(held)
        held = following


def own_forward(heads):
    def steps(start_ref, q_ref, k_ref, v_ref, sum_ref, top_ref, total_ref):
        keys = k_ref[...].T

        def scores_of(tile, at):
            query, start = q_ref[:, at], start_ref[:, at]
            return [
                masked(dot_nn(keys[key : key + count], query), kind, key, tile * TILE, start)
                for key, count, kind in key_parts(tile)
            ]

        def mix(tile, at, parts):
            highest = jnp.max(parts[0], axis=0, keepdims=True)
            for scores in parts[1:]:
                highest = jnp.maximum(highest, jnp.max(scores, axis=0, keepdims=True))
            total, mixed = 0.0, 0.0
            for scores, (key, count, _) in zip(parts, key_parts(tile)):
                weights = jnp.exp2(scores - highest)
                total = total + jnp.sum(weights, axis=0, keepdims=True)
                mixed = mixed + dot_nn(v_ref[:, key : key + count], lowered(weights))
            sum_ref[:, at] = mixed
            top_ref[:, at] = highest
            total_ref[:, at] = total

        return [(partial(scores_of, *item), partial(mix, *item)) for item in spans(q_ref)]

    ahead([step for refs in heads for step in steps(*refs)])


def sides(side_ref, q_ref, run):
    tiles = [at for _, at in spans(q_ref)]
    conts = [at for tile, at in spans(q_ref) if tile * TILE >= PROMPT_DEV]

    @pl.when(side_ref[0] == 0)
    def _():
        run(conts, [at for at in tiles if at not in conts])

    @pl.when(side_ref[0] != 0)
    def _():
        run(tiles, [])


def far_forward(heads):
    def steps(tiles, _, q_ref, k_ref, v_ref, sum_ref, top_ref, total_ref, out_ref, lse_ref):
        keys = k_ref[...].T

        def scores_of(at):
            return dot_nn(keys, q_ref[:, at])

        def mix(at, scores):
            highest = jnp.maximum(top_ref[:, at], jnp.max(scores, axis=0, keepdims=True))
            weights = jnp.exp2(scores - highest)
            scale = jnp.exp2(top_ref[:, at] - highest)
            total = total_ref[:, at] * scale + jnp.sum(weights, axis=0, keepdims=True)
            mixed = sum_ref[:, at] * scale + dot_nn(v_ref[...], lowered(weights))
            out_ref[:, at] = lowered(mixed / total)
            lse_ref[:, at] = highest + jnp.log2(total)

        return [(partial(scores_of, at), partial(mix, at)) for at in tiles]

    def run(tiles, others):
        for _, _, _, _, sum_ref, top_ref, total_ref, out_ref, lse_ref in heads:
            for at in others:
                out_ref[:, at] = lowered(sum_ref[:, at] / total_ref[:, at])
                lse_ref[:, at] = top_ref[:, at] + jnp.log2(total_ref[:, at])
        ahead([step for refs in heads for step in steps(tiles, *refs)])

    sides(heads[0][0], heads[0][1], run)


def score_grads(scores, lse, d_shares, delta):
    shares = jnp.exp2(scores - lse)
    return lowered(shares), lowered(shares * (d_shares - delta))


def far_backward(heads):
    def steps(
        tiles, _, q_ref, k_ref, v_ref, out_ref, grad_ref, lse_ref, dq_ref, delta_ref, dkv_ref
    ):
        keys, values = k_ref[...].T, v_ref[...].T
        delta_ref[...] = jnp.sum(
            out_ref[...].astype(jnp.float32) * grad_ref[...].astype(jnp.float32),
            axis=0,
            keepdims=True,
        )
        sums = [0.0, 0.0]

        def begin(at):
            return dot_nn(keys, q_ref[:, at]), dot_nn(values, grad_ref[:, at])

        def terms(at, held):
            scores, d_shares = held
            shares, d_scores = score_grads(scores, lse_ref[:, at], d_shares, delta_ref[:, at])
            dq_ref[:, at] = dot_nn(k_ref[...], d_scores)
            sums[0] = sums[0] + dot_nt(q_ref[:, at], d_scores)
            sums[1] = sums[1] + dot_nt(grad_ref[:, at], shares)
            if at is tiles[-1]:
                dkv_ref[0] = lowered(sums[0] * LN_TWO)
                dkv_ref[1] = lowered(sums[1])

        return [(partial(begin, at), partial(terms, at)) for at in tiles]

    def run(tiles, others):
        for refs in heads:
            for at in others:
                refs[7][:, at] = jnp.zeros_like(refs[7][:, at])
        ahead([step for refs in heads for step in steps(tiles, *refs)])

    sides(heads[0][0], heads[0][1], run)


def own_backward(heads):
    def steps(
        start_ref,
        gain_ref,
        q_ref,
        k_ref,
        v_ref,
        grad_ref,
        lse_ref,
        delta_ref,
        far_dq_ref,
        dq_ref,
        dk_ref,
        dv_ref,
        scale_ref,
        k_total,
        v_total,
    ):
        keys, values = k_ref[...].T, v_ref[...].T
        seen, dqs, scales = set(), {}, [0.0]
        final = spans(q_ref)[-1][0]

        def begin(tile, at, part, last):
            key, count, kind = part
            scores = dot_nn(keys[key : key + count], q_ref[:, at])
            scores = masked(scores, kind, key, tile * TILE, start_ref[:, at])
            return scores, dot_nn(values[key : key + count], grad_ref[:, at])

        def terms(tile, at, part, last, held):
            key, count, _ = part
            scores, d_shares = held
            query, grad = q_ref[:, at], grad_ref[:, at]
            shares, d_scores = score_grads(scores, lse_ref[:, at], d_shares, delta_ref[:, at])
            dv = dot_nt(grad, shares)
            dk = dot_nt(query, d_scores)
            dq = dqs.get(tile, far_dq_ref[:, at])
            dqs[tile] = dq = dq + dot_nn(k_ref[:, key : key + count], d_scores)
            for offset in range(0, count, TILE):
                there = slice(key + offset, key + offset + TILE)
                here = slice(offset, offset + TILE)
                if key + offset in seen:
                    k_total[:, there] += dk[:, here]
                    v_total[:, there] += dv[:, here]
                else:
                    seen.add(key + offset)
                    k_total[:, there] = dk[:, here]
                    v_total[:, there] = dv[:, here]
            if last:
                dq_ref[:, at] = lowered(dq * gain_ref[...])
                product = jnp.sum(dq * query.astype(jnp.float32), axis=1, keepdims=True)
                scales[0] = scales[0] + product
                if tile == final:
                    dk_ref[...] = lowered(k_total[...] * LN_TWO)
                    dv_ref[...] = lowered(v_total[...])
                    scale_ref[...] = scales[0]

        items = []
        for tile, at in spans(q_ref):
            parts = key_parts(tile)
            items += [(tile, at, part, part is parts[-1]) for part in parts]
        return [(partial(begin, *item), partial(terms, *item)) for item in items]

    ahead([step for refs in heads for step in steps(*refs)])


def per_head(kernel, name, heads, area, products, ins, outs, after=(), scratch=()):
    group = 2 - heads % 2
    moved = sum(array.size * array.dtype.itemsize for _, array in ins)

    def spec(kind, shape):
        if kind == "rows":
            return pl.BlockSpec((group * HD, shape[1]), lambda step: (step, 0))
        if kind == "flat":
            return pl.BlockSpec((group, 1, shape[2]), lambda step: (step, 0, 0))
        if kind == "pair":
            return pl.BlockSpec((2, group * HD, shape[2]), lambda step: (0, step, 0))
        return pl.BlockSpec(shape, lambda step: (0, 0)) if kind == "same" else SCALAR

    def view(kind, ref, head):
        rows = pl.ds(head * HD, HD)
        if kind == "rows":
            return ref.at[rows]
        if kind == "flat":
            return ref.at[head]
        return ref.at[:, rows] if kind == "pair" else ref

    count = len(ins)
    kinds = [kind for kind, _ in ins] + [out[0] for out in outs] + ["rows"] * len(scratch)

    def work(*refs):
        refs = refs[:count] + refs[count + len(after) :]
        kernel(
            [[view(kind, ref, head) for kind, ref in zip(kinds, refs)] for head in range(group)]
        )

    return pl.pallas_call(
        work,
        grid=(heads // group,),
        in_specs=[spec(kind, array.shape) for kind, array in ins] + [UNREAD] * len(after),
        out_specs=[spec(kind, shape) for kind, shape, _ in outs],
        out_shape=[jax.ShapeDtypeStruct(shape, kind) for _, shape, kind in outs],
        scratch_shapes=[pltpu.VMEM((group * HD, tokens), jnp.float32) for tokens in scratch],
        compiler_params=pltpu.CompilerParams(vmem_limit_bytes=40 << 20),
        cost_estimate=pl.CostEstimate(
            flops=40 * area * heads * products,
            bytes_accessed=moved,
            transcendentals=area * heads,
        ),
        name=name,
    )(*[array for _, array in ins], *after)


def attention_own(start, queries, keys, values, after):
    width, tokens = queries.shape
    heads = width // HD
    flat = ("flat", (heads, 1, tokens), jnp.float32)
    return per_head(
        own_forward,
        "attention_own",
        heads,
        tokens * tokens * 5 // 8,
        3,
        [("same", start), ("rows", queries), ("rows", keys), ("rows", values)],
        [("rows", (width, tokens), jnp.float32), flat, flat],
        after,
    )


def attention_far(side, queries, keys, values, partial_sum, top, total, after):
    width, tokens = queries.shape
    heads = width // HD
    return per_head(
        far_forward,
        "attention_far",
        heads,
        tokens * PROMPT_DEV,
        2,
        [
            ("scalar", side),
            ("rows", queries),
            ("rows", keys),
            ("rows", values),
            ("rows", partial_sum),
            ("flat", top),
            ("flat", total),
        ],
        [
            ("rows", (width, tokens), jnp.bfloat16),
            ("flat", (heads, 1, tokens), jnp.float32),
        ],
        after,
    )


def attention_far_back(side, queries, keys, values, mixed, grads, lse, after):
    width, tokens = queries.shape
    heads = width // HD
    return per_head(
        far_backward,
        "attention_far_back",
        heads,
        tokens * PROMPT_DEV,
        3,
        [
            ("scalar", side),
            ("rows", queries),
            ("rows", keys),
            ("rows", values),
            ("rows", mixed),
            ("rows", grads),
            ("flat", lse),
        ],
        [
            ("rows", (width, tokens), jnp.float32),
            ("flat", (heads, 1, tokens), jnp.float32),
            ("pair", (2, width, PROMPT_DEV), jnp.bfloat16),
        ],
        after,
    )


def attention_own_back(start, gain, queries, keys, values, grads, lse, delta, far_dq, after):
    width, tokens = queries.shape
    heads = width // HD
    return per_head(
        own_backward,
        "attention_own_back",
        heads,
        tokens * tokens * 5 // 8,
        76,
        [
            ("same", start),
            ("same", gain),
            ("rows", queries),
            ("rows", keys),
            ("rows", values),
            ("rows", grads),
            ("flat", lse),
            ("flat", delta),
            ("rows", far_dq),
        ],
        [
            ("rows", (width, tokens), jnp.bfloat16),
            ("rows", (width, tokens), jnp.bfloat16),
            ("rows", (width, tokens), jnp.bfloat16),
            ("rows", (width, 1), jnp.float32),
        ],
        after,
        (tokens, tokens),
    )


def segment_starts(lengths_row, tokens):
    place = jnp.arange(tokens, dtype=jnp.int32) - PROMPT_DEV
    bounds = jnp.cumsum(lengths_row)
    passed = jnp.where(place[:, None] >= bounds[None, :], bounds[None, :], 0)
    return (PROMPT_DEV + jnp.max(passed, axis=1))[None, :]


def body(
    inputs,
    cotangent,
    query_weight,
    key_weight,
    value_weight,
    output_weight,
    up_weight,
    down_weight,
    attention_gain,
    feed_gain,
    query_scale,
    cont_lengths,
):
    tokens = inputs.shape[0] * lax.axis_size("tensor")
    heads = query_weight.shape[2] // HD
    orders = exchange_orders(lax.axis_size("dp"))
    side = (lax.axis_index("dp") % 2).astype(jnp.int32)[None]
    start = segment_starts(cont_lengths[0], tokens)

    pairs = []
    for layer in range(LAYERS):
        pairs.append((key_weight[layer], value_weight[layer]))
        pairs.append((query_weight[layer], output_weight[layer].T))
        pairs.append((up_weight[layer], down_weight[layer].T))

    gather = Gather(pairs, orders)
    stored = []
    terms = [inputs.T]
    ready = ()
    grad = cotangent.T
    for layer in range(LAYERS):
        attn_gain = attention_gain[layer][:, None]
        ff_gain = feed_gain[layer][:, None]
        current, inverse_attn, low = norm(terms, attn_gain, ready)
        normed, came = gather_tokens(low)
        gather.tick(came)
        if layer == 0:
            far = far_part(normed)
            gather.tick(far)
            far_normed, came = gather_tokens(far)
            gather.tick(came)
            gather.tick(grad)
            wk, wv = gather.take()
            gather.tick()
        keys = lowered(dot_tn(wk, normed))
        values = lowered(dot_tn(wv, normed))
        gather.tick(keys, values)
        wq, wo = gather.take()
        gain_q = softplus(query_scale[layer]) * LOG_TWO_E / math.sqrt(HD)
        gain_rows = jnp.tile(gain_q, heads)[:, None]
        queries = lowered(dot_tn(wq, normed) * (gain_rows * LOG_TWO_E))
        own_sum, top, total = attention_own(start, queries, keys, values, ())
        if layer:
            far = far_part(normed)
            ready = gather.tick(top, far)
            far_normed, _ = gather_tokens(far)
        far_keys = lowered(dot_tn(wk, far_normed))
        far_values = lowered(dot_tn(wv, far_normed))
        if not layer:
            ready = gather.tick(top, far_keys, far_values)
        mixed, lse = attention_far(side, queries, far_keys, far_values, own_sum, top, total, ready)
        gather.tick(lse)
        (both,) = gather.take()
        terms = scatter_tokens(lambda rows: dot_nn(wo, rows), mixed)
        ups, downs = feed_parts(both)
        ready = gather.tick(terms[-1])
        middle, inverse_feed, feed = norm([current, *terms], ff_gain, ready)
        uppers = [dot_tn(w, feed) for w in ups]
        ready = gather.tick(*uppers)
        if layer + 1 < LAYERS:
            following = gather.take()
        hiddens = [lowered(upper * jax.nn.sigmoid(upper)) for upper in uppers]
        stored.append(
            (
                (current, inverse_attn, attn_gain, normed),
                (gain_q, queries, keys, values, far_keys, far_values, mixed, lse),
                (middle, inverse_feed, ff_gain, feed, uppers, hiddens),
                (wk, wv, wq, wo, ups, downs),
            )
        )
        if layer + 1 < LAYERS:
            terms = [middle, sum(dot_nn(w, hidden) for w, hidden in zip(downs, hiddens))]
            wk, wv = following
    final = (middle, downs, hiddens)

    sums = Scatter(orders)
    small_grads = [None] * LAYERS
    grad_low = lowered(grad)
    for layer in reversed(range(LAYERS)):
        (
            (source, inverse_attn, attn_gain, normed),
            (gain_q, queries, keys, values, far_keys, far_values, mixed, lse),
            (middle, inverse_feed, ff_gain, feed, uppers, hiddens),
            (wk, wv, wq, wo, ups, downs),
        ) = stored[layer]
        d_uppers = []
        for w, upper in zip(downs, uppers):
            d_hidden = lowered(dot_tn(w, grad_low)).astype(jnp.float32)
            sigmoid = jax.nn.sigmoid(upper)
            d_uppers.append(lowered(d_hidden * (sigmoid * (1.0 + upper * (1.0 - sigmoid)))))
        d_feed = sum(dot_nn(w, d_upper) for w, d_upper in zip(ups, d_uppers))
        ready = sums.tick(d_feed)
        grad_middle, low, feed_gain_grad = norm_back(
            middle, inverse_feed, ff_gain, grad, [d_feed], ready
        )
        middle_low, came = gather_tokens(low)
        down_grad, down_came = feed_total([dot_nt(grad_low, hidden) for hidden in hiddens])
        up_grad, up_came = feed_total([dot_nt(feed, d_upper) for d_upper in d_uppers])
        if down_came is None:
            stepped = sums.tick(came, down_grad, up_grad)
            sums.push(down_grad, up_grad)
        else:
            stepped = sums.tick(came, down_came, up_came)
            sums.push(down_grad, up_grad, came=(down_came, up_came))
        d_mixed = lowered(dot_tn(wo, middle_low))
        out_grad = lowered(dot_nt(middle_low, mixed))
        ready = [*sums.enter(), *stepped]
        far_dq, delta, far_dkv = attention_far_back(
            side, queries, far_keys, far_values, mixed, d_mixed, lse, ready
        )
        back = pair_swap(far_dkv, "dp", 1)
        ready = sums.tick(delta)
        d_raw, own_dk, own_dv, scale_rows = attention_own_back(
            start,
            gain_q[:, None],
            queries,
            keys,
            values,
            d_mixed,
            lse,
            delta,
            far_dq,
            ready,
        )
        ready = sums.tick(scale_rows)
        query_grad = lowered(dot_nt(normed, d_raw))
        sums.push(out_grad, query_grad)
        ready = [*ready, *sums.enter()]
        d_keys, d_values = add_back(own_dk, own_dv, back, ready)
        scale_raw = jnp.sum(scale_rows.reshape(heads, HD), 0) / (gain_q * LOG_TWO_E)
        scale_grad = scale_raw * jax.nn.sigmoid(query_scale[layer]) * LOG_TWO_E / math.sqrt(HD)
        if not layer:
            key_grad, value_grad = [lowered(dot_nt(normed, d)) for d in (d_keys, d_values)]
            ready = sums.tick(key_grad, value_grad)
            last = Scatter(orders)
            last.push(key_grad, value_grad)
            last.enter()
        terms = scatter_tokens(
            lambda dq, dk, dv: dot_nn(wq, dq) + dot_nn(wk, dk) + dot_nn(wv, dv),
            d_raw,
            d_keys,
            d_values,
        )
        if layer:
            ready = sums.tick(terms[-1])
        else:
            sums.tick(terms[-1])
            ready = last.tick(terms[-1])
            hiddens = [lowered(tied(h.astype(jnp.float32), ready)) for h in final[2]]
            current = final[0] + sum(dot_nn(w, h) for w, h in zip(final[1], hiddens))
        grad, grad_low, attn_gain_grad = norm_back(
            source, inverse_attn, attn_gain, grad_middle, terms, ready
        )
        if layer:
            key_grad, value_grad = [lowered(dot_nt(normed, d)) for d in (d_keys, d_values)]
            sums.push(key_grad, value_grad)
            sums.tick(grad, key_grad, value_grad)
        small_grads[layer] = jnp.concatenate([attn_gain_grad, feed_gain_grad, scale_grad])
    small = jnp.stack(small_grads)
    for axis, bits in (("tensor", 1), ("dp", 2)):
        bit = 1
        while bit < lax.axis_size(axis):
            small, bit = exchange_sum(small, axis, bit, bits, last), bit << bits
    done = sums.finish() + last.finish()
    layer_grads = []
    for layer in range(LAYERS):
        at = 3 * (LAYERS - 1 - layer)
        (down_grad, up_grad), (out_grad, query_grad), (key_grad, value_grad) = done[at : at + 3]
        layer_grads.append(
            (query_grad, key_grad, value_grad, out_grad.T, up_grad, down_grad.T)
        )

    summed = [jnp.stack(members) for members in zip(*layer_grads)]
    width = current.shape[0]
    return (
        current.T,
        grad.T,
        *summed,
        small[:, :width],
        small[:, width : 2 * width],
        small[:, 2 * width :],
    )


def solution(mesh):
    in_specs = (
        P(("dp", "tensor"), None),
        P(("dp", "tensor"), None),
        P(None, "dp", "tensor"),
        P(None, "dp", "tensor"),
        P(None, "dp", "tensor"),
        P(None, "tensor", "dp"),
        P(None, "dp", "tensor"),
        P(None, "tensor", "dp"),
        P(),
        P(),
        P(),
        P("dp", None),
    )
    out_specs = (
        P(("dp", "tensor"), None),
        P(("dp", "tensor"), None),
        P(None, "dp", "tensor"),
        P(None, "dp", "tensor"),
        P(None, "dp", "tensor"),
        P(None, "tensor", "dp"),
        P(None, "dp", "tensor"),
        P(None, "tensor", "dp"),
        P(),
        P(),
        P(),
    )
    return jax.shard_map(body, mesh=mesh, in_specs=in_specs, out_specs=out_specs, check_vma=False)
```

```python
from functools import partial
import math

import jax
import jax.numpy as jnp
from jax import lax
from jax.experimental.layout import Layout, with_layout_constraint
from jax.experimental import pallas as pl
from jax.experimental.pallas import tpu as pltpu
from jax.sharding import PartitionSpec as P

HD = 80
LAYERS = 2
PROMPT_DEV = 512
TILE = 256

EPSILON = 1e-06
LOG_TWO_E = 1.4426950408889634
LN_TWO = 0.6931471805599453
NEGATIVE = -1e30


def lowered(values):
    return values.astype(jnp.bfloat16)


def dot_nn(former, latter):
    return jnp.dot(former, latter, preferred_element_type=jnp.float32)


def dot_tn(former, latter):
    return lax.dot_general(
        former, latter, (((0,), (0,)), ((), ())), preferred_element_type=jnp.float32
    )


def dot_nt(former, latter):
    return lax.dot_general(
        former, latter, (((1,), (1,)), ((), ())), preferred_element_type=jnp.float32
    )


def softplus(values):
    return jnp.log1p(jnp.exp(values))


def pair_swap(values, axis, bit):
    size = lax.axis_size(axis)
    return lax.ppermute(values, axis, [(i, i ^ bit) for i in range(size)])


def exchange_orders(size):
    if size == 16:
        return (8, 4), ((2, 1), (1, 2))
    bits = tuple(1 << k for k in reversed(range(size.bit_length() - 1)))
    first, rest = bits[:1], bits[1:]
    half = len(rest) // 2
    return first, (rest, rest[half:] + rest[:half])


WHOLE = pl.BlockSpec(memory_space=pltpu.VMEM)
SCALAR = pl.BlockSpec(memory_space=pltpu.SMEM)
UNREAD = pl.BlockSpec(memory_space=pl.ANY)


def dp_bits(bits):
    place = lax.axis_index("dp")
    return jnp.stack([((place & bit) != 0).astype(jnp.int32) for bit in bits])


def quick_call(kernel, name, arrays, after, out_shape):
    out = pl.pallas_call(
        kernel,
        in_specs=[SCALAR] + [WHOLE] * (len(arrays) - 1) + [UNREAD] * len(after),
        out_specs=[WHOLE] * len(out_shape),
        out_shape=out_shape,
        compiler_params=pltpu.CompilerParams(vmem_limit_bytes=48 << 20),
        cost_estimate=pl.CostEstimate(flops=1, bytes_accessed=1, transcendentals=0),
        name=name,
    )(*arrays, *after)
    return list(out)


class Gather:
    def __init__(self, pairs, orders):
        self.first, self.rest = orders
        self.queue = [jnp.stack(pair)[:, None] for pair in pairs]
        self.left = len(pairs)
        self.early, self.early_at = None, 0
        self.late, self.late_at = None, 0
        self.ready = []

    def tick(self, *after):
        if self.early is None and self.queue:
            self.early, self.early_at = self.queue.pop(0), 0
        if self.late is None and self.early is not None and self.early_at == len(self.first):
            self.late, self.late_at = self.early, 0
            self.early, self.early_at = (self.queue.pop(0), 0) if self.queue else (None, 0)
        jobs = []
        early = self.early is not None and self.early_at < len(self.first)
        if early:
            jobs.append((self.early, self.first[: self.early_at + 1]))
        if self.late is not None:
            for values, order in zip(self.late, self.rest):
                jobs.append((values, self.first + order[: self.late_at + 1]))
        if not jobs:
            return []
        got = [pair_swap(values, "dp", done[-1]) for values, done in jobs]
        plans, shapes = [], []
        for values, done in jobs:
            members, blocks, rows, width = values.shape
            before = 1 << sum(1 for bit in done[:-1] if bit > done[-1])
            parts = members if members > 1 and len(done) == len(self.first) else 1
            plans.append((members, before, blocks // before, parts, len(shapes)))
            shapes += [(members // parts, 2 * blocks, rows, width)] * parts
        count = len(jobs)
        merged = self.late is not None and self.merges() and (
            self.late_at + 1 == len(self.rest[0])
        )
        if merged:
            at = plans[-2][-1]
            shapes[at:] = [(2,) + shapes[at][1:]]
        following = self.queue[:1]

        def join(bit_ref, *refs):
            outs = refs[len(refs) - len(shapes) - len(following) :]
            if following:
                outs[-1][...] = refs[2 * count][...]
            for job, (members, before, blocks, parts, at) in enumerate(plans):
                bit = bit_ref[job]
                for member in range(members):
                    if merged and job == count - 1:
                        out, row = outs[at - 1], 1
                    elif parts > 1:
                        out, row = outs[at + member], 0
                    else:
                        out, row = outs[at], member
                    for step in range(before):
                        here = pl.ds(step * blocks, blocks)
                        place = 2 * step * blocks
                        ours, theirs = place + bit * blocks, place + (1 - bit) * blocks
                        out[row, pl.ds(ours, blocks)] = refs[job][member, here]
                        out[row, pl.ds(theirs, blocks)] = refs[count + job][member, here]

        outs = quick_call(
            join,
            "join_halves",
            [
                dp_bits([done[-1] for _, done in jobs]),
                *[values for values, _ in jobs],
                *got,
                *following,
            ],
            after,
            [
                jax.ShapeDtypeStruct(shape, jnp.bfloat16)
                for shape in shapes + [values.shape for values in following]
            ],
        )
        if following:
            self.queue[0] = outs.pop()
        if early:
            self.early_at += 1
            done = self.early_at == len(self.first)
            self.early = outs[:2] if done else outs[0]
        if self.late is not None:
            self.late, self.late_at = outs[-1:] if merged else outs[-2:], self.late_at + 1
            if self.late_at == len(self.rest[0]):
                width = self.late[0].shape[-1]
                shape = (2, -1, width) if merged else (-1, width)
                self.ready.append([values.reshape(shape) for values in self.late])
                self.late = None
                self.left -= 1
        return outs

    def merges(self):
        return self.left % 3 == 1

    def take(self):
        while not self.ready:
            self.tick()
        return self.ready.pop(0)


class Scatter:
    def __init__(self, orders):
        self.first, self.rest = orders
        self.bits = sorted(self.first + self.rest[0], reverse=True)
        self.queue, self.late, self.early, self.done = [], None, None, []

    def push(self, *pair, came=(None, None)):
        rows = pair[0].shape[0] >> len(self.bits)
        shape = (1, 1 << len(self.bits), rows, pair[0].shape[1])
        self.queue.append(
            [
                ([values.reshape(shape)], None if more is None else [more.reshape(shape)], order)
                for values, more, order in zip(pair, came, self.rest)
            ]
        )

    def run(self, jobs, after):
        plans, ins, shapes, bits = [], [], [], []
        for held, got, left, bit, joined in jobs:
            blocks, rows, width = held[0].shape[1:]
            members = sum(values.shape[0] for values in held)
            at = left.index(bit) if bit else 0
            behind = blocks // 2 >> at if bit else blocks
            plans.append((len(held), len(ins), bool(got), 1 << at, behind, bit, joined, len(shapes)))
            ins += held + (got or [])
            bits.append(bit or 1)
            if bit:
                groups = 1 if joined else members
                shapes += [((members // groups, blocks // 2, rows, width), jnp.bfloat16)] * (
                    2 * groups
                )
            else:
                shapes += [((rows, width), jnp.float32)] * members
        inputs = len(ins)

        def add(bit_ref, *refs):
            sources, outs = refs[:inputs], refs[len(refs) - len(shapes) :]
            for job, (arrays, at, come, before, behind, bit, joined, out_at) in enumerate(plans):
                mine = bit_ref[job]
                member = 0
                for array in range(arrays):
                    held = sources[at + array]
                    for row in range(held.shape[0]):

                        def total(start):
                            values = held[row, pl.ds(start, behind)]
                            if come:
                                other = sources[at + arrays + array][row, pl.ds(start, behind)]
                                values = values.astype(jnp.float32) + other.astype(jnp.float32)
                            return values

                        if bit is None:
                            outs[out_at + member][...] = total(0)[0]
                        else:
                            keep, send, place = (
                                (outs[out_at], outs[out_at + 1], member)
                                if joined
                                else (outs[out_at + 2 * member], outs[out_at + 2 * member + 1], 0)
                            )
                            for step in range(before):
                                start = 2 * step * behind
                                there = pl.ds(step * behind, behind)
                                keep[place, there] = lowered(total(start + mine * behind))
                                send[place, there] = lowered(total(start + (1 - mine) * behind))
                        member += 1

        return quick_call(
            add,
            "add_halves",
            [dp_bits(bits), *ins],
            after,
            [jax.ShapeDtypeStruct(shape, kind) for shape, kind in shapes],
        )

    def enter(self):
        if self.late is not None or not self.queue:
            return []
        jobs = [
            (held, came, self.bits, order[-1], False) for held, came, order in self.queue.pop(0)
        ]
        outs = self.run(jobs, ())
        self.late = (outs[0::2], outs[1::2], 1)
        return outs

    def tick(self, *after):
        self.enter()
        jobs, steps = [], len(self.rest[0])
        if self.early is not None:
            keep, send, at = self.early
            bits = self.first[: len(self.first) - at + 1]
            left = sorted(bits[:-1], reverse=True)
            got = [pair_swap(send, "dp", bits[-1])]
            jobs.append(([keep], got, left, bits[-2] if left else None, True))
        if self.late is not None:
            keeps, sends, at = self.late
            got = [
                pair_swap(send, "dp", order[steps - at]) for send, order in zip(sends, self.rest)
            ]
            for keep, come, order in zip(keeps, got, self.rest):
                left = sorted(self.first + order[: steps - at], reverse=True)
                if at < steps:
                    jobs.append(([keep], [come], left, order[steps - at - 1], False))
            if at == steps:
                jobs.append((keeps, got, left, self.first[-1], True))
        if not jobs:
            return []
        outs = self.run(jobs, after)
        rest = outs
        if self.early is not None:
            if at_end(self.early[2], self.first):
                self.done.append(rest[:2])
                self.early = None
            else:
                self.early = (rest[0], rest[1], self.early[2] + 1)
            rest = rest[2:]
        if self.late is not None:
            if self.late[2] == steps:
                self.early, self.late = (rest[0], rest[1], 1), None
            else:
                self.late = (rest[0::2], rest[1::2], self.late[2] + 1)
        return outs

    def finish(self):
        while self.queue or self.late or self.early:
            self.tick()
        return self.done


def at_end(step, bits):
    return step == len(bits)


def gather_tokens(local):
    if lax.axis_size("tensor") != 2:
        values = lax.all_gather(local, "tensor", axis=1, tiled=True)
        return values, values
    other = pair_swap(local, "tensor", 1)
    upper = lax.axis_index("tensor") != 0
    values = [jnp.where(upper, other, local), jnp.where(upper, local, other)]
    return jnp.concatenate(values, axis=1), other


def far_part(normed):
    part = PROMPT_DEV // lax.axis_size("tensor")
    place = lax.axis_index("tensor") * part
    return pair_swap(lax.dynamic_slice_in_dim(normed, place, part, 1), "dp", 1)


def scatter_tokens(product, *values):
    if lax.axis_size("tensor") != 2:
        return [
            lax.psum_scatter(
                lowered(product(*values)), "tensor", scatter_dimension=1, tiled=True
            )
        ]
    count = values[0].shape[1] // 2
    place = lax.axis_index("tensor")
    theirs = [lax.dynamic_slice_in_dim(v, (1 - place) * count, count, 1) for v in values]
    got = pair_swap(lowered(product(*theirs)), "tensor", 1)
    mine = [lax.dynamic_slice_in_dim(v, place * count, count, 1) for v in values]
    return [lowered(product(*mine)), got]


def feed_parts(both):
    if lax.axis_size("tensor") != 2:
        whole = lax.all_gather(both, "tensor", axis=2, tiled=True)
        return [whole[0]], [whole[1]]
    other = pair_swap(both, "tensor", 1)
    return [both[0], other[0]], [both[1], other[1]]


def feed_total(parts):
    if lax.axis_size("tensor") != 2:
        whole = lax.psum_scatter(lowered(parts[0]), "tensor", scatter_dimension=1, tiled=True)
        return whole, None
    mine, theirs = [with_layout_constraint(lowered(part), Layout((0, 1))) for part in parts]
    return mine, pair_swap(theirs, "tensor", 1)


def exchange_sum(values, axis, bit, bits, exchange):
    wide = bits == 2 and 2 * bit < lax.axis_size(axis)
    came = [pair_swap(values, axis, bit * by) for by in ((1, 2, 3) if wide else (1,))]
    after = exchange.tick(*came)
    total = values + came[0]
    if wide:
        total = total + (came[1] + came[2])
    return tied(total, after)


def tied(gain, after):
    if not after:
        return gain
    corner = after[0][(0,) * after[0].ndim].astype(jnp.float32)
    return gain + jnp.minimum((corner > 3e38).astype(jnp.int32), 0).astype(jnp.float32)


def norm(terms, gain, after=()):
    total = sum(term.astype(jnp.float32) for term in terms)
    inverse = lax.rsqrt(jnp.mean(total * total, axis=0, keepdims=True) + EPSILON)
    return total, inverse, lowered(total * inverse * tied(gain, after))


def norm_back(source, inverse, gain, grad, terms, after=()):
    incoming = sum(term.astype(jnp.float32) for term in terms)
    if len(terms) > 1:
        incoming = lax.optimization_barrier(lowered(incoming)).astype(jnp.float32)
    unit = source * inverse
    gain_grad = jnp.sum(incoming * unit, axis=1)
    scaled = incoming * tied(gain, after)
    total = grad + inverse * (scaled - unit * jnp.mean(scaled * unit, axis=0, keepdims=True))
    return total, lowered(total), gain_grad


def first_slot(_):
    return jnp.zeros((1,), jnp.int32)


def add_back(own_keys, own_values, back, after):
    def kernel(_, keys_ref, values_ref, back_ref, *refs):
        for place, (ref, out) in enumerate(zip((keys_ref, values_ref), refs[-2:])):
            prompt = ref[:, :PROMPT_DEV].astype(jnp.float32) + back_ref[place].astype(jnp.float32)
            out[:, :PROMPT_DEV] = lowered(prompt)
            out[:, PROMPT_DEV:] = ref[:, PROMPT_DEV:]

    out = [jax.ShapeDtypeStruct(own_keys.shape, jnp.bfloat16)] * 2
    arrays = [first_slot(back), own_keys, own_values, back]
    return quick_call(kernel, "add_back", arrays, after, out)


def key_parts(tile):
    first = tile * TILE
    if first < PROMPT_DEV:
        return ([(0, first, "free")] if first else []) + [(first, TILE, "earlier")]
    return [(0, PROMPT_DEV, "free"), (PROMPT_DEV, first - PROMPT_DEV + TILE, "segment")]


def masked(scores, kind, first_key, first_query, start):
    if kind == "free":
        return scores
    key = lax.broadcasted_iota(jnp.int32, scores.shape, 0) + first_key
    query = lax.broadcasted_iota(jnp.int32, scores.shape, 1) + first_query
    allowed = key <= query
    if kind == "segment":
        allowed = allowed & (key >= start)
    return jnp.where(allowed, scores, NEGATIVE)


def spans(reference):
    tokens = reference.shape[1]
    return [(tile, slice(tile * TILE, tile * TILE + TILE)) for tile in range(tokens // TILE)]


def ahead(steps):
    held = steps[0][0]()
    for place, (_, second) in enumerate(steps):
        following = steps[place + 1][0]() if place + 1 < len(steps) else None
        second(held)
        held = following


def own_forward(heads):
    def steps(start_ref, q_ref, k_ref, v_ref, sum_ref, top_ref, total_ref):
        keys = k_ref[...].T

        def scores_of(tile, at):
            query, start = q_ref[:, at], start_ref[:, at]
            return [
                masked(dot_nn(keys[key : key + count], query), kind, key, tile * TILE, start)
                for key, count, kind in key_parts(tile)
            ]

        def mix(tile, at, parts):
            highest = jnp.max(parts[0], axis=0, keepdims=True)
            for scores in parts[1:]:
                highest = jnp.maximum(highest, jnp.max(scores, axis=0, keepdims=True))
            total, mixed = 0.0, 0.0
            for scores, (key, count, _) in zip(parts, key_parts(tile)):
                weights = jnp.exp2(scores - highest)
                total = total + jnp.sum(weights, axis=0, keepdims=True)
                mixed = mixed + dot_nn(v_ref[:, key : key + count], lowered(weights))
            sum_ref[:, at] = mixed
            top_ref[:, at] = highest
            total_ref[:, at] = total

        return [(partial(scores_of, *item), partial(mix, *item)) for item in spans(q_ref)]

    ahead([step for refs in heads for step in steps(*refs)])


def sides(side_ref, q_ref, run):
    tiles = [at for _, at in spans(q_ref)]
    conts = [at for tile, at in spans(q_ref) if tile * TILE >= PROMPT_DEV]

    @pl.when(side_ref[0] == 0)
    def _():
        run(conts, [at for at in tiles if at not in conts])

    @pl.when(side_ref[0] != 0)
    def _():
        run(tiles, [])


def far_forward(heads):
    def steps(tiles, _, q_ref, k_ref, v_ref, sum_ref, top_ref, total_ref, out_ref, lse_ref):
        keys = k_ref[...].T

        def scores_of(at):
            return dot_nn(keys, q_ref[:, at])

        def mix(at, scores):
            highest = jnp.maximum(top_ref[:, at], jnp.max(scores, axis=0, keepdims=True))
            weights = jnp.exp2(scores - highest)
            scale = jnp.exp2(top_ref[:, at] - highest)
            total = total_ref[:, at] * scale + jnp.sum(weights, axis=0, keepdims=True)
            mixed = sum_ref[:, at] * scale + dot_nn(v_ref[...], lowered(weights))
            out_ref[:, at] = lowered(mixed / total)
            lse_ref[:, at] = highest + jnp.log2(total)

        return [(partial(scores_of, at), partial(mix, at)) for at in tiles]

    def run(tiles, others):
        for _, _, _, _, sum_ref, top_ref, total_ref, out_ref, lse_ref in heads:
            for at in others:
                out_ref[:, at] = lowered(sum_ref[:, at] / total_ref[:, at])
                lse_ref[:, at] = top_ref[:, at] + jnp.log2(total_ref[:, at])
        ahead([step for refs in heads for step in steps(tiles, *refs)])

    sides(heads[0][0], heads[0][1], run)


def score_grads(scores, lse, d_shares, delta):
    shares = jnp.exp2(scores - lse)
    return lowered(shares), lowered(shares * (d_shares - delta))


def far_backward(heads):
    def steps(
        tiles, _, q_ref, k_ref, v_ref, out_ref, grad_ref, lse_ref, dq_ref, delta_ref, dkv_ref
    ):
        keys, values = k_ref[...].T, v_ref[...].T
        delta_ref[...] = jnp.sum(
            out_ref[...].astype(jnp.float32) * grad_ref[...].astype(jnp.float32),
            axis=0,
            keepdims=True,
        )
        sums = [0.0, 0.0]

        def begin(at):
            return dot_nn(keys, q_ref[:, at]), dot_nn(values, grad_ref[:, at])

        def terms(at, held):
            scores, d_shares = held
            shares, d_scores = score_grads(scores, lse_ref[:, at], d_shares, delta_ref[:, at])
            dq_ref[:, at] = dot_nn(k_ref[...], d_scores)
            sums[0] = sums[0] + dot_nt(q_ref[:, at], d_scores)
            sums[1] = sums[1] + dot_nt(grad_ref[:, at], shares)
            if at is tiles[-1]:
                dkv_ref[0] = lowered(sums[0] * LN_TWO)
                dkv_ref[1] = lowered(sums[1])

        return [(partial(begin, at), partial(terms, at)) for at in tiles]

    def run(tiles, others):
        for refs in heads:
            for at in others:
                refs[7][:, at] = jnp.zeros_like(refs[7][:, at])
        ahead([step for refs in heads for step in steps(tiles, *refs)])

    sides(heads[0][0], heads[0][1], run)


def own_backward(heads):
    def steps(
        start_ref,
        gain_ref,
        q_ref,
        k_ref,
        v_ref,
        grad_ref,
        lse_ref,
        delta_ref,
        far_dq_ref,
        dq_ref,
        dk_ref,
        dv_ref,
        scale_ref,
        k_total,
        v_total,
    ):
        keys, values = k_ref[...].T, v_ref[...].T
        seen, dqs, scales = set(), {}, [0.0]
        final = spans(q_ref)[-1][0]

        def begin(tile, at, part, last):
            key, count, kind = part
            scores = dot_nn(keys[key : key + count], q_ref[:, at])
            scores = masked(scores, kind, key, tile * TILE, start_ref[:, at])
            return scores, dot_nn(values[key : key + count], grad_ref[:, at])

        def terms(tile, at, part, last, held):
            key, count, _ = part
            scores, d_shares = held
            query, grad = q_ref[:, at], grad_ref[:, at]
            shares, d_scores = score_grads(scores, lse_ref[:, at], d_shares, delta_ref[:, at])
            dv = dot_nt(grad, shares)
            dk = dot_nt(query, d_scores)
            dq = dqs.get(tile, far_dq_ref[:, at])
            dqs[tile] = dq = dq + dot_nn(k_ref[:, key : key + count], d_scores)
            for offset in range(0, count, TILE):
                there = slice(key + offset, key + offset + TILE)
                here = slice(offset, offset + TILE)
                if key + offset in seen:
                    k_total[:, there] += dk[:, here]
                    v_total[:, there] += dv[:, here]
                else:
                    seen.add(key + offset)
                    k_total[:, there] = dk[:, here]
                    v_total[:, there] = dv[:, here]
            if last:
                dq_ref[:, at] = lowered(dq * gain_ref[...])
                product = jnp.sum(dq * query.astype(jnp.float32), axis=1, keepdims=True)
                scales[0] = scales[0] + product
                if tile == final:
                    dk_ref[...] = lowered(k_total[...] * LN_TWO)
                    dv_ref[...] = lowered(v_total[...])
                    scale_ref[...] = scales[0]

        items = []
        for tile, at in spans(q_ref):
            parts = key_parts(tile)
            items += [(tile, at, part, part is parts[-1]) for part in parts]
        return [(partial(begin, *item), partial(terms, *item)) for item in items]

    ahead([step for refs in heads for step in steps(*refs)])


def per_head(kernel, name, heads, area, products, ins, outs, after=(), scratch=()):
    group = 2 - heads % 2
    moved = sum(array.size * array.dtype.itemsize for _, array in ins)

    def spec(kind, shape):
        if kind == "rows":
            return pl.BlockSpec((group * HD, shape[1]), lambda step: (step, 0))
        if kind == "flat":
            return pl.BlockSpec((group, 1, shape[2]), lambda step: (step, 0, 0))
        if kind == "pair":
            return pl.BlockSpec((2, group * HD, shape[2]), lambda step: (0, step, 0))
        return pl.BlockSpec(shape, lambda step: (0, 0)) if kind == "same" else SCALAR

    def view(kind, ref, head):
        rows = pl.ds(head * HD, HD)
        if kind == "rows":
            return ref.at[rows]
        if kind == "flat":
            return ref.at[head]
        return ref.at[:, rows] if kind == "pair" else ref

    count = len(ins)
    kinds = [kind for kind, _ in ins] + [out[0] for out in outs] + ["rows"] * len(scratch)

    def work(*refs):
        refs = refs[:count] + refs[count + len(after) :]
        kernel(
            [[view(kind, ref, head) for kind, ref in zip(kinds, refs)] for head in range(group)]
        )

    return pl.pallas_call(
        work,
        grid=(heads // group,),
        in_specs=[spec(kind, array.shape) for kind, array in ins] + [UNREAD] * len(after),
        out_specs=[spec(kind, shape) for kind, shape, _ in outs],
        out_shape=[jax.ShapeDtypeStruct(shape, kind) for _, shape, kind in outs],
        scratch_shapes=[pltpu.VMEM((group * HD, tokens), jnp.float32) for tokens in scratch],
        compiler_params=pltpu.CompilerParams(vmem_limit_bytes=40 << 20),
        cost_estimate=pl.CostEstimate(
            flops=40 * area * heads * products,
            bytes_accessed=moved,
            transcendentals=area * heads,
        ),
        name=name,
    )(*[array for _, array in ins], *after)


def attention_own(start, queries, keys, values, after):
    width, tokens = queries.shape
    heads = width // HD
    flat = ("flat", (heads, 1, tokens), jnp.float32)
    return per_head(
        own_forward,
        "attention_own",
        heads,
        tokens * tokens * 5 // 8,
        3,
        [("same", start), ("rows", queries), ("rows", keys), ("rows", values)],
        [("rows", (width, tokens), jnp.float32), flat, flat],
        after,
    )


def attention_far(side, queries, keys, values, partial_sum, top, total, after):
    width, tokens = queries.shape
    heads = width // HD
    return per_head(
        far_forward,
        "attention_far",
        heads,
        tokens * PROMPT_DEV,
        2,
        [
            ("scalar", side),
            ("rows", queries),
            ("rows", keys),
            ("rows", values),
            ("rows", partial_sum),
            ("flat", top),
            ("flat", total),
        ],
        [
            ("rows", (width, tokens), jnp.bfloat16),
            ("flat", (heads, 1, tokens), jnp.float32),
        ],
        after,
    )


def attention_far_back(side, queries, keys, values, mixed, grads, lse, after):
    width, tokens = queries.shape
    heads = width // HD
    return per_head(
        far_backward,
        "attention_far_back",
        heads,
        tokens * PROMPT_DEV,
        3,
        [
            ("scalar", side),
            ("rows", queries),
            ("rows", keys),
            ("rows", values),
            ("rows", mixed),
            ("rows", grads),
            ("flat", lse),
        ],
        [
            ("rows", (width, tokens), jnp.float32),
            ("flat", (heads, 1, tokens), jnp.float32),
            ("pair", (2, width, PROMPT_DEV), jnp.bfloat16),
        ],
        after,
    )


def attention_own_back(start, gain, queries, keys, values, grads, lse, delta, far_dq, after):
    width, tokens = queries.shape
    heads = width // HD
    return per_head(
        own_backward,
        "attention_own_back",
        heads,
        tokens * tokens * 5 // 8,
        76,
        [
            ("same", start),
            ("same", gain),
            ("rows", queries),
            ("rows", keys),
            ("rows", values),
            ("rows", grads),
            ("flat", lse),
            ("flat", delta),
            ("rows", far_dq),
        ],
        [
            ("rows", (width, tokens), jnp.bfloat16),
            ("rows", (width, tokens), jnp.bfloat16),
            ("rows", (width, tokens), jnp.bfloat16),
            ("rows", (width, 1), jnp.float32),
        ],
        after,
        (tokens, tokens),
    )


def segment_starts(lengths_row, tokens):
    place = jnp.arange(tokens, dtype=jnp.int32) - PROMPT_DEV
    bounds = jnp.cumsum(lengths_row)
    passed = jnp.where(place[:, None] >= bounds[None, :], bounds[None, :], 0)
    return (PROMPT_DEV + jnp.max(passed, axis=1))[None, :]


def body(
    inputs,
    cotangent,
    query_weight,
    key_weight,
    value_weight,
    output_weight,
    up_weight,
    down_weight,
    attention_gain,
    feed_gain,
    query_scale,
    cont_lengths,
):
    tokens = inputs.shape[0] * lax.axis_size("tensor")
    heads = query_weight.shape[2] // HD
    orders = exchange_orders(lax.axis_size("dp"))
    side = (lax.axis_index("dp") % 2).astype(jnp.int32)[None]
    start = segment_starts(cont_lengths[0], tokens)

    pairs = []
    for layer in range(LAYERS):
        pairs.append((key_weight[layer], value_weight[layer]))
        pairs.append((query_weight[layer], output_weight[layer].T))
        pairs.append((up_weight[layer], down_weight[layer].T))

    gather = Gather(pairs, orders)
    stored = []
    terms = [inputs.T]
    ready = ()
    grad = cotangent.T
    for layer in range(LAYERS):
        attn_gain = attention_gain[layer][:, None]
        ff_gain = feed_gain[layer][:, None]
        current, inverse_attn, low = norm(terms, attn_gain, ready)
        normed, came = gather_tokens(low)
        gather.tick(came)
        if layer == 0:
            far = far_part(normed)
            gather.tick(far)
            far_normed, came = gather_tokens(far)
            gather.tick(came)
            gather.tick(grad)
            wk, wv = gather.take()
            gather.tick()
        keys = lowered(dot_tn(wk, normed))
        values = lowered(dot_tn(wv, normed))
        gather.tick(keys, values)
        wq, wo = gather.take()
        gain_q = softplus(query_scale[layer]) * LOG_TWO_E / math.sqrt(HD)
        gain_rows = jnp.tile(gain_q, heads)[:, None]
        queries = lowered(dot_tn(wq, normed) * (gain_rows * LOG_TWO_E))
        own_sum, top, total = attention_own(start, queries, keys, values, ())
        if layer:
            far = far_part(normed)
            ready = gather.tick(top, far)
            far_normed, _ = gather_tokens(far)
        far_keys = lowered(dot_tn(wk, far_normed))
        far_values = lowered(dot_tn(wv, far_normed))
        if not layer:
            ready = gather.tick(top, far_keys, far_values)
        mixed, lse = attention_far(side, queries, far_keys, far_values, own_sum, top, total, ready)
        gather.tick(lse)
        (both,) = gather.take()
        terms = scatter_tokens(lambda rows: dot_nn(wo, rows), mixed)
        ups, downs = feed_parts(both)
        ready = gather.tick(terms[-1])
        middle, inverse_feed, feed = norm([current, *terms], ff_gain, ready)
        uppers = [dot_tn(w, feed) for w in ups]
        ready = gather.tick(*uppers)
        if layer + 1 < LAYERS:
            following = gather.take()
        hiddens = [lowered(upper * jax.nn.sigmoid(upper)) for upper in uppers]
        stored.append(
            (
                (current, inverse_attn, attn_gain, normed),
                (gain_q, queries, keys, values, far_keys, far_values, mixed, lse),
                (middle, inverse_feed, ff_gain, feed, uppers, hiddens),
                (wk, wv, wq, wo, ups, downs),
            )
        )
        if layer + 1 < LAYERS:
            terms = [middle, sum(dot_nn(w, hidden) for w, hidden in zip(downs, hiddens))]
            wk, wv = following
    final = (middle, downs, hiddens)

    sums = Scatter(orders)
    small_grads = [None] * LAYERS
    grad_low = lowered(grad)
    for layer in reversed(range(LAYERS)):
        (
            (source, inverse_attn, attn_gain, normed),
            (gain_q, queries, keys, values, far_keys, far_values, mixed, lse),
            (middle, inverse_feed, ff_gain, feed, uppers, hiddens),
            (wk, wv, wq, wo, ups, downs),
        ) = stored[layer]
        d_uppers = []
        for w, upper in zip(downs, uppers):
            d_hidden = lowered(dot_tn(w, grad_low)).astype(jnp.float32)
            sigmoid = jax.nn.sigmoid(upper)
            d_uppers.append(lowered(d_hidden * (sigmoid * (1.0 + upper * (1.0 - sigmoid)))))
        d_feed = sum(dot_nn(w, d_upper) for w, d_upper in zip(ups, d_uppers))
        ready = sums.tick(d_feed)
        grad_middle, low, feed_gain_grad = norm_back(
            middle, inverse_feed, ff_gain, grad, [d_feed], ready
        )
        middle_low, came = gather_tokens(low)
        down_grad, down_came = feed_total([dot_nt(grad_low, hidden) for hidden in hiddens])
        up_grad, up_came = feed_total([dot_nt(feed, d_upper) for d_upper in d_uppers])
        if down_came is None:
            stepped = sums.tick(came, down_grad, up_grad)
            sums.push(down_grad, up_grad)
        else:
            stepped = sums.tick(came, down_came, up_came)
            sums.push(down_grad, up_grad, came=(down_came, up_came))
        d_mixed = lowered(dot_tn(wo, middle_low))
        out_grad = lowered(dot_nt(middle_low, mixed))
        ready = [*sums.enter(), *stepped]
        far_dq, delta, far_dkv = attention_far_back(
            side, queries, far_keys, far_values, mixed, d_mixed, lse, ready
        )
        back = pair_swap(far_dkv, "dp", 1)
        ready = sums.tick(delta)
        d_raw, own_dk, own_dv, scale_rows = attention_own_back(
            start,
            gain_q[:, None],
            queries,
            keys,
            values,
            d_mixed,
            lse,
            delta,
            far_dq,
            ready,
        )
        query_grad = lowered(dot_nt(normed, d_raw))
        if layer:
            d_keys, d_values = add_back(own_dk, own_dv, back, ())
            sums.tick(d_keys)
            sums.push(out_grad, query_grad)
            sums.enter()
        else:
            ready = sums.tick(scale_rows)
            sums.push(out_grad, query_grad)
            d_keys, d_values = add_back(own_dk, own_dv, back, [*ready, *sums.enter()])
        scale_raw = jnp.sum(scale_rows.reshape(heads, HD), 0) / (gain_q * LOG_TWO_E)
        scale_grad = scale_raw * jax.nn.sigmoid(query_scale[layer]) * LOG_TWO_E / math.sqrt(HD)
        if not layer:
            key_grad, value_grad = [lowered(dot_nt(normed, d)) for d in (d_keys, d_values)]
            ready = sums.tick(key_grad, value_grad)
            last = Scatter(orders)
            last.push(key_grad, value_grad)
            last.enter()
        terms = scatter_tokens(
            lambda dq, dk, dv: dot_nn(wq, dq) + dot_nn(wk, dk) + dot_nn(wv, dv),
            d_raw,
            d_keys,
            d_values,
        )
        if layer:
            ready = sums.tick(terms[-1])
        else:
            sums.tick(terms[-1])
            ready = last.tick(terms[-1])
            hiddens = [lowered(tied(h.astype(jnp.float32), ready)) for h in final[2]]
            current = final[0] + sum(dot_nn(w, h) for w, h in zip(final[1], hiddens))
        grad, grad_low, attn_gain_grad = norm_back(
            source, inverse_attn, attn_gain, grad_middle, terms, ready
        )
        if layer:
            key_grad, value_grad = [lowered(dot_nt(normed, d)) for d in (d_keys, d_values)]
            sums.push(key_grad, value_grad)
            sums.tick(grad, key_grad, value_grad)
        small_grads[layer] = jnp.concatenate([attn_gain_grad, feed_gain_grad, scale_grad])
    small = jnp.stack(small_grads)
    for axis, bits in (("tensor", 1), ("dp", 2)):
        bit = 1
        while bit < lax.axis_size(axis):
            small, bit = exchange_sum(small, axis, bit, bits, last), bit << bits
    done = sums.finish() + last.finish()
    layer_grads = []
    for layer in range(LAYERS):
        at = 3 * (LAYERS - 1 - layer)
        (down_grad, up_grad), (out_grad, query_grad), (key_grad, value_grad) = done[at : at + 3]
        layer_grads.append(
            (query_grad, key_grad, value_grad, out_grad.T, up_grad, down_grad.T)
        )

    summed = [jnp.stack(members) for members in zip(*layer_grads)]
    width = current.shape[0]
    return (
        current.T,
        grad.T,
        *summed,
        small[:, :width],
        small[:, width : 2 * width],
        small[:, 2 * width :],
    )


def solution(mesh):
    in_specs = (
        P(("dp", "tensor"), None),
        P(("dp", "tensor"), None),
        P(None, "dp", "tensor"),
        P(None, "dp", "tensor"),
        P(None, "dp", "tensor"),
        P(None, "tensor", "dp"),
        P(None, "dp", "tensor"),
        P(None, "tensor", "dp"),
        P(),
        P(),
        P(),
        P("dp", None),
    )
    out_specs = (
        P(("dp", "tensor"), None),
        P(("dp", "tensor"), None),
        P(None, "dp", "tensor"),
        P(None, "dp", "tensor"),
        P(None, "dp", "tensor"),
        P(None, "tensor", "dp"),
        P(None, "dp", "tensor"),
        P(None, "tensor", "dp"),
        P(),
        P(),
        P(),
    )
    return jax.shard_map(body, mesh=mesh, in_specs=in_specs, out_specs=out_specs, check_vma=False)
```

```python
from functools import partial
import math

import jax
import jax.numpy as jnp
from jax import lax
from jax.experimental.layout import Layout, with_layout_constraint
from jax.experimental import pallas as pl
from jax.experimental.pallas import tpu as pltpu
from jax.sharding import PartitionSpec as P

HD = 80
LAYERS = 2
PROMPT_DEV = 512
TILE = 256

EPSILON = 1e-06
LOG_TWO_E = 1.4426950408889634
LN_TWO = 0.6931471805599453
NEGATIVE = -1e30


def lowered(values):
    return values.astype(jnp.bfloat16)


def dot_nn(former, latter):
    return jnp.dot(former, latter, preferred_element_type=jnp.float32)


def dot_tn(former, latter):
    return lax.dot_general(
        former, latter, (((0,), (0,)), ((), ())), preferred_element_type=jnp.float32
    )


def dot_nt(former, latter):
    return lax.dot_general(
        former, latter, (((1,), (1,)), ((), ())), preferred_element_type=jnp.float32
    )


def softplus(values):
    return jnp.log1p(jnp.exp(values))


def pair_swap(values, axis, bit):
    size = lax.axis_size(axis)
    return lax.ppermute(values, axis, [(i, i ^ bit) for i in range(size)])


def exchange_orders(size):
    if size == 16:
        return (8, 4), ((2, 1), (1, 2))
    bits = tuple(1 << k for k in reversed(range(size.bit_length() - 1)))
    first, rest = bits[:1], bits[1:]
    half = len(rest) // 2
    return first, (rest, rest[half:] + rest[:half])


WHOLE = pl.BlockSpec(memory_space=pltpu.VMEM)
SCALAR = pl.BlockSpec(memory_space=pltpu.SMEM)
UNREAD = pl.BlockSpec(memory_space=pl.ANY)


def dp_bits(bits):
    place = lax.axis_index("dp")
    return jnp.stack([((place & bit) != 0).astype(jnp.int32) for bit in bits])


def quick_call(kernel, name, arrays, after, out_shape):
    out = pl.pallas_call(
        kernel,
        in_specs=[SCALAR] + [WHOLE] * (len(arrays) - 1) + [UNREAD] * len(after),
        out_specs=[WHOLE] * len(out_shape),
        out_shape=out_shape,
        compiler_params=pltpu.CompilerParams(vmem_limit_bytes=48 << 20),
        cost_estimate=pl.CostEstimate(flops=1, bytes_accessed=1, transcendentals=0),
        name=name,
    )(*arrays, *after)
    return list(out)


class Gather:
    def __init__(self, pairs, orders):
        self.first, self.rest = orders
        self.queue = [jnp.stack(pair)[:, None] for pair in pairs]
        self.left = len(pairs)
        self.early, self.early_at = None, 0
        self.late, self.late_at = None, 0
        self.ready = []

    def tick(self, *after):
        if self.early is None and self.queue:
            self.early, self.early_at = self.queue.pop(0), 0
        if self.late is None and self.early is not None and self.early_at == len(self.first):
            self.late, self.late_at = self.early, 0
            self.early, self.early_at = (self.queue.pop(0), 0) if self.queue else (None, 0)
        jobs = []
        early = self.early is not None and self.early_at < len(self.first)
        if early:
            jobs.append((self.early, self.first[: self.early_at + 1]))
        if self.late is not None:
            for values, order in zip(self.late, self.rest):
                jobs.append((values, self.first + order[: self.late_at + 1]))
        if not jobs:
            return []
        got = [pair_swap(values, "dp", done[-1]) for values, done in jobs]
        plans, shapes = [], []
        for values, done in jobs:
            members, blocks, rows, width = values.shape
            before = 1 << sum(1 for bit in done[:-1] if bit > done[-1])
            parts = members if members > 1 and len(done) == len(self.first) else 1
            plans.append((members, before, blocks // before, parts, len(shapes)))
            shapes += [(members // parts, 2 * blocks, rows, width)] * parts
        count = len(jobs)
        merged = self.late is not None and self.merges() and (
            self.late_at + 1 == len(self.rest[0])
        )
        if merged:
            at = plans[-2][-1]
            shapes[at:] = [(2,) + shapes[at][1:]]
        following = self.queue[:1]

        def join(bit_ref, *refs):
            outs = refs[len(refs) - len(shapes) - len(following) :]
            if following:
                outs[-1][...] = refs[2 * count][...]
            for job, (members, before, blocks, parts, at) in enumerate(plans):
                bit = bit_ref[job]
                for member in range(members):
                    if merged and job == count - 1:
                        out, row = outs[at - 1], 1
                    elif parts > 1:
                        out, row = outs[at + member], 0
                    else:
                        out, row = outs[at], member
                    for step in range(before):
                        here = pl.ds(step * blocks, blocks)
                        place = 2 * step * blocks
                        ours, theirs = place + bit * blocks, place + (1 - bit) * blocks
                        out[row, pl.ds(ours, blocks)] = refs[job][member, here]
                        out[row, pl.ds(theirs, blocks)] = refs[count + job][member, here]

        outs = quick_call(
            join,
            "join_halves",
            [
                dp_bits([done[-1] for _, done in jobs]),
                *[values for values, _ in jobs],
                *got,
                *following,
            ],
            after,
            [
                jax.ShapeDtypeStruct(shape, jnp.bfloat16)
                for shape in shapes + [values.shape for values in following]
            ],
        )
        if following:
            self.queue[0] = outs.pop()
        if early:
            self.early_at += 1
            done = self.early_at == len(self.first)
            self.early = outs[:2] if done else outs[0]
        if self.late is not None:
            self.late, self.late_at = outs[-1:] if merged else outs[-2:], self.late_at + 1
            if self.late_at == len(self.rest[0]):
                width = self.late[0].shape[-1]
                shape = (2, -1, width) if merged else (-1, width)
                self.ready.append([values.reshape(shape) for values in self.late])
                self.late = None
                self.left -= 1
        return outs

    def merges(self):
        return self.left % 3 == 1

    def take(self):
        while not self.ready:
            self.tick()
        return self.ready.pop(0)


class Scatter:
    def __init__(self, orders):
        self.first, self.rest = orders
        self.bits = sorted(self.first + self.rest[0], reverse=True)
        self.queue, self.late, self.early, self.done = [], None, None, []

    def push(self, *pair, came=(None, None)):
        rows = pair[0].shape[0] >> len(self.bits)
        shape = (1, 1 << len(self.bits), rows, pair[0].shape[1])
        self.queue.append(
            [
                ([values.reshape(shape)], None if more is None else [more.reshape(shape)], order)
                for values, more, order in zip(pair, came, self.rest)
            ]
        )

    def run(self, jobs, after):
        plans, ins, shapes, bits = [], [], [], []
        for held, got, left, bit, joined in jobs:
            blocks, rows, width = held[0].shape[1:]
            members = sum(values.shape[0] for values in held)
            at = left.index(bit) if bit else 0
            behind = blocks // 2 >> at if bit else blocks
            plans.append((len(held), len(ins), bool(got), 1 << at, behind, bit, joined, len(shapes)))
            ins += held + (got or [])
            bits.append(bit or 1)
            if bit:
                groups = 1 if joined else members
                shapes += [((members // groups, blocks // 2, rows, width), jnp.bfloat16)] * (
                    2 * groups
                )
            else:
                shapes += [((rows, width), jnp.float32)] * members
        inputs = len(ins)

        def add(bit_ref, *refs):
            sources, outs = refs[:inputs], refs[len(refs) - len(shapes) :]
            for job, (arrays, at, come, before, behind, bit, joined, out_at) in enumerate(plans):
                mine = bit_ref[job]
                member = 0
                for array in range(arrays):
                    held = sources[at + array]
                    for row in range(held.shape[0]):

                        def total(start):
                            values = held[row, pl.ds(start, behind)]
                            if come:
                                other = sources[at + arrays + array][row, pl.ds(start, behind)]
                                values = values.astype(jnp.float32) + other.astype(jnp.float32)
                            return values

                        if bit is None:
                            outs[out_at + member][...] = total(0)[0]
                        else:
                            keep, send, place = (
                                (outs[out_at], outs[out_at + 1], member)
                                if joined
                                else (outs[out_at + 2 * member], outs[out_at + 2 * member + 1], 0)
                            )
                            for step in range(before):
                                start = 2 * step * behind
                                there = pl.ds(step * behind, behind)
                                keep[place, there] = lowered(total(start + mine * behind))
                                send[place, there] = lowered(total(start + (1 - mine) * behind))
                        member += 1

        return quick_call(
            add,
            "add_halves",
            [dp_bits(bits), *ins],
            after,
            [jax.ShapeDtypeStruct(shape, kind) for shape, kind in shapes],
        )

    def enter(self):
        if self.late is not None or not self.queue:
            return []
        jobs = [
            (held, came, self.bits, order[-1], False) for held, came, order in self.queue.pop(0)
        ]
        outs = self.run(jobs, ())
        self.late = (outs[0::2], outs[1::2], 1)
        return outs

    def tick(self, *after):
        self.enter()
        jobs, steps = [], len(self.rest[0])
        if self.early is not None:
            keep, send, at = self.early
            bits = self.first[: len(self.first) - at + 1]
            left = sorted(bits[:-1], reverse=True)
            got = [pair_swap(send, "dp", bits[-1])]
            jobs.append(([keep], got, left, bits[-2] if left else None, True))
        if self.late is not None:
            keeps, sends, at = self.late
            got = [
                pair_swap(send, "dp", order[steps - at]) for send, order in zip(sends, self.rest)
            ]
            for keep, come, order in zip(keeps, got, self.rest):
                left = sorted(self.first + order[: steps - at], reverse=True)
                if at < steps:
                    jobs.append(([keep], [come], left, order[steps - at - 1], False))
            if at == steps:
                jobs.append((keeps, got, left, self.first[-1], True))
        if not jobs:
            return []
        outs = self.run(jobs, after)
        rest = outs
        if self.early is not None:
            if at_end(self.early[2], self.first):
                self.done.append(rest[:2])
                self.early = None
            else:
                self.early = (rest[0], rest[1], self.early[2] + 1)
            rest = rest[2:]
        if self.late is not None:
            if self.late[2] == steps:
                self.early, self.late = (rest[0], rest[1], 1), None
            else:
                self.late = (rest[0::2], rest[1::2], self.late[2] + 1)
        return outs

    def finish(self):
        while self.queue or self.late or self.early:
            self.tick()
        return self.done


def at_end(step, bits):
    return step == len(bits)


def gather_tokens(local):
    if lax.axis_size("tensor") != 2:
        values = lax.all_gather(local, "tensor", axis=1, tiled=True)
        return values, values
    other = pair_swap(local, "tensor", 1)
    upper = lax.axis_index("tensor") != 0
    values = [jnp.where(upper, other, local), jnp.where(upper, local, other)]
    return jnp.concatenate(values, axis=1), other


def far_part(normed):
    part = PROMPT_DEV // lax.axis_size("tensor")
    place = lax.axis_index("tensor") * part
    return pair_swap(lax.dynamic_slice_in_dim(normed, place, part, 1), "dp", 1)


def scatter_tokens(product, *values):
    if lax.axis_size("tensor") != 2:
        return [
            lax.psum_scatter(
                lowered(product(*values)), "tensor", scatter_dimension=1, tiled=True
            )
        ]
    count = values[0].shape[1] // 2
    place = lax.axis_index("tensor")
    theirs = [lax.dynamic_slice_in_dim(v, (1 - place) * count, count, 1) for v in values]
    got = pair_swap(lowered(product(*theirs)), "tensor", 1)
    mine = [lax.dynamic_slice_in_dim(v, place * count, count, 1) for v in values]
    return [lowered(product(*mine)), got]


def feed_parts(both):
    if lax.axis_size("tensor") != 2:
        whole = lax.all_gather(both, "tensor", axis=2, tiled=True)
        return [whole[0]], [whole[1]]
    other = pair_swap(both, "tensor", 1)
    return [both[0], other[0]], [both[1], other[1]]


def feed_total(parts):
    if lax.axis_size("tensor") != 2:
        whole = lax.psum_scatter(lowered(parts[0]), "tensor", scatter_dimension=1, tiled=True)
        return whole, None
    mine, theirs = [with_layout_constraint(lowered(part), Layout((0, 1))) for part in parts]
    return mine, pair_swap(theirs, "tensor", 1)


def exchange_sum(values, axis, bit, bits, exchange):
    wide = bits == 2 and 2 * bit < lax.axis_size(axis)
    came = [pair_swap(values, axis, bit * by) for by in ((1, 2, 3) if wide else (1,))]
    after = exchange.tick(*came)
    total = values + came[0]
    if wide:
        total = total + (came[1] + came[2])
    return tied(total, after)


def tied(gain, after):
    if not after:
        return gain
    corner = after[0][(0,) * after[0].ndim].astype(jnp.float32)
    return gain + jnp.minimum((corner > 3e38).astype(jnp.int32), 0).astype(jnp.float32)


def norm(terms, gain, after=()):
    total = sum(term.astype(jnp.float32) for term in terms)
    inverse = lax.rsqrt(jnp.mean(total * total, axis=0, keepdims=True) + EPSILON)
    return total, inverse, lowered(total * inverse * tied(gain, after))


def norm_back(source, inverse, gain, grad, terms, after=()):
    incoming = sum(term.astype(jnp.float32) for term in terms)
    if len(terms) > 1:
        incoming = lax.optimization_barrier(lowered(incoming)).astype(jnp.float32)
    unit = source * inverse
    gain_grad = jnp.sum(incoming * unit, axis=1)
    scaled = incoming * tied(gain, after)
    total = grad + inverse * (scaled - unit * jnp.mean(scaled * unit, axis=0, keepdims=True))
    return total, lowered(total), gain_grad


def first_slot(_):
    return jnp.zeros((1,), jnp.int32)


def add_back(own_keys, own_values, back, after):
    def kernel(_, keys_ref, values_ref, back_ref, *refs):
        for place, (ref, out) in enumerate(zip((keys_ref, values_ref), refs[-2:])):
            prompt = ref[:, :PROMPT_DEV].astype(jnp.float32) + back_ref[place].astype(jnp.float32)
            out[:, :PROMPT_DEV] = lowered(prompt)
            out[:, PROMPT_DEV:] = ref[:, PROMPT_DEV:]

    out = [jax.ShapeDtypeStruct(own_keys.shape, jnp.bfloat16)] * 2
    arrays = [first_slot(back), own_keys, own_values, back]
    return quick_call(kernel, "add_back", arrays, after, out)


def key_parts(tile):
    first = tile * TILE
    if first < PROMPT_DEV:
        return ([(0, first, "free")] if first else []) + [(first, TILE, "earlier")]
    return [(0, PROMPT_DEV, "free"), (PROMPT_DEV, first - PROMPT_DEV + TILE, "segment")]


def masked(scores, kind, first_key, first_query, start):
    if kind == "free":
        return scores
    key = lax.broadcasted_iota(jnp.int32, scores.shape, 0) + first_key
    query = lax.broadcasted_iota(jnp.int32, scores.shape, 1) + first_query
    allowed = key <= query
    if kind == "segment":
        allowed = allowed & (key >= start)
    return jnp.where(allowed, scores, NEGATIVE)


def spans(reference):
    tokens = reference.shape[1]
    return [(tile, slice(tile * TILE, tile * TILE + TILE)) for tile in range(tokens // TILE)]


def ahead(steps):
    held = steps[0][0]()
    for place, (_, second) in enumerate(steps):
        following = steps[place + 1][0]() if place + 1 < len(steps) else None
        second(held)
        held = following


def own_forward(heads):
    def steps(start_ref, q_ref, k_ref, v_ref, sum_ref, top_ref, total_ref):
        keys = k_ref[...].T

        def scores_of(tile, at):
            query, start = q_ref[:, at], start_ref[:, at]
            return [
                masked(dot_nn(keys[key : key + count], query), kind, key, tile * TILE, start)
                for key, count, kind in key_parts(tile)
            ]

        def mix(tile, at, parts):
            highest = jnp.max(parts[0], axis=0, keepdims=True)
            for scores in parts[1:]:
                highest = jnp.maximum(highest, jnp.max(scores, axis=0, keepdims=True))
            total, mixed = 0.0, 0.0
            for scores, (key, count, _) in zip(parts, key_parts(tile)):
                weights = jnp.exp2(scores - highest)
                total = total + jnp.sum(weights, axis=0, keepdims=True)
                mixed = mixed + dot_nn(v_ref[:, key : key + count], lowered(weights))
            sum_ref[:, at] = mixed
            top_ref[:, at] = highest
            total_ref[:, at] = total

        return [(partial(scores_of, *item), partial(mix, *item)) for item in spans(q_ref)]

    ahead([step for refs in heads for step in steps(*refs)])


def sides(side_ref, q_ref, run):
    tiles = [at for _, at in spans(q_ref)]
    conts = [at for tile, at in spans(q_ref) if tile * TILE >= PROMPT_DEV]

    @pl.when(side_ref[0] == 0)
    def _():
        run(conts, [at for at in tiles if at not in conts])

    @pl.when(side_ref[0] != 0)
    def _():
        run(tiles, [])


def far_forward(heads):
    def steps(tiles, _, q_ref, k_ref, v_ref, sum_ref, top_ref, total_ref, out_ref, lse_ref):
        keys = k_ref[...].T

        def scores_of(at):
            return dot_nn(keys, q_ref[:, at])

        def mix(at, scores):
            highest = jnp.maximum(top_ref[:, at], jnp.max(scores, axis=0, keepdims=True))
            weights = jnp.exp2(scores - highest)
            scale = jnp.exp2(top_ref[:, at] - highest)
            total = total_ref[:, at] * scale + jnp.sum(weights, axis=0, keepdims=True)
            mixed = sum_ref[:, at] * scale + dot_nn(v_ref[...], lowered(weights))
            out_ref[:, at] = lowered(mixed / total)
            lse_ref[:, at] = highest + jnp.log2(total)

        return [(partial(scores_of, at), partial(mix, at)) for at in tiles]

    def run(tiles, others):
        for _, _, _, _, sum_ref, top_ref, total_ref, out_ref, lse_ref in heads:
            for at in others:
                out_ref[:, at] = lowered(sum_ref[:, at] / total_ref[:, at])
                lse_ref[:, at] = top_ref[:, at] + jnp.log2(total_ref[:, at])
        ahead([step for refs in heads for step in steps(tiles, *refs)])

    sides(heads[0][0], heads[0][1], run)


def score_grads(scores, lse, d_shares, delta):
    shares = jnp.exp2(scores - lse)
    return lowered(shares), lowered(shares * (d_shares - delta))


def far_backward(heads):
    def steps(
        tiles, _, q_ref, k_ref, v_ref, out_ref, grad_ref, lse_ref, dq_ref, delta_ref, dkv_ref
    ):
        keys, values = k_ref[...].T, v_ref[...].T
        delta_ref[...] = jnp.sum(
            out_ref[...].astype(jnp.float32) * grad_ref[...].astype(jnp.float32),
            axis=0,
            keepdims=True,
        )
        sums = [0.0, 0.0]

        def begin(at):
            return dot_nn(keys, q_ref[:, at]), dot_nn(values, grad_ref[:, at])

        def terms(at, held):
            scores, d_shares = held
            shares, d_scores = score_grads(scores, lse_ref[:, at], d_shares, delta_ref[:, at])
            dq_ref[:, at] = dot_nn(k_ref[...], d_scores)
            sums[0] = sums[0] + dot_nt(q_ref[:, at], d_scores)
            sums[1] = sums[1] + dot_nt(grad_ref[:, at], shares)
            if at is tiles[-1]:
                dkv_ref[0] = lowered(sums[0] * LN_TWO)
                dkv_ref[1] = lowered(sums[1])

        return [(partial(begin, at), partial(terms, at)) for at in tiles]

    def run(tiles, others):
        for refs in heads:
            for at in others:
                refs[7][:, at] = jnp.zeros_like(refs[7][:, at])
        ahead([step for refs in heads for step in steps(tiles, *refs)])

    sides(heads[0][0], heads[0][1], run)


def own_backward(heads):
    def steps(
        start_ref,
        gain_ref,
        q_ref,
        k_ref,
        v_ref,
        grad_ref,
        lse_ref,
        delta_ref,
        far_dq_ref,
        dq_ref,
        dk_ref,
        dv_ref,
        scale_ref,
        k_total,
        v_total,
    ):
        keys, values = k_ref[...].T, v_ref[...].T
        seen, dqs, scales = set(), {}, [0.0]
        final = spans(q_ref)[-1][0]

        def begin(tile, at, part, last):
            key, count, kind = part
            scores = dot_nn(keys[key : key + count], q_ref[:, at])
            scores = masked(scores, kind, key, tile * TILE, start_ref[:, at])
            return scores, dot_nn(values[key : key + count], grad_ref[:, at])

        def terms(tile, at, part, last, held):
            key, count, _ = part
            scores, d_shares = held
            query, grad = q_ref[:, at], grad_ref[:, at]
            shares, d_scores = score_grads(scores, lse_ref[:, at], d_shares, delta_ref[:, at])
            dv = dot_nt(grad, shares)
            dk = dot_nt(query, d_scores)
            dq = dqs.get(tile, far_dq_ref[:, at])
            dqs[tile] = dq = dq + dot_nn(k_ref[:, key : key + count], d_scores)
            for offset in range(0, count, TILE):
                there = slice(key + offset, key + offset + TILE)
                here = slice(offset, offset + TILE)
                if key + offset in seen:
                    k_total[:, there] += dk[:, here]
                    v_total[:, there] += dv[:, here]
                else:
                    seen.add(key + offset)
                    k_total[:, there] = dk[:, here]
                    v_total[:, there] = dv[:, here]
            if last:
                dq_ref[:, at] = lowered(dq * gain_ref[...])
                product = jnp.sum(dq * query.astype(jnp.float32), axis=1, keepdims=True)
                scales[0] = scales[0] + product
                if tile == final:
                    dk_ref[...] = lowered(k_total[...] * LN_TWO)
                    dv_ref[...] = lowered(v_total[...])
                    scale_ref[...] = scales[0]

        items = []
        for tile, at in spans(q_ref):
            parts = key_parts(tile)
            items += [(tile, at, part, part is parts[-1]) for part in parts]
        return [(partial(begin, *item), partial(terms, *item)) for item in items]

    ahead([step for refs in heads for step in steps(*refs)])


def per_head(kernel, name, heads, area, products, ins, outs, after=(), scratch=()):
    group = 2 - heads % 2
    moved = sum(array.size * array.dtype.itemsize for _, array in ins)

    def spec(kind, shape):
        if kind == "rows":
            return pl.BlockSpec((group * HD, shape[1]), lambda step: (step, 0))
        if kind == "flat":
            return pl.BlockSpec((group, 1, shape[2]), lambda step: (step, 0, 0))
        if kind == "pair":
            return pl.BlockSpec((2, group * HD, shape[2]), lambda step: (0, step, 0))
        return pl.BlockSpec(shape, lambda step: (0, 0)) if kind == "same" else SCALAR

    def view(kind, ref, head):
        rows = pl.ds(head * HD, HD)
        if kind == "rows":
            return ref.at[rows]
        if kind == "flat":
            return ref.at[head]
        return ref.at[:, rows] if kind == "pair" else ref

    count = len(ins)
    kinds = [kind for kind, _ in ins] + [out[0] for out in outs] + ["rows"] * len(scratch)

    def work(*refs):
        refs = refs[:count] + refs[count + len(after) :]
        kernel(
            [[view(kind, ref, head) for kind, ref in zip(kinds, refs)] for head in range(group)]
        )

    return pl.pallas_call(
        work,
        grid=(heads // group,),
        in_specs=[spec(kind, array.shape) for kind, array in ins] + [UNREAD] * len(after),
        out_specs=[spec(kind, shape) for kind, shape, _ in outs],
        out_shape=[jax.ShapeDtypeStruct(shape, kind) for _, shape, kind in outs],
        scratch_shapes=[pltpu.VMEM((group * HD, tokens), jnp.float32) for tokens in scratch],
        compiler_params=pltpu.CompilerParams(vmem_limit_bytes=40 << 20),
        cost_estimate=pl.CostEstimate(
            flops=40 * area * heads * products,
            bytes_accessed=moved,
            transcendentals=area * heads,
        ),
        name=name,
    )(*[array for _, array in ins], *after)


def attention_own(start, queries, keys, values, after):
    width, tokens = queries.shape
    heads = width // HD
    flat = ("flat", (heads, 1, tokens), jnp.float32)
    return per_head(
        own_forward,
        "attention_own",
        heads,
        tokens * tokens * 5 // 8,
        3,
        [("same", start), ("rows", queries), ("rows", keys), ("rows", values)],
        [("rows", (width, tokens), jnp.float32), flat, flat],
        after,
    )


def attention_far(side, queries, keys, values, partial_sum, top, total, after):
    width, tokens = queries.shape
    heads = width // HD
    return per_head(
        far_forward,
        "attention_far",
        heads,
        tokens * PROMPT_DEV,
        2,
        [
            ("scalar", side),
            ("rows", queries),
            ("rows", keys),
            ("rows", values),
            ("rows", partial_sum),
            ("flat", top),
            ("flat", total),
        ],
        [
            ("rows", (width, tokens), jnp.bfloat16),
            ("flat", (heads, 1, tokens), jnp.float32),
        ],
        after,
    )


def attention_far_back(side, queries, keys, values, mixed, grads, lse, after):
    width, tokens = queries.shape
    heads = width // HD
    return per_head(
        far_backward,
        "attention_far_back",
        heads,
        tokens * PROMPT_DEV,
        3,
        [
            ("scalar", side),
            ("rows", queries),
            ("rows", keys),
            ("rows", values),
            ("rows", mixed),
            ("rows", grads),
            ("flat", lse),
        ],
        [
            ("rows", (width, tokens), jnp.float32),
            ("flat", (heads, 1, tokens), jnp.float32),
            ("pair", (2, width, PROMPT_DEV), jnp.bfloat16),
        ],
        after,
    )


def attention_own_back(start, gain, queries, keys, values, grads, lse, delta, far_dq, after):
    width, tokens = queries.shape
    heads = width // HD
    return per_head(
        own_backward,
        "attention_own_back",
        heads,
        tokens * tokens * 5 // 8,
        76,
        [
            ("same", start),
            ("same", gain),
            ("rows", queries),
            ("rows", keys),
            ("rows", values),
            ("rows", grads),
            ("flat", lse),
            ("flat", delta),
            ("rows", far_dq),
        ],
        [
            ("rows", (width, tokens), jnp.bfloat16),
            ("rows", (width, tokens), jnp.bfloat16),
            ("rows", (width, tokens), jnp.bfloat16),
            ("rows", (width, 1), jnp.float32),
        ],
        after,
        (tokens, tokens),
    )


def segment_starts(lengths_row, tokens):
    place = jnp.arange(tokens, dtype=jnp.int32) - PROMPT_DEV
    bounds = jnp.cumsum(lengths_row)
    passed = jnp.where(place[:, None] >= bounds[None, :], bounds[None, :], 0)
    return (PROMPT_DEV + jnp.max(passed, axis=1))[None, :]


def body(
    inputs,
    cotangent,
    query_weight,
    key_weight,
    value_weight,
    output_weight,
    up_weight,
    down_weight,
    attention_gain,
    feed_gain,
    query_scale,
    cont_lengths,
):
    tokens = inputs.shape[0] * lax.axis_size("tensor")
    heads = query_weight.shape[2] // HD
    orders = exchange_orders(lax.axis_size("dp"))
    side = (lax.axis_index("dp") % 2).astype(jnp.int32)[None]
    start = segment_starts(cont_lengths[0], tokens)

    pairs = []
    for layer in range(LAYERS):
        pairs.append((key_weight[layer], value_weight[layer]))
        pairs.append((query_weight[layer], output_weight[layer].T))
        pairs.append((up_weight[layer], down_weight[layer].T))

    gather = Gather(pairs, orders)
    stored = []
    terms = [inputs.T]
    ready = ()
    grad = cotangent.T
    for layer in range(LAYERS):
        attn_gain = attention_gain[layer][:, None]
        ff_gain = feed_gain[layer][:, None]
        current, inverse_attn, low = norm(terms, attn_gain, ready)
        normed, came = gather_tokens(low)
        gather.tick(came)
        if layer == 0:
            far = far_part(normed)
            gather.tick(far)
            far_normed, came = gather_tokens(far)
            gather.tick(came)
            gather.tick(grad)
            wk, wv = gather.take()
            gather.tick()
        keys = lowered(dot_tn(wk, normed))
        values = lowered(dot_tn(wv, normed))
        gather.tick(keys, values)
        wq, wo = gather.take()
        gain_q = softplus(query_scale[layer]) * LOG_TWO_E / math.sqrt(HD)
        gain_rows = jnp.tile(gain_q, heads)[:, None]
        queries = lowered(dot_tn(wq, normed) * (gain_rows * LOG_TWO_E))
        own_sum, top, total = attention_own(start, queries, keys, values, ())
        if layer:
            far = far_part(normed)
            ready = gather.tick(top, far)
            far_normed, _ = gather_tokens(far)
        far_keys = lowered(dot_tn(wk, far_normed))
        far_values = lowered(dot_tn(wv, far_normed))
        if not layer:
            ready = gather.tick(top, far_keys, far_values)
        mixed, lse = attention_far(side, queries, far_keys, far_values, own_sum, top, total, ready)
        gather.tick(lse)
        (both,) = gather.take()
        terms = scatter_tokens(lambda rows: dot_nn(wo, rows), mixed)
        ups, downs = feed_parts(both)
        ready = gather.tick(terms[-1])
        middle, inverse_feed, feed = norm([current, *terms], ff_gain, ready)
        uppers = [dot_tn(w, feed) for w in ups]
        ready = gather.tick(*uppers)
        if layer + 1 < LAYERS:
            following = gather.take()
        hiddens = [lowered(upper * jax.nn.sigmoid(upper)) for upper in uppers]
        stored.append(
            (
                (current, inverse_attn, attn_gain, normed),
                (gain_q, queries, keys, values, far_keys, far_values, mixed, lse),
                (middle, inverse_feed, ff_gain, feed, uppers, hiddens),
                (wk, wv, wq, wo, ups, downs),
            )
        )
        if layer + 1 < LAYERS:
            terms = [middle, sum(dot_nn(w, hidden) for w, hidden in zip(downs, hiddens))]
            wk, wv = following
    final = (middle, downs, hiddens)

    sums = Scatter(orders)
    small_grads = [None] * LAYERS
    grad_low = lowered(grad)
    for layer in reversed(range(LAYERS)):
        (
            (source, inverse_attn, attn_gain, normed),
            (gain_q, queries, keys, values, far_keys, far_values, mixed, lse),
            (middle, inverse_feed, ff_gain, feed, uppers, hiddens),
            (wk, wv, wq, wo, ups, downs),
        ) = stored[layer]
        d_uppers = []
        for w, upper in zip(downs, uppers):
            d_hidden = lowered(dot_tn(w, grad_low)).astype(jnp.float32)
            sigmoid = jax.nn.sigmoid(upper)
            d_uppers.append(lowered(d_hidden * (sigmoid * (1.0 + upper * (1.0 - sigmoid)))))
        d_feed = sum(dot_nn(w, d_upper) for w, d_upper in zip(ups, d_uppers))
        ready = sums.tick(d_feed)
        grad_middle, low, feed_gain_grad = norm_back(
            middle, inverse_feed, ff_gain, grad, [d_feed], ready
        )
        middle_low, came = gather_tokens(low)
        down_grad, down_came = feed_total([dot_nt(grad_low, hidden) for hidden in hiddens])
        up_grad, up_came = feed_total([dot_nt(feed, d_upper) for d_upper in d_uppers])
        if down_came is None:
            stepped = sums.tick(came, down_grad, up_grad)
            sums.push(down_grad, up_grad)
        else:
            stepped = sums.tick(came, down_came, up_came)
            sums.push(down_grad, up_grad, came=(down_came, up_came))
        d_mixed = lowered(dot_tn(wo, middle_low))
        out_grad = lowered(dot_nt(middle_low, mixed))
        ready = [*sums.enter(), *stepped]
        far_dq, delta, far_dkv = attention_far_back(
            side, queries, far_keys, far_values, mixed, d_mixed, lse, ready
        )
        back = pair_swap(far_dkv, "dp", 1)
        ready = sums.tick(delta)
        d_raw, own_dk, own_dv, scale_rows = attention_own_back(
            start,
            gain_q[:, None],
            queries,
            keys,
            values,
            d_mixed,
            lse,
            delta,
            far_dq,
            ready,
        )
        query_grad = lowered(dot_nt(normed, d_raw))
        d_keys, d_values = add_back(own_dk, own_dv, back, ())
        sums.tick(d_keys)
        sums.push(out_grad, query_grad)
        sums.enter()
        scale_raw = jnp.sum(scale_rows.reshape(heads, HD), 0) / (gain_q * LOG_TWO_E)
        scale_grad = scale_raw * jax.nn.sigmoid(query_scale[layer]) * LOG_TWO_E / math.sqrt(HD)
        if not layer:
            key_grad, value_grad = [lowered(dot_nt(normed, d)) for d in (d_keys, d_values)]
            ready = sums.tick(key_grad, value_grad)
            last = Scatter(orders)
            last.push(key_grad, value_grad)
            last.enter()
        terms = scatter_tokens(
            lambda dq, dk, dv: dot_nn(wq, dq) + dot_nn(wk, dk) + dot_nn(wv, dv),
            d_raw,
            d_keys,
            d_values,
        )
        if layer:
            ready = sums.tick(terms[-1])
        else:
            sums.tick(terms[-1])
            ready = last.tick(terms[-1])
            hiddens = [lowered(tied(h.astype(jnp.float32), ready)) for h in final[2]]
            current = final[0] + sum(dot_nn(w, h) for w, h in zip(final[1], hiddens))
        grad, grad_low, attn_gain_grad = norm_back(
            source, inverse_attn, attn_gain, grad_middle, terms, ready
        )
        if layer:
            key_grad, value_grad = [lowered(dot_nt(normed, d)) for d in (d_keys, d_values)]
            sums.push(key_grad, value_grad)
            sums.tick(grad, key_grad, value_grad)
        small_grads[layer] = jnp.concatenate([attn_gain_grad, feed_gain_grad, scale_grad])
    small = jnp.stack(small_grads)
    for axis, bits in (("tensor", 1), ("dp", 2)):
        bit = 1
        while bit < lax.axis_size(axis):
            small, bit = exchange_sum(small, axis, bit, bits, last), bit << bits
    done = sums.finish() + last.finish()
    layer_grads = []
    for layer in range(LAYERS):
        at = 3 * (LAYERS - 1 - layer)
        (down_grad, up_grad), (out_grad, query_grad), (key_grad, value_grad) = done[at : at + 3]
        layer_grads.append(
            (query_grad, key_grad, value_grad, out_grad.T, up_grad, down_grad.T)
        )

    summed = [jnp.stack(members) for members in zip(*layer_grads)]
    width = current.shape[0]
    return (
        current.T,
        grad.T,
        *summed,
        small[:, :width],
        small[:, width : 2 * width],
        small[:, 2 * width :],
    )


def solution(mesh):
    in_specs = (
        P(("dp", "tensor"), None),
        P(("dp", "tensor"), None),
        P(None, "dp", "tensor"),
        P(None, "dp", "tensor"),
        P(None, "dp", "tensor"),
        P(None, "tensor", "dp"),
        P(None, "dp", "tensor"),
        P(None, "tensor", "dp"),
        P(),
        P(),
        P(),
        P("dp", None),
    )
    out_specs = (
        P(("dp", "tensor"), None),
        P(("dp", "tensor"), None),
        P(None, "dp", "tensor"),
        P(None, "dp", "tensor"),
        P(None, "dp", "tensor"),
        P(None, "tensor", "dp"),
        P(None, "dp", "tensor"),
        P(None, "tensor", "dp"),
        P(),
        P(),
        P(),
    )
    return jax.shard_map(body, mesh=mesh, in_specs=in_specs, out_specs=out_specs, check_vma=False)
```
